256 devices in a mesh: slab: 64 (over y, x_lo, z), gy: 4 (over x_hi, core).
Axes of the slice: x: 4 (x_hi: 2, x_lo: 2; x = x_hi * 2 + x_lo), y: 4, z: 8, core: 2. Of those that a mesh axis runs over, the one named last changes fastest.
Arguments:
- field_in: bfloat16 [32, 192, 2, 32, 512], P(None, 'slab', None, None, 'gy'), may hold values from -6 to 6
- cotangent: bfloat16 [32, 192, 2, 32, 512], P(None, 'slab', None, None, 'gy'), may hold values from -6 to 6
- spectral_weight: bfloat16 [2, 3456, 32, 32], P(None, 'slab', None, 'gy'), may hold values from -0.75 to 0.75
- local_weight: bfloat16 [32, 32], replicated, may hold values from -1 to 1
Outputs:
- output: bfloat16 [32, 192, 2, 32, 512], P(None, 'slab', None, None, 'gy')
- grad_input: bfloat16 [32, 192, 2, 32, 512], P(None, 'slab', None, None, 'gy')
- grad_spectral: float32 [2, 3456, 32, 32], P(None, 'slab', None, 'gy')
- grad_local: float32 [32, 32], replicated
The draws below stay inside these ranges and needn't reach their ends.
All inputs are finite; a program needn't handle non-finite values.
Results may differ from the reference program's by a relative error of at most 0.0053.
Values sent between devices are 32-bit elements; how exact they have to be, the bound alone decides.
A program may use at most 64 MiB of HBM per device.

```python
import math
import jax
import jax.numpy as jnp
from jax import lax

C = 32
KX = 12
KY = 12
KZ = 12
NT = 2
NZ = 32
CX = 3
NX = 192
NY = 512
MODES = 3456
N_SLAB = 64


def block_scale(stream_key, shape, split, smallest, high):
    def one(dim, parts):
        heights = jax.random.uniform(jax.random.fold_in(jax.random.fold_in(stream_key, 6), dim), (parts,), jnp.float32, smallest / len(split), high / len(split))
        return jnp.repeat(jnp.exp(heights), shape[dim] // parts).reshape((-1,) + (1,) * (len(shape) - dim - 1))

    factor_of = one(*split[0])
    for cut in split[1:]:
        factor_of = factor_of * one(*cut)
    return factor_of


def centred(own_key, extent, spread, most, cuts=(), held_as=jnp.bfloat16):
    result = jax.random.normal(own_key, extent, jnp.float32) * spread
    if len(cuts) > 0:
        result = block_scale(own_key, extent, cuts, -0.22, 0.18) * result
    return jnp.clip(result, min=-most, max=most).astype(held_as)


def setup_inputs(seed: int = 0) -> dict:
    key_of = jax.random.split(jax.random.key(seed), 5)
    field_in = centred(key_of[0], (C, NX, NT, NZ, NY), 1.0, 6.0, ((1, 64), (4, 4)))
    cotangent = centred(key_of[1], (C, NX, NT, NZ, NY), 1.0, 6.0, ((1, 64), (4, 4)))
    spectral_weight = centred(key_of[2], (2, MODES, C, C), (2 * C) ** -0.5, 0.75, ((1, 64), (3, 4)))
    local_weight = centred(key_of[3], (C, C), C ** -0.5, 1.0)
    return dict(field_in=field_in, cotangent=cotangent, spectral_weight=spectral_weight, local_weight=local_weight)


highest = lax.Precision.HIGHEST
root_half = 0.7071067811865476
inv_root_two_pi = 0.3989422804014327

def centred_frequencies(kept_count):
    values = jnp.arange(kept_count, dtype=jnp.int32)
    return jnp.where(values < kept_count // 2, values, values - kept_count)

def angle_table(row_count, length, kept_count, first_index):
    position = first_index + jnp.arange(row_count, dtype=jnp.int32)
    product = position[:, None] * centred_frequencies(kept_count)[None, :] % length
    phases = product.astype(jnp.float32) * (2.0 * math.pi / length)
    return (jnp.cos(phases), jnp.sin(phases))

def depth_tables(depth_count, level_count, kept_count):
    depth_pos = jnp.arange(depth_count, dtype=jnp.int32)
    level_pos = jnp.arange(level_count, dtype=jnp.int32)
    level_freq = jnp.arange(level_count, dtype=jnp.int32)
    depth_freq = centred_frequencies(kept_count)
    product = (level_pos[:, None, None, None] * level_freq[None, None, :, None] * depth_count + depth_pos[None, :, None, None] * depth_freq[None, None, None, :] * level_count) % (depth_count * level_count)
    phases = product.astype(jnp.float32).reshape(level_count * depth_count, level_count * kept_count)
    phases = phases * (2.0 * math.pi / (depth_count * level_count))
    return (jnp.cos(phases), jnp.sin(phases))

def depth_forward(values, table):
    return jnp.einsum('crsk,sq->crkq', values, table, precision=highest)

def depth_inverse(values, table):
    return jnp.einsum('crkq,sq->crsk', values, table, precision=highest)

def rows_forward(values, table):
    return jnp.einsum('crkq,rp->pkqc', values, table, precision=highest)

def rows_inverse(values, table):
    return jnp.einsum('pkqc,rp->crkq', values, table, precision=highest)

def along_depth(field_data, y_table, depth_cos, depth_sin):
    channels, row_count = (field_data.shape[0], field_data.shape[1])
    kept_count = y_table.shape[1] // 2
    partial_value = jnp.dot(field_data.reshape(-1, field_data.shape[-1]), y_table, preferred_element_type=jnp.float32)
    partial_value = partial_value.reshape(channels, row_count, -1, 2, kept_count)
    cosine_part, sine_part = (partial_value[:, :, :, 0], partial_value[:, :, :, 1])
    real_part = depth_forward(cosine_part, depth_cos) + depth_forward(sine_part, depth_sin)
    imag_part = depth_forward(sine_part, depth_cos) - depth_forward(cosine_part, depth_sin)
    return (real_part, imag_part)

def along_rows(spectrum, row_cos, row_sin):
    real_part = rows_forward(spectrum[0], row_cos) + rows_forward(spectrum[1], row_sin)
    imag_part = rows_forward(spectrum[1], row_cos) - rows_forward(spectrum[0], row_sin)
    return (real_part.reshape(-1, real_part.shape[-1]), imag_part.reshape(-1, imag_part.shape[-1]))

def from_rows(spectrum, row_cos, row_sin):
    real_part = spectrum[0].reshape(KX, KY, NT * KZ, -1)
    imag_part = spectrum[1].reshape(KX, KY, NT * KZ, -1)
    first_out = rows_inverse(real_part, row_cos) - rows_inverse(imag_part, row_sin)
    second_out = rows_inverse(real_part, row_sin) + rows_inverse(imag_part, row_cos)
    return (first_out, second_out)

def from_depth(spectrum, y_table32, depth_cos, depth_sin):
    channels, row_count = (spectrum[0].shape[0], spectrum[0].shape[1])
    cosine_part = depth_inverse(spectrum[0], depth_cos) - depth_inverse(spectrum[1], depth_sin)
    sine_part = depth_inverse(spectrum[0], depth_sin) + depth_inverse(spectrum[1], depth_cos)
    stacked = jnp.concatenate([cosine_part, sine_part], axis=-1)
    field_data = jnp.dot(stacked.reshape(-1, stacked.shape[-1]), y_table32.T, precision=highest, preferred_element_type=jnp.float32)
    return field_data.reshape(channels, row_count, NT, NZ, -1)

def mode_product(values, weight):
    return jnp.einsum('mi,mio->mo', values, weight, precision=highest)

def mode_adjoint(values, weight):
    return jnp.einsum('mo,mio->mi', values, weight, precision=highest)

def mode_outer(left, right):
    return jnp.einsum('mi,mo->mio', left, right, precision=highest)

def mix_modes(spectrum, weight):
    real_part = mode_product(spectrum[0], weight[0]) - mode_product(spectrum[1], weight[1])
    imag_part = mode_product(spectrum[0], weight[1]) + mode_product(spectrum[1], weight[0])
    return (real_part, imag_part)

def mix_back(spectrum, weight):
    real_part = mode_adjoint(spectrum[0], weight[0]) + mode_adjoint(spectrum[1], weight[1])
    imag_part = mode_adjoint(spectrum[1], weight[0]) - mode_adjoint(spectrum[0], weight[1])
    return (real_part, imag_part)

def weight_grad(mode_data, grad_modes):
    real_part = mode_outer(mode_data[0], grad_modes[0]) + mode_outer(mode_data[1], grad_modes[1])
    imag_part = mode_outer(mode_data[0], grad_modes[1]) - mode_outer(mode_data[1], grad_modes[0])
    return jnp.stack([real_part, imag_part])

def activate(values):
    return 0.5 * values * (1.0 + lax.erf(values * root_half))

def gelu_slope(values):
    return 0.5 * (1.0 + lax.erf(values * root_half)) + values * jnp.exp(-0.5 * values * values) * inv_root_two_pi

def assemble(blocks):
    return jnp.moveaxis(blocks, 0, 1).reshape(C, NX, NT, NZ, NY)

def reference(field_in, cotangent, spectral_weight, local_weight):
    y_cos, y_sin = angle_table(NY, NY, KY, 0)
    y_table32 = jnp.concatenate([y_cos, -y_sin], axis=1)
    y_table = y_table32.astype(jnp.bfloat16)
    depth_cos, depth_sin = depth_tables(NZ, NT, KZ)
    forward_scale = 1.0 / math.sqrt(NX * NY * NZ * NT)
    inverse_scale = 1.0 / math.sqrt(KX * KY * KZ * NT)
    weight = spectral_weight.astype(jnp.float32)
    block_ids = jnp.arange(N_SLAB, dtype=jnp.int32)

    def to_modes(field_data):

        def add_block(totals, block_index):
            first_row = block_index * CX
            slab_block = lax.dynamic_slice_in_dim(field_data, first_row, CX, 1)
            row_cos, row_sin = angle_table(CX, NX, KX, first_row)
            addend = along_rows(along_depth(slab_block, y_table, depth_cos, depth_sin), row_cos, row_sin)
            return ((totals[0] + addend[0], totals[1] + addend[1]), None)
        zeros_modes = jnp.zeros((MODES, C), jnp.float32)
        totals, ignored = lax.scan(add_block, (zeros_modes, zeros_modes), block_ids)
        return (totals[0] * forward_scale, totals[1] * forward_scale)

    def from_modes(spectrum, block_index):
        row_cos, row_sin = angle_table(CX, NX, KX, block_index * CX)
        return from_depth(from_rows(spectrum, row_cos, row_sin), y_table32, depth_cos, depth_sin) * inverse_scale
    mode_data = to_modes(field_in)
    mixed_modes = mix_modes(mode_data, weight)

    def forward_block(block_index):
        slab_block = lax.dynamic_slice_in_dim(field_in, block_index * CX, CX, 1)
        cot_block = lax.dynamic_slice_in_dim(cotangent, block_index * CX, CX, 1)
        local_part = jnp.dot(local_weight.T, slab_block.reshape(C, -1), preferred_element_type=jnp.float32).reshape(slab_block.shape)
        pre_act = from_modes(mixed_modes, block_index) + local_part
        grad_pre = (cot_block.astype(jnp.float32) * gelu_slope(pre_act)).astype(jnp.bfloat16)
        return (activate(pre_act).astype(jnp.bfloat16), grad_pre)
    out_blocks, grad_blocks = lax.map(forward_block, block_ids)
    output = assemble(out_blocks)
    grad_pre = assemble(grad_blocks)
    grad_modes = to_modes(grad_pre)
    grad_spectral = weight_grad(mode_data, grad_modes)
    back_modes = mix_back(grad_modes, weight)

    def backward_block(block_index):
        slab_block = lax.dynamic_slice_in_dim(grad_pre, block_index * CX, CX, 1)
        local_part = jnp.dot(local_weight, slab_block.reshape(C, -1), preferred_element_type=jnp.float32).reshape(slab_block.shape)
        return (from_modes(back_modes, block_index) + local_part).astype(jnp.bfloat16)
    grad_input = assemble(lax.map(backward_block, block_ids))
    grad_local = jnp.dot(field_in.reshape(C, -1), grad_pre.reshape(C, -1).T, preferred_element_type=jnp.float32) * forward_scale
    return (output, grad_input, grad_spectral, grad_local)
```

```python
import functools
import math

import jax
import jax.numpy as jnp
import numpy as np
from jax import lax
from jax.experimental import pallas as pl
from jax.experimental.pallas import tpu as pltpu
from jax.sharding import PartitionSpec as P

C = 32
KX = 12
KY = 12
KZ = 12
NT = 2
NZ = 32
NX = 192
NY = 512
CX = 3
N_GY = 4
N_Y = 4
N_R = 16
Q = C // N_GY
K = NT * KZ
TZ = NT * NZ
Y = NY // N_GY
BLOCK = 54
UNITS = 9
ROWS = 72
LANES = K * Q

FORWARD_SCALE = 1.0 / math.sqrt(NX * NY * NZ * NT)
INVERSE_SCALE = 1.0 / math.sqrt(KX * KY * KZ * NT)
ROOT_HALF = 0.7071067811865476
INV_ROOT_TWO_PI = 0.3989422804014327
HIGHEST = lax.Precision.HIGHEST
F32 = jnp.float32
BF16 = jnp.bfloat16
MESH = pl.DeviceIdType.MESH


def frequencies(kept):
    values = np.arange(kept)
    return np.where(values < kept // 2, values, values - kept)


def depth_table():
    t, z = np.divmod(np.arange(TZ), NZ)
    kt, kz = np.divmod(np.arange(K), KZ)
    product = (t[None] * kt[:, None] * NZ + z[None] * frequencies(KZ)[kz][:, None] * NT) % TZ
    angle = product * (2.0 * np.pi / TZ)
    parts = np.stack([np.cos(angle), -np.sin(angle)])
    full = np.einsum("pks,cd->pkcds", parts, np.eye(Q))
    return full.reshape(2 * K * Q, Q * TZ)


def y_tables():
    product = (frequencies(KY)[:, None] * np.arange(NY)[None]) % NY
    angle = product * (2.0 * np.pi / NY)
    cos, sin = np.cos(angle), np.sin(angle)
    full = np.stack([np.stack([cos, sin]), np.stack([-sin, cos])])
    full = full.reshape(2, 2, KY, N_GY, Y).transpose(3, 0, 2, 1, 4)
    return full.reshape(N_GY, 2 * KY, 2 * Y)


def unit_tables():
    lane = np.arange(128)
    row = np.arange(96)
    expand = (lane[None] // 6 == np.arange(16)[:, None]) & (lane[None] < BLOCK)
    keep = ((row[:, None] // 8) % 6 == lane[None] % 6) & (lane[None] < BLOCK)
    return expand.astype(np.float32), keep.astype(np.float32)


def row_matrix(slab):
    shape = (N_Y * ROWS, ROWS)
    row = lax.broadcasted_iota(jnp.int32, shape, 0)
    col = lax.broadcasted_iota(jnp.int32, shape, 1)
    part, part_in = (row % 72) // 36, (col % 24) // 12
    kx = (row // 72) * 3 + (row % 36) // 12
    freq = jnp.where(kx < KX // 2, kx, kx - KX)
    product = (freq * (slab * CX + col // 24)) % NX
    phase = product.astype(F32) * (2.0 * math.pi / NX)
    cos, sin = jnp.cos(phase), jnp.sin(phase)
    value = jnp.where(part == part_in, cos, jnp.where(part == 0, sin, -sin))
    return jnp.where(row % 12 == col % 12, value, 0.0) * FORWARD_SCALE


def dot(a, b, dims, precision=None):
    return lax.dot_general(a, b, (dims, ((), ())), precision=precision, preferred_element_type=F32)


NN = ((1,), (0,))
NT_DIMS = ((1,), (1,))
TN = ((0,), (0,))


def to_pieces(field_ref, depth_ref, y_ref, gy, gsend):
    table = y_ref[gy]
    for x in range(CX):
        for pair in range(2):
            blocks = [
                field_ref[(2 * pair + h) * Q : (2 * pair + h + 1) * Q, x].reshape(Q * TZ, Y)
                for h in range(2)
            ]
            z = dot(depth_ref[...], jnp.concatenate(blocks, axis=1), NN)
            for h in range(2):
                part = z[:, h * Y : (h + 1) * Y]
                both = jnp.concatenate([part[:LANES], part[LANES:]], axis=1).astype(BF16)
                gsend[2 * pair + h, x * 24 : (x + 1) * 24, 0:LANES] = dot(table, both, NT_DIMS)


def comm_kernel(backward, *refs):
    field_ref, depth_ref, y_ref, rows_ref, w_ref, expand_ref, keep_ref = refs[:7]
    if backward:
        modes_ref, local_ref, hall_out, gs_ref, gl_ref = refs[7:12]
        refs = refs[12:]
    else:
        hall_out, modes_out = refs[7:9]
        refs = refs[9:]
    (gsend, grecv, fsend, frecv, units, msend, mrecv, qsend, qbuf, rsend, rall, fall, hsend, hall) = refs[:14]
    sems = refs[14:]

    slab, gy = lax.axis_index("slab"), lax.axis_index("gy")
    yy, rr = lax.div(slab, N_R), lax.rem(slab, N_R)

    def gy_at(d):
        index = lax.rem(gy + d, N_GY)
        return index, {"gy": index}

    def y_at(d):
        index = lax.rem(yy + d, N_Y)
        return index, {"slab": index * N_R + rr}

    def r_at(d):
        index = lax.rem(rr + d, N_R)
        return index, {"slab": yy * N_R + index}

    barrier = pltpu.get_barrier_semaphore()
    for n, at in ((N_GY, gy_at), (N_Y, y_at), (N_R, r_at)):
        for d in range(1, n):
            pl.semaphore_signal(barrier, inc=1, device_id=at(d)[1], device_id_type=MESH)

    started = []

    def send_all(round_index, n, at, source, target):
        send_sem, recv_sem = sems[2 * round_index], sems[2 * round_index + 1]
        copies = []
        for d in range(1, n):
            index, device = at(d)
            copy = pltpu.make_async_remote_copy(
                src_ref=source(index),
                dst_ref=target(d),
                send_sem=send_sem.at[d - 1],
                recv_sem=recv_sem.at[d - 1],
                device_id=device,
                device_id_type=MESH,
            )
            copy.start()
            copies.append(copy)
        for copy in copies:
            copy.wait_recv()
        started.extend(copies)

    to_pieces(field_ref, depth_ref, y_ref, gy, gsend)
    msend[...] = jnp.zeros_like(msend)
    qsend[...] = jnp.zeros_like(qsend)
    rsend[...] = jnp.zeros_like(rsend)
    if backward:
        local = local_ref[...]
        for q in range(N_GY):
            for a in range(2):
                gsend[q, 8 * a : 8 * a + 8, 192:224] = local[16 * a : 16 * a + 8]
                gsend[q, 8 * a : 8 * a + 8, 224:256] = local[16 * a + 8 : 16 * a + 16]
    pl.semaphore_wait(barrier, N_GY + N_Y + N_R - 3)

    send_all(0, N_GY, gy_at, lambda i: gsend.at[i], lambda d: grecv.at[d - 1])
    g = gsend[gy] + grecv[0] + grecv[1] + grecv[2]

    f = dot(rows_ref[...], g[:, 0:LANES], NN, HIGHEST)
    for j in range(N_Y):
        fsend[j, :, 0:LANES] = f[j * ROWS : (j + 1) * ROWS]
        if backward:
            fsend[j, 0:16, LANES:256] = g[0:16, LANES:256]
    send_all(1, N_Y, y_at, lambda i: fsend.at[i], lambda d: frecv.at[d - 1])
    f = fsend[yy] + frecv[0] + frecv[1] + frecv[2]

    blank = jnp.zeros((36, 32), F32)
    for kq in range(4):
        lanes = slice(kq * 48, kq * 48 + 48)
        units[pl.ds(kq, 36, stride=4), :] = jnp.concatenate([f[0:36, lanes], f[36:72, lanes], blank], axis=1)
    for j in range(N_R):
        msend[j, 0:UNITS, :] = units[j * UNITS : (j + 1) * UNITS, :]
        if backward:
            msend[j, 16:24, 0:64] = f[0:8, LANES:256]
            msend[j, 16:24, 64:128] = f[8:16, LANES:256]
    send_all(2, N_R, r_at, lambda i: msend.at[i], lambda d: mrecv.at[d - 1])
    m = msend[rr]
    for d in range(1, N_R):
        m = m + mrecv[d - 1]

    spread = dot(m[0:16, 0:96], expand_ref[...], TN, HIGHEST) * keep_ref[...]
    parts = []
    for part in range(2):
        total = spread[part * 48 : part * 48 + 8]
        for j in range(1, 6):
            total = total + spread[part * 48 + 8 * j : part * 48 + 8 * j + 8]
        parts.append(total)

    if backward:
        for a in range(4):
            gl_ref[8 * a : 8 * a + 8, :] = m[16:24, 32 * a : 32 * a + 32] * FORWARD_SCALE
        gr, gi = parts[0][:, 0:BLOCK], parts[1][:, 0:BLOCK]
        for i in range(C):
            q, c = divmod(i, Q)
            mr, mi = modes_ref[q, c : c + 1, 0:BLOCK], modes_ref[q, 8 + c : 9 + c, 0:BLOCK]
            gs_ref[0, i] = mr * gr + mi * gi
            gs_ref[1, i] = mr * gi - mi * gr
            w0, w1 = w_ref[0, i].astype(F32), w_ref[1, i].astype(F32)
            qsend[q, c : c + 1, 0:BLOCK] = jnp.sum(gr * w0 + gi * w1, axis=0, keepdims=True)
            qsend[q, 8 + c : 9 + c, 0:BLOCK] = jnp.sum(gi * w0 - gr * w1, axis=0, keepdims=True)
        send_all(3, N_GY, gy_at, lambda i: qsend.at[i], lambda d: qbuf.at[d - 1])
        mixed = qsend[gy] + qbuf[0] + qbuf[1] + qbuf[2]
        mixed = [mixed[0:8], mixed[8:16]]
    else:
        qsend[...] = jnp.concatenate(parts, axis=0)
        qbuf[gy] = qsend[...]
        send_all(3, N_GY, gy_at, lambda i: qsend, lambda d: qbuf.at[gy])
        modes_out[...] = qbuf[...]
        mixed_r = jnp.zeros((Q, BLOCK), F32)
        mixed_i = jnp.zeros((Q, BLOCK), F32)
        for i in range(C):
            q, c = divmod(i, Q)
            mr, mi = qbuf[q, c : c + 1, 0:BLOCK], qbuf[q, 8 + c : 9 + c, 0:BLOCK]
            w0, w1 = w_ref[0, i].astype(F32), w_ref[1, i].astype(F32)
            mixed_r = mixed_r + (mr * w0 - mi * w1)
            mixed_i = mixed_i + (mr * w1 + mi * w0)
        pad = jnp.zeros((Q, 128 - BLOCK), F32)
        mixed = [jnp.concatenate([v, pad], axis=1) for v in (mixed_r, mixed_i)]

    tiled = jnp.concatenate([mixed[0]] * 6 + [mixed[1]] * 6, axis=0) * keep_ref[...]
    rsend[:, 0:96] = dot(expand_ref[...], tiled, NT_DIMS, HIGHEST)
    rall[rr] = rsend[...]
    send_all(4, N_R, r_at, lambda i: rsend, lambda d: rall.at[rr])
    for j in range(N_R):
        units[j * UNITS : (j + 1) * UNITS, :] = rall[j, 0:UNITS, :]

    for kq in range(4):
        both = units[pl.ds(kq, 36, stride=4), :]
        for part in range(2):
            fall[yy, part * 36 : part * 36 + 36, kq * 48 : kq * 48 + 48] = both[:, part * 48 : part * 48 + 48]
    send_all(5, N_Y, y_at, lambda i: fall.at[yy], lambda d: fall.at[yy])

    h = dot(rows_ref[...], fall[...].reshape(N_Y * ROWS, 256)[:, 0:LANES], TN, HIGHEST)
    hsend[:, 0:LANES] = h * (INVERSE_SCALE / FORWARD_SCALE)
    hall[gy] = hsend[...]
    send_all(6, N_GY, gy_at, lambda i: hsend, lambda d: hall.at[gy])
    hall_out[...] = hall[...]
    for copy in started:
        copy.wait_send()


def vmem():
    return pl.BlockSpec(memory_space=pltpu.VMEM)


def comm_call(backward, *operands):
    message = 24 if backward else 16
    outs = [jax.ShapeDtypeStruct((N_GY, ROWS, 256), F32)]
    if backward:
        outs.append(jax.ShapeDtypeStruct((2, C, Q, BLOCK), F32))
        outs.append(jax.ShapeDtypeStruct((C, C), F32))
    else:
        outs.append(jax.ShapeDtypeStruct((N_GY, 16, 128), F32))
    big, small = (ROWS, 256), (16, 128)
    shapes = [
        (N_GY, *big),
        (N_GY - 1, *big),
        (N_Y, *big),
        (N_Y - 1, *big),
        (N_R * UNITS, 128),
        (N_R, message, 128),
        (N_R - 1, message, 128),
        (N_GY, *small) if backward else small,
        (N_GY - 1, *small) if backward else (N_GY, *small),
        small,
        (N_R, *small),
        (N_Y, *big),
        big,
        (N_GY, *big),
    ]
    scratch = [pltpu.VMEM(shape, F32) for shape in shapes]
    for n in (N_GY, N_Y, N_R, N_GY, N_R, N_Y, N_GY):
        scratch += [pltpu.SemaphoreType.DMA((n - 1,))] * 2
    return pl.pallas_call(
        functools.partial(comm_kernel, backward),
        out_shape=outs,
        in_specs=[vmem() for _ in operands],
        out_specs=[vmem() for _ in outs],
        scratch_shapes=scratch,
        compiler_params=pltpu.CompilerParams(
            collective_id=1 if backward else 0,
            has_side_effects=True,
            vmem_limit_bytes=32 * 1024 * 1024,
        ),
        name="modes_backward" if backward else "modes_forward",
    )(*operands)


def spectral_rows(hall_ref, y_ref, depth_ref, gy, x, spec):
    for pair in range(2):
        halves = []
        for q in (2 * pair, 2 * pair + 1):
            h = hall_ref[q, pl.ds(pl.multiple_of(x * 24, 8), 24), 0:LANES]
            high = h.astype(BF16).astype(F32)
            stacked = jnp.concatenate([high, high, h - high], axis=0).astype(BF16)
            u = dot(stacked, y_ref[gy], TN)
            halves.append(jnp.concatenate([u[:, :Y], u[:, Y:]], axis=0).astype(BF16))
        s = dot(depth_ref[...], jnp.concatenate(halves, axis=1), NN)
        for h in range(2):
            q = 2 * pair + h
            spec[q * Q : (q + 1) * Q] = s[:, h * Y : (h + 1) * Y].reshape(Q, TZ, Y)


def chunk_of(ref, r):
    values = ref[:, r * 16 : (r + 1) * 16, :].astype(F32)
    return jnp.concatenate([values[:, 0:8].reshape(256, Y), values[:, 8:16].reshape(256, Y)], axis=1)


def unchunk(values):
    halves = [values[:, :Y].reshape(C, 8, Y), values[:, Y:].reshape(C, 8, Y)]
    return jnp.concatenate(halves, axis=1)


def channel_matrix(weight, repeat_ref, transposed):
    repeat = repeat_ref[...]
    half = dot(repeat, weight, NT_DIMS if transposed else NN).astype(BF16)
    full = dot(half, repeat, NT_DIMS)
    row = lax.broadcasted_iota(jnp.int32, full.shape, 0)
    col = lax.broadcasted_iota(jnp.int32, full.shape, 1)
    return jnp.where(row % 8 == col % 8, full, 0.0).astype(BF16)


def forward_kernel(field_ref, cot_ref, hall_ref, y_ref, depth_ref, lw_ref, repeat_ref, out_ref, grad_ref, local_ref, spec, acc, kron):
    x, gy = pl.program_id(0), lax.axis_index("gy")

    @pl.when(x == 0)
    def _():
        kron[...] = channel_matrix(lw_ref[...], repeat_ref, True)
        acc[...] = jnp.zeros_like(acc)

    spectral_rows(hall_ref, y_ref, depth_ref, gy, x, spec)
    for r in range(TZ // 16):
        cells = chunk_of(field_ref.at[:, 0], r).astype(BF16)
        pre = chunk_of(spec, r) + dot(kron[...], cells, NN)
        cdf = 0.5 * (1.0 + lax.erf(pre * ROOT_HALF))
        slope = cdf + pre * jnp.exp(-0.5 * pre * pre) * INV_ROOT_TWO_PI
        grad = chunk_of(cot_ref.at[:, 0], r) * slope
        out_ref[:, 0, r * 16 : (r + 1) * 16, :] = unchunk(pre * cdf).astype(BF16)
        grad_ref[:, 0, r * 16 : (r + 1) * 16, :] = unchunk(grad).astype(BF16)
        acc[...] += dot(cells, grad.astype(BF16), NT_DIMS)

    @pl.when(x == CX - 1)
    def _():
        row = lax.broadcasted_iota(jnp.int32, acc.shape, 0)
        col = lax.broadcasted_iota(jnp.int32, acc.shape, 1)
        kept = jnp.where(row % 8 == col % 8, acc[...], 0.0)
        repeat = repeat_ref[...].astype(F32)
        local_ref[...] = dot(dot(repeat, kept, TN, HIGHEST), repeat, NN, HIGHEST)


def backward_kernel(grad_ref, hall_ref, y_ref, depth_ref, lw_ref, repeat_ref, out_ref, spec, kron):
    x, gy = pl.program_id(0), lax.axis_index("gy")

    @pl.when(x == 0)
    def _():
        kron[...] = channel_matrix(lw_ref[...], repeat_ref, False)

    spectral_rows(hall_ref, y_ref, depth_ref, gy, x, spec)
    for r in range(TZ // 16):
        cells = chunk_of(grad_ref.at[:, 0], r).astype(BF16)
        total = chunk_of(spec, r) + dot(kron[...], cells, NN)
        out_ref[:, 0, r * 16 : (r + 1) * 16, :] = unchunk(total).astype(BF16)


def row_spec():
    return pl.BlockSpec((C, 1, TZ, Y), lambda x: (0, x, 0, 0))


def per_device(field_in, cotangent, spectral_weight, local_weight):
    cells = (C, CX, TZ, Y)
    field = field_in.reshape(cells)
    cot = cotangent.reshape(cells)
    weight = jnp.transpose(spectral_weight, (0, 2, 3, 1))
    depth = depth_table()
    tables = y_tables()
    high = tables.astype(BF16)
    low = (tables - high.astype(np.float64)).astype(BF16)
    depth_forward = jnp.asarray(depth.astype(BF16))
    depth_back = jnp.asarray(np.ascontiguousarray(depth.T).astype(BF16))
    y_forward = jnp.asarray(high)
    y_back = jnp.asarray(np.concatenate([high, low, high], axis=1))
    expand, keep = unit_tables()
    expand, keep = jnp.asarray(expand), jnp.asarray(keep)
    repeat = jnp.asarray(np.repeat(np.eye(C), 8, axis=0).astype(BF16))
    rows = row_matrix(lax.axis_index("slab"))

    hall, modes = comm_call(False, field, depth_forward, y_forward, rows, weight, expand, keep)
    field_shape = jax.ShapeDtypeStruct(cells, BF16)
    params = pltpu.CompilerParams(vmem_limit_bytes=32 * 1024 * 1024)
    output, grad_pre, local_terms = pl.pallas_call(
        forward_kernel,
        grid=(CX,),
        out_shape=[field_shape, field_shape, jax.ShapeDtypeStruct((C, C), F32)],
        in_specs=[row_spec(), row_spec()] + [vmem()] * 5,
        out_specs=[row_spec(), row_spec(), pl.BlockSpec((C, C), lambda x: (0, 0))],
        scratch_shapes=[pltpu.VMEM((C, TZ, Y), F32), pltpu.VMEM((256, 256), F32), pltpu.VMEM((256, 256), BF16)],
        compiler_params=params,
        name="cells_forward",
    )(field, cot, hall, y_back, depth_back, local_weight, repeat)
    hall, grad_spectral, grad_local = comm_call(
        True, grad_pre, depth_forward, y_forward, rows, weight, expand, keep, modes, local_terms
    )
    grad_input = pl.pallas_call(
        backward_kernel,
        grid=(CX,),
        out_shape=field_shape,
        in_specs=[row_spec()] + [vmem()] * 5,
        out_specs=row_spec(),
        scratch_shapes=[pltpu.VMEM((C, TZ, Y), F32), pltpu.VMEM((256, 256), BF16)],
        compiler_params=params,
        name="cells_backward",
    )(grad_pre, hall, y_back, depth_back, local_weight, repeat)
    return (
        output.reshape(field_in.shape),
        grad_input.reshape(field_in.shape),
        jnp.transpose(grad_spectral, (0, 3, 1, 2)),
        grad_local,
    )


def solution(mesh):
    placed = (
        P(None, "slab", None, None, "gy"),
        P(None, "slab", None, None, "gy"),
        P(None, "slab", None, "gy"),
        P(),
    )
    return jax.shard_map(
        per_device,
        mesh=mesh,
        in_specs=placed,
        out_specs=(
            P(None, "slab", None, None, "gy"),
            P(None, "slab", None, None, "gy"),
            P(None, "slab", None, "gy"),
            P(),
        ),
        check_vma=False,
    )
```

```python
import functools
import math

import jax
import jax.numpy as jnp
import numpy as np
from jax import lax
from jax.experimental import pallas as pl
from jax.experimental.pallas import tpu as pltpu
from jax.sharding import PartitionSpec as P

C = 32
KX = 12
KY = 12
KZ = 12
NT = 2
NZ = 32
NX = 192
NY = 512
CX = 3
N_GY = 4
N_Y = 4
N_R = 16
Q = C // N_GY
K = NT * KZ
TZ = NT * NZ
Y = NY // N_GY
BLOCK = 54
UNITS = 9
ROWS = 72
LANES = K * Q

FORWARD_SCALE = 1.0 / math.sqrt(NX * NY * NZ * NT)
INVERSE_SCALE = 1.0 / math.sqrt(KX * KY * KZ * NT)
ROOT_HALF = 0.7071067811865476
INV_ROOT_TWO_PI = 0.3989422804014327
HIGHEST = lax.Precision.HIGHEST
WINDOW = [(z % 4) * 4 + x * 2 + z // 4 for x in range(2) for z in range(8)]
PLANE = [(h, c, y) for h in range(2) for c in range(2) for y in range(N_Y) if (h, c, y) != (0, 0, 0)]
PLANE.sort(key=lambda d: -(2 * d[0] + min(d[2], N_Y - d[2])))
COLUMN = [(x, z) for x in range(2) for z in range(8) if (x, z) != (0, 0)]
COLUMN.sort(key=lambda d: -(d[0] + min(d[1], 8 - d[1])))
QUARTER = [(1, 1), (1, 0), (0, 1)]
F32 = jnp.float32
BF16 = jnp.bfloat16
MESH = pl.DeviceIdType.MESH


def frequencies(kept):
    values = np.arange(kept)
    return np.where(values < kept // 2, values, values - kept)


def depth_table():
    t, z = np.divmod(np.arange(TZ), NZ)
    kt, kz = np.divmod(np.arange(K), KZ)
    product = (t[None] * kt[:, None] * NZ + z[None] * frequencies(KZ)[kz][:, None] * NT) % TZ
    angle = product * (2.0 * np.pi / TZ)
    parts = np.stack([np.cos(angle), -np.sin(angle)])
    full = np.einsum("pks,cd->pkcds", parts, np.eye(Q))
    return full.reshape(2 * K * Q, Q * TZ)


def y_tables():
    product = (frequencies(KY)[:, None] * np.arange(NY)[None]) % NY
    angle = product * (2.0 * np.pi / NY)
    cos, sin = np.cos(angle), np.sin(angle)
    full = np.stack([np.stack([cos, sin]), np.stack([-sin, cos])])
    full = full.reshape(2, 2, KY, N_GY, Y).transpose(3, 0, 2, 1, 4)
    return full.reshape(N_GY, 2 * KY, 2 * Y)


def unit_tables():
    lane = np.arange(128)
    row = np.arange(96)
    expand = (lane[None] // 6 == np.arange(16)[:, None]) & (lane[None] < BLOCK)
    keep = ((row[:, None] // 8) % 6 == lane[None] % 6) & (lane[None] < BLOCK)
    return expand.astype(np.float32), keep.astype(np.float32)


def row_tables():
    main = [9 * w + j for w in WINDOW for j in range(8)]
    ninth = [9 * w + 8 for w in WINDOW]
    pairs = np.array(main + main + ninth + ninth)
    part = np.array([0] * 128 + [1] * 128 + [0] * 16 + [1] * 16)
    y, x, part_in, ky = np.unravel_index(np.arange(288), (N_Y, CX, 2, KY))
    row = 48 * y[None] + 3 * np.arange(N_R)[:, None] + x[None]
    freq = frequencies(KX)[pairs // KY]
    angle = (freq[None, :, None] * row[:, None, :]) % NX * (2.0 * np.pi / NX)
    sign = np.where(part == 0, 1.0, -1.0)[:, None]
    value = np.where(part[:, None] == part_in[None], np.cos(angle), sign * np.sin(angle))
    value = np.where((pairs % KY)[:, None] == ky[None], value, 0.0)
    forward, inverse = value * FORWARD_SCALE, value.transpose(0, 2, 1) * INVERSE_SCALE
    parts = []
    for full in (forward, inverse):
        high = full.astype(BF16)
        parts += [high, (full - high.astype(np.float64)).astype(BF16)]
    return np.stack(parts, axis=1)


def owner_tables():
    select = np.zeros((4, 72, 128))
    place = np.zeros((4, 2, 72, 128))
    gather = np.zeros((4, 4, 128, 128))
    for t in range(4):
        count = [0] * 4
        for mode in range(BLOCK):
            unit = 9 * t + mode // 6
            y, other = unit % 4, 6 * (unit // 4) + mode % 6
            n = count[y]
            count[y] += 1
            if n < 12:
                select[t, 16 * y + n, mode] = 1.0
            else:
                select[t, 64 + n - 12, mode] = 1.0
            for half in range(2):
                row = 8 * t + n if n < 8 else 40 + 8 * t + 4 * half + n - 8 if n < 12 else 32 + n - 12
                place[y, half, row, other] = 1.0
            for part in range(2):
                gather[t, y, part * BLOCK + other, part * BLOCK + mode] = 1.0
    return select, place.reshape(4, 144, 128), gather.reshape(4, 512, 128)


def dot(a, b, dims, precision=None):
    return lax.dot_general(a, b, (dims, ((), ())), precision=precision, preferred_element_type=F32)


NN = ((1,), (0,))
NT_DIMS = ((1,), (1,))
TN = ((0,), (0,))


def comm_kernel(backward, *refs):
    field_ref, depth_hbm, y_hbm, rows_hbm, expand_hbm, keep_hbm, gather_hbm = refs[:7]
    if backward:
        owned_ref, modes_ref, local_ref, hall_out, gs_ref, gl_ref = refs[7:13]
        refs = refs[13:]
    else:
        w_hbm, select_hbm, place_hbm, hall_out, modes_out, owned_out = refs[7:13]
        refs = refs[13:]
    (depth_ref, y_ref, rows_ref, expand_ref, keep_ref, gather_ref) = refs[:6]
    (z_all, gsend, grecv, g12, msend, mrecv, qsend, qbuf, rows8, rsend, rall, hsend, hall, l1buf) = refs[6:20]
    load_sem, *sems = refs[20:28]
    if not backward:
        w_ref, select_ref, place_ref, wsend, wrecv, third_unit, third_sem, field_vmem, field_sem = refs[28:]

    slab, gy = lax.axis_index("slab"), lax.axis_index("gy")
    yy, rr = lax.div(slab, N_R), lax.rem(slab, N_R)
    x_hi, core = lax.div(gy, 2), lax.rem(gy, 2)
    x_lo, z = lax.div(rr, 8), lax.rem(rr, 8)
    turn, half = lax.rem(z, 4), lax.div(z, 4)

    staged = [
        (depth_hbm, depth_ref),
        (y_hbm.at[gy], y_ref),
        (rows_hbm.at[rr], rows_ref),
        (expand_hbm, expand_ref),
        (keep_hbm, keep_ref),
        (gather_hbm.at[turn], gather_ref),
    ]
    if not backward:
        staged += [(w_hbm, w_ref), (select_hbm.at[turn], select_ref), (place_hbm.at[yy], place_ref)]
    loads = [pltpu.make_async_copy(a, b, load_sem.at[k]) for k, (a, b) in enumerate(staged)]
    if not backward:
        pieces = [
            pltpu.make_async_copy(field_ref.at[:, x], field_vmem.at[x], field_sem.at[x]) for x in range(CX)
        ]
        pieces[0].start()
    for load in loads:
        load.start()
    if not backward:
        pieces[1].start()
        pieces[2].start()

    def plane(k):
        d_hi, d_core, dy = PLANE[k]
        g_to = lax.rem(x_hi + d_hi, 2) * 2 + lax.rem(core + d_core, 2)
        y_to = lax.rem(yy + dy, N_Y)
        return g_to, y_to, {"gy": g_to, "slab": y_to * N_R + rr}

    def column(k):
        d_lo, dz = COLUMN[k]
        r_to = lax.rem(x_lo + d_lo, 2) * 8 + lax.rem(z + dz, 8)
        return r_to, {"slab": yy * N_R + r_to}

    def quarter(k):
        d_hi, d_core = QUARTER[k]
        g_to = lax.rem(x_hi + d_hi, 2) * 2 + lax.rem(core + d_core, 2)
        return g_to, {"gy": g_to}

    owners = [k * N_R + x_lo * 8 + half * 4 + yy for k in range(4)]
    blocks = [turn * N_R + x_lo * 8 + half * 4 + k for k in range(4)]
    at_home = (turn == yy).astype(jnp.int32)

    barrier = pltpu.get_barrier_semaphore()

    def greet(device):
        pl.semaphore_signal(barrier, inc=1, device_id=device, device_id_type=MESH)

    for k in range(15):
        greet(plane(k)[2])
        greet(column(k)[1])
    for other in owners + blocks:
        pl.when(other != slab)(functools.partial(greet, {"slab": other}))

    def copy_to(source, target, send_sem, recv_sem, device):
        return pltpu.make_async_remote_copy(
            src_ref=source,
            dst_ref=target,
            send_sem=send_sem,
            recv_sem=recv_sem,
            device_id=device,
            device_id_type=MESH,
        )

    started = []

    def start_all(round_index, copies):
        sem = sems[round_index]
        made = [copy_to(a, b, sem.at[0, k], sem.at[1, k], device) for k, (a, b, device) in enumerate(copies)]
        for copy in made:
            copy.start()
        started.extend(made)
        return made

    def finish(made):
        for copy in made:
            copy.wait_recv()

    def cross(index, buffer, source, target):
        sem = sems[5 + index]
        return [
            (target[k] != slab, copy_to(source(k), buffer, sem.at[0, k], sem.at[1, slot], {"slab": target[k]}))
            for k, slot in ((k, turn if index == 0 else yy) for k in range(4))
        ]

    def start_cross(made):
        for away, copy in made:
            pl.when(away)(copy.start)

    def finish_cross(index, buffer, source, origin):
        sem = sems[5 + index]
        for k in range(4):
            copy = copy_to(source, buffer.at[k], sem.at[0, k], sem.at[1, k], {"slab": origin[k]})
            pl.when(origin[k] != slab)(copy.wait_recv)

    loads[0].wait()
    loads[1].wait()
    table = y_ref[...]
    for x in range(CX):
        if not backward:
            pieces[x].wait()
        for pair in range(2):
            channels = [slice((2 * pair + h) * Q, (2 * pair + h + 1) * Q) for h in range(2)]
            cells = [(field_ref[c, x] if backward else field_vmem[x, c]).reshape(Q * TZ, Y) for c in channels]
            zz = dot(depth_ref[...], jnp.concatenate(cells, axis=1), NN)
            for h in range(2):
                part = zz[:, h * Y : (h + 1) * Y]
                both = jnp.concatenate([part[:LANES], part[LANES:]], axis=1).astype(BF16)
                z_all[2 * pair + h, x] = both
    pl.semaphore_wait(barrier, 30 + 8 - 2 * at_home)
    if not backward:
        for load in loads[6:]:
            load.wait()
        flat = w_ref[...].astype(F32).reshape(2 * C * Q, BLOCK).astype(BF16)
        picked = dot(select_ref[...][:, 0:BLOCK].astype(BF16), flat, NT_DIMS)
        for k in range(4):
            four = picked[16 * k + 8 : 16 * k + 12]
            four = jnp.concatenate([four[:, 0:256], four[:, 256:512]], axis=0)
            wsend[k] = jnp.concatenate([picked[16 * k : 16 * k + 8], four], axis=1)
        third_unit[0] = picked[64:72]
        w_copies = cross(0, wrecv.at[turn], lambda k: wsend.at[k], owners)
        home = turn * N_R + x_lo * 8 + half * 4 + yy
        extra = copy_to(third_unit.at[0], third_unit.at[1], third_sem.at[0], third_sem.at[1], {"slab": home})
        w_copies.append((turn != yy, extra))

        @pl.when(turn == yy)
        def _():
            wrecv[turn] = wsend[yy]
            third_unit[1] = third_unit[0]

    for q in range(N_GY):
        for kq in range(4):
            rows = [z_all[q, x, kq * 48 : kq * 48 + 48, :] for x in range(CX)]
            g = dot(table, jnp.concatenate(rows, axis=0), NT_DIMS)
            tail = [local_ref[8 * q : 8 * q + 8, 8 * kq : 8 * kq + 8]] if backward else []
            gsend[q, kq] = pack(g, tail)

    plane_to = [plane(k) for k in range(15)]
    first = start_all(0, [(gsend.at[g, y], grecv.at[k], device) for k, (g, y, device) in enumerate(plane_to)])
    for load in loads[2:6]:
        load.wait()
    if not backward:
        start_cross(w_copies)
    finish(first)
    slot = {PLANE[k]: k for k in range(15)}
    local = None
    for dy in range(N_Y):
        total = gsend[gy, yy] if dy == 0 else None
        for d_hi in range(2):
            for d_core in range(2):
                if (d_hi, d_core, dy) in slot:
                    term = grecv[slot[d_hi, d_core, dy]]
                    total = term if total is None else total + term
        if backward:
            block = total[24:32, 48:56]
            local = block if local is None else local + block
        base = lax.rem(yy + N_Y - dy, N_Y) * ROWS
        for x, piece in enumerate(unpack(total)):
            g12[pl.ds(pl.multiple_of(base + 24 * x, 8), 24), 0:48] = piece

    f = product(rows_ref, 0, g12[:, 0:48])
    blank = jnp.zeros((128, 24), F32)
    corner = jnp.concatenate([local] * N_R, axis=0) if backward else jnp.zeros((128, 8), F32)
    msend[...] = jnp.concatenate([f[0:128], f[128:256], blank, corner], axis=1)
    ninth = jnp.concatenate([f[256:272], f[272:288]], axis=1)
    for j in range(4):
        old = msend[pl.ds(j, N_R, stride=8), :]
        msend[pl.ds(j, N_R, stride=8), :] = jnp.concatenate(
            [old[:, 0:96], ninth[:, 24 * j : 24 * j + 24], old[:, 120:128]], axis=1
        )

    def window(r):
        return pl.ds(pl.multiple_of(r * 8, 8), 8)

    column_to = [column(k) for k in range(15)]
    second = start_all(1, [(msend.at[window(r)], mrecv.at[k], device) for k, (r, device) in enumerate(column_to)])
    if not backward:
        finish_cross(0, wrecv, wsend.at[0], blocks)
        pl.when(turn != yy)(extra.wait_recv)
        eights = jnp.concatenate([wrecv[t, :, 0:512] for t in range(4)] + [third_unit[1]], axis=0)
        fours = jnp.concatenate([wrecv[t, :, 512:768] for t in range(4)], axis=0)
        for side in range(2):
            lanes = slice(256 * side, 256 * side + 256)
            received = jnp.concatenate([eights[:, lanes], fours], axis=0).astype(BF16)
            owned_out[lanes] = dot(received, place_ref[72 * side : 72 * side + 72, :].astype(BF16), TN)
    finish(second)
    m = msend[window(rr), :]
    for k in range(15):
        m = m + mrecv[k]

    last = jnp.concatenate([m[j : j + 1, 96:120] for j in range(4)], axis=1)
    nine = jnp.concatenate([m[:, 0:96], last, jnp.zeros((7, 96), F32)], axis=0)
    spread = dot(nine, expand_ref[...], TN, HIGHEST) * keep_ref[...]
    parts = []
    for part in range(2):
        total = spread[part * 48 : part * 48 + 8]
        for j in range(1, 6):
            total = total + spread[part * 48 + 8 * j : part * 48 + 8 * j + 8]
        parts.append(total[:, 0:BLOCK])

    def weights(i):
        source = owned_ref if backward else owned_out
        return source[8 * i : 8 * i + 8, 0:BLOCK], source[256 + 8 * i : 264 + 8 * i, 0:BLOCK]

    end = jnp.zeros((Q, 128 - 2 * BLOCK), F32)
    if backward:
        total_local = m[:, 120:128]
        gr, gi = parts
        l1_source = rsend.at[1]
        rsend[1] = jnp.concatenate([gr, gi, end], axis=1)
        for i in range(C):
            q, c = divmod(i, Q)
            w0, w1 = weights(i)
            rows8[q, c : c + 1, 0:BLOCK] = jnp.sum(gr * w0 + gi * w1, axis=0, keepdims=True)
            rows8[q, 8 + c : 9 + c, 0:BLOCK] = jnp.sum(gi * w0 - gr * w1, axis=0, keepdims=True)
        for q in range(N_GY):
            qsend[q] = jnp.concatenate([rows8[q, 0:8, 0:BLOCK], rows8[q, 8:16, 0:BLOCK], end], axis=1)
        third = start_all(2, [(qsend.at[g], qbuf.at[k], device) for k, (g, device) in enumerate(map(quarter, range(3)))])
    else:
        l1_source = qbuf
        qsend[0] = jnp.concatenate([*parts, end], axis=1)
        qbuf[gy] = qsend[0]
        third = start_all(2, [(qsend.at[0], qbuf.at[gy], device) for g, device in map(quarter, range(3))])

    if backward:
        l1_copies = cross(1, l1buf.at[yy], lambda k: l1_source, blocks)
        start_cross(l1_copies)
        finish(third)
        mixed = qsend[gy] + qbuf[0] + qbuf[1] + qbuf[2]
        mixed = [mixed[:, 0:BLOCK], mixed[:, BLOCK : 2 * BLOCK]]
    else:
        finish(third)
        mixed_r = jnp.zeros((Q, BLOCK), F32)
        mixed_i = jnp.zeros((Q, BLOCK), F32)
        for q in range(N_GY):
            real, imag = qbuf[q, :, 0:BLOCK], qbuf[q, :, BLOCK : 2 * BLOCK]
            for c in range(Q):
                mr, mi = real[c : c + 1], imag[c : c + 1]
                w0, w1 = weights(q * Q + c)
                mixed_r = mixed_r + (mr * w0 - mi * w1)
                mixed_i = mixed_i + (mr * w1 + mi * w0)
        mixed = [mixed_r, mixed_i]

    pad = jnp.zeros((Q, 128 - BLOCK), F32)
    mixed = [jnp.concatenate([v, pad], axis=1) for v in mixed]
    tiled = jnp.concatenate([mixed[0]] * 6 + [mixed[1]] * 6, axis=0) * keep_ref[...]
    u = dot(expand_ref[...], tiled, NT_DIMS, HIGHEST)
    last = jnp.concatenate([u[8:9, 24 * j : 24 * j + 24] for j in range(4)] + [jnp.zeros((4, 24), F32)], axis=0)
    rsend[0] = jnp.concatenate([u[0:8], last, jnp.zeros((8, 8), F32)], axis=1)
    rall[window(rr), :] = rsend[0]
    fourth = start_all(3, [(rsend.at[0], rall.at[window(rr)], device) for r, device in column_to])
    if not backward:
        l1_copies = cross(1, l1buf.at[yy], lambda k: l1_source, blocks)
        start_cross(l1_copies)

    @pl.when(turn == yy)
    def _():
        l1buf[yy] = l1_source[...]

    finish(fourth)
    ninth = jnp.concatenate([rall[pl.ds(j, N_R, stride=8), :][:, 96:120] for j in range(4)], axis=1)
    f = jnp.concatenate([rall[:, 0:48], rall[:, 48:96], ninth[:, 0:48], ninth[:, 48:96]], axis=0)

    h = product(rows_ref, 2, f)
    for y in range(N_Y):
        pieces_of = [h[y * ROWS + 24 * x : y * ROWS + 24 * x + 24] for x in range(CX)]
        hsend[y] = pack(jnp.concatenate(pieces_of, axis=1), [total_local] if backward else [])
    hall[yy, gy] = hsend[yy]
    fifth = start_all(4, [(hsend.at[y], hall.at[yy, gy], device) for g, y, device in plane_to])

    finish_cross(1, l1buf, l1_source, owners)
    held = [l1buf[k] if backward else l1buf[k].reshape(C, 128) for k in range(4)]
    block = dot(jnp.concatenate(held, axis=1), gather_ref[...], NN, HIGHEST)
    if backward:
        gr, gi = block[:, 0:BLOCK], block[:, BLOCK : 2 * BLOCK]
        for i in range(C):
            mr, mi = modes_ref[i : i + 1, 0:BLOCK], modes_ref[i : i + 1, BLOCK : 2 * BLOCK]
            gs_ref[0, i] = mr * gr + mi * gi
            gs_ref[1, i] = mr * gi - mi * gr
    else:
        modes_out[...] = block
    finish(fifth)
    for y in range(N_Y):
        for g in range(N_GY):
            piece = hall[y, g]
            if backward:
                gl_ref[8 * g : 8 * g + 8, 8 * y : 8 * y + 8] = piece[24:32, 48:56] * FORWARD_SCALE
            for x, rows in enumerate(unpack(piece)):
                hall_out[x, g, :, y * 48 : y * 48 + 48] = rows
    for copy in started:
        copy.wait_send()
    for away, copy in l1_copies if backward else w_copies + l1_copies:
        pl.when(away)(copy.wait_send)


def pack(g, corner):
    tail = g[:, 128:144]
    width = 80 - 8 * len(corner)
    below = jnp.concatenate([tail[0:8], tail[8:16], tail[16:24], *corner, jnp.zeros((8, width), F32)], axis=1)
    return jnp.concatenate([g[:, 0:128], below], axis=0)


def unpack(message):
    below = message[24:32]
    tail = jnp.concatenate([below[:, 0:16], below[:, 16:32], below[:, 32:48]], axis=0)
    body = message[0:24]
    return [body[:, 0:48], body[:, 48:96], jnp.concatenate([body[:, 96:128], tail], axis=1)]


def product(rows_ref, first, values):
    high = values.astype(BF16)
    low = (values - high.astype(F32)).astype(BF16)
    both = dot(rows_ref[first], jnp.concatenate([high, low], axis=1), NN)
    width = values.shape[1]
    return both[:, :width] + both[:, width:] + dot(rows_ref[first + 1], high, NN)


def vmem():
    return pl.BlockSpec(memory_space=pltpu.VMEM)


def hbm():
    return pl.BlockSpec(memory_space=pltpu.HBM)


def comm_call(backward, field, tables, *operands):
    names = ["depth", "y", "rows", "expand", "keep", "gather"]
    outs = [jax.ShapeDtypeStruct((CX, N_GY, 24, 256), F32)]
    if backward:
        outs.append(jax.ShapeDtypeStruct((2, C, Q, BLOCK), F32))
        outs.append(jax.ShapeDtypeStruct((C, C), F32))
        kept = [vmem()] * 3
    else:
        outs.append(jax.ShapeDtypeStruct((C, 128), F32))
        outs.append(jax.ShapeDtypeStruct((2 * C * Q, 128), F32))
        kept = [hbm()] * 3
    pair = pltpu.SemaphoreType.DMA
    tile = (8, 128)
    scratch = [
        pltpu.VMEM((2 * K * Q, Q * TZ), BF16),
        pltpu.VMEM((2 * KY, 2 * Y), BF16),
        pltpu.VMEM((4, 288, 288), BF16),
        pltpu.VMEM((16, 128), F32),
        pltpu.VMEM((96, 128), F32),
        pltpu.VMEM((512, 128), F32),
        pltpu.VMEM((N_GY, CX, LANES, 256), BF16),
        pltpu.VMEM((N_GY, N_Y, 32, 128), F32),
        pltpu.VMEM((15, 32, 128), F32),
        pltpu.VMEM((288, 128), F32),
        pltpu.VMEM((128, 128), F32),
        pltpu.VMEM((15, *tile), F32),
        pltpu.VMEM((N_GY, *tile) if backward else (1, *tile), F32),
        pltpu.VMEM((N_GY - 1, *tile) if backward else (N_GY, *tile), F32),
        pltpu.VMEM((N_GY, 16, 128), F32),
        pltpu.VMEM((2, *tile), F32),
        pltpu.VMEM((128, 128), F32),
        pltpu.VMEM((N_Y, 32, 128), F32),
        pltpu.VMEM((N_Y, N_GY, 32, 128), F32),
        pltpu.VMEM((4, *tile) if backward else (4, N_GY, *tile), F32),
        pair((9,)),
        pair((2, 15)),
        pair((2, 15)),
        pair((2, 3)),
        pair((2, 15)),
        pair((2, 15)),
        pair((2, 4)),
        pair((2, 4)),
    ]
    if not backward:
        scratch += [
            pltpu.VMEM((2, C, Q, BLOCK), BF16),
            pltpu.VMEM((72, 128), F32),
            pltpu.VMEM((144, 128), F32),
            pltpu.VMEM((4, 8, 768), F32),
            pltpu.VMEM((4, 8, 768), F32),
            pltpu.VMEM((2, 8, 512), F32),
            pair((2,)),
            pltpu.VMEM((CX, C, TZ, Y), BF16),
            pair((CX,)),
        ]
    return pl.pallas_call(
        functools.partial(comm_kernel, backward),
        out_shape=outs,
        in_specs=[vmem() if backward else hbm()] + [hbm()] * len(names) + kept,
        out_specs=[vmem() for _ in outs],
        scratch_shapes=scratch,
        compiler_params=pltpu.CompilerParams(
            collective_id=1 if backward else 0,
            has_side_effects=True,
            vmem_limit_bytes=60 * 1024 * 1024,
        ),
        name="modes_backward" if backward else "modes_forward",
    )(field, *[tables[name] for name in names], *operands)


def spectral_rows(hall_ref, y_ref, depth_ref, gy, x, spec):
    for pair in range(2):
        halves = []
        for q in (2 * pair, 2 * pair + 1):
            h = hall_ref[x, q, :, 0:LANES]
            high = h.astype(BF16).astype(F32)
            stacked = jnp.concatenate([high, high, h - high], axis=0).astype(BF16)
            u = dot(stacked, y_ref[gy], TN)
            halves.append(jnp.concatenate([u[:, :Y], u[:, Y:]], axis=0).astype(BF16))
        s = dot(depth_ref[...], jnp.concatenate(halves, axis=1), NN)
        for h in range(2):
            q = 2 * pair + h
            spec[q * Q : (q + 1) * Q] = s[:, h * Y : (h + 1) * Y].reshape(Q, TZ, Y)


def chunk_of(ref, r):
    values = ref[:, r * 16 : (r + 1) * 16, :].astype(F32)
    return jnp.concatenate([values[:, 0:8].reshape(256, Y), values[:, 8:16].reshape(256, Y)], axis=1)


def unchunk(values):
    halves = [values[:, :Y].reshape(C, 8, Y), values[:, Y:].reshape(C, 8, Y)]
    return jnp.concatenate(halves, axis=1)


def channel_matrix(weight, repeat_ref, transposed):
    repeat = repeat_ref[...]
    half = dot(repeat, weight, NT_DIMS if transposed else NN).astype(BF16)
    full = dot(half, repeat, NT_DIMS)
    row = lax.broadcasted_iota(jnp.int32, full.shape, 0)
    col = lax.broadcasted_iota(jnp.int32, full.shape, 1)
    return jnp.where(row % 8 == col % 8, full, 0.0).astype(BF16)


def forward_kernel(field_ref, cot_ref, hall_ref, y_ref, depth_ref, lw_ref, repeat_ref, out_ref, grad_ref, local_ref, spec, acc, kron):
    x, gy = pl.program_id(0), lax.axis_index("gy")

    @pl.when(x == 0)
    def _():
        kron[...] = channel_matrix(lw_ref[...], repeat_ref, True)
        acc[...] = jnp.zeros_like(acc)

    spectral_rows(hall_ref, y_ref, depth_ref, gy, x, spec)
    for r in range(TZ // 16):
        cells = chunk_of(field_ref.at[:, 0], r).astype(BF16)
        pre = chunk_of(spec, r) + dot(kron[...], cells, NN)
        cdf = 0.5 * (1.0 + lax.erf(pre * ROOT_HALF))
        slope = cdf + pre * jnp.exp(-0.5 * pre * pre) * INV_ROOT_TWO_PI
        grad = chunk_of(cot_ref.at[:, 0], r) * slope
        out_ref[:, 0, r * 16 : (r + 1) * 16, :] = unchunk(pre * cdf).astype(BF16)
        grad_ref[:, 0, r * 16 : (r + 1) * 16, :] = unchunk(grad).astype(BF16)
        acc[...] += dot(cells, grad.astype(BF16), NT_DIMS)

    @pl.when(x == CX - 1)
    def _():
        row = lax.broadcasted_iota(jnp.int32, acc.shape, 0)
        col = lax.broadcasted_iota(jnp.int32, acc.shape, 1)
        kept = jnp.where(row % 8 == col % 8, acc[...], 0.0)
        repeat = repeat_ref[...].astype(F32)
        local_ref[...] = dot(dot(repeat, kept, TN, HIGHEST), repeat, NN, HIGHEST)


def backward_kernel(grad_ref, hall_ref, y_ref, depth_ref, lw_ref, repeat_ref, out_ref, spec, kron):
    x, gy = pl.program_id(0), lax.axis_index("gy")

    @pl.when(x == 0)
    def _():
        kron[...] = channel_matrix(lw_ref[...], repeat_ref, False)

    spectral_rows(hall_ref, y_ref, depth_ref, gy, x, spec)
    for r in range(TZ // 16):
        cells = chunk_of(grad_ref.at[:, 0], r).astype(BF16)
        total = chunk_of(spec, r) + dot(kron[...], cells, NN)
        out_ref[:, 0, r * 16 : (r + 1) * 16, :] = unchunk(total).astype(BF16)


def row_spec():
    return pl.BlockSpec((C, 1, TZ, Y), lambda x: (0, x, 0, 0))


def per_device(field_in, cotangent, spectral_weight, local_weight):
    cells = (C, CX, TZ, Y)
    field = field_in.reshape(cells)
    cot = cotangent.reshape(cells)
    weight = jnp.transpose(spectral_weight, (0, 2, 3, 1))
    depth = depth_table()
    tables = y_tables()
    high = tables.astype(BF16)
    low = (tables - high.astype(np.float64)).astype(BF16)
    depth_forward = jnp.asarray(depth.astype(BF16))
    depth_back = jnp.asarray(np.ascontiguousarray(depth.T).astype(BF16))
    y_forward = jnp.asarray(high)
    y_back = jnp.asarray(np.concatenate([high, low, high], axis=1))
    expand, keep = unit_tables()
    select, place, gather = owner_tables()
    forms = {
        "depth": depth_forward,
        "y": y_forward,
        "rows": jnp.asarray(row_tables()),
        "expand": jnp.asarray(expand),
        "keep": jnp.asarray(keep),
        "gather": jnp.asarray(gather.astype(np.float32)),
    }
    select, place = jnp.asarray(select.astype(np.float32)), jnp.asarray(place.astype(np.float32))
    repeat = jnp.asarray(np.repeat(np.eye(C), 8, axis=0).astype(BF16))

    hall, modes, owned = comm_call(False, field, forms, weight, select, place)
    field_shape = jax.ShapeDtypeStruct(cells, BF16)
    params = pltpu.CompilerParams(vmem_limit_bytes=60 * 1024 * 1024)
    output, grad_pre, local_terms = pl.pallas_call(
        forward_kernel,
        grid=(CX,),
        out_shape=[field_shape, field_shape, jax.ShapeDtypeStruct((C, C), F32)],
        in_specs=[row_spec(), row_spec()] + [vmem()] * 5,
        out_specs=[row_spec(), row_spec(), pl.BlockSpec((C, C), lambda x: (0, 0))],
        scratch_shapes=[pltpu.VMEM((C, TZ, Y), F32), pltpu.VMEM((256, 256), F32), pltpu.VMEM((256, 256), BF16)],
        compiler_params=params,
        name="cells_forward",
    )(field, cot, hall, y_back, depth_back, local_weight, repeat)
    hall, grad_spectral, grad_local = comm_call(True, grad_pre, forms, owned, modes, local_terms)
    grad_input = pl.pallas_call(
        backward_kernel,
        grid=(CX,),
        out_shape=field_shape,
        in_specs=[row_spec()] + [vmem()] * 5,
        out_specs=row_spec(),
        scratch_shapes=[pltpu.VMEM((C, TZ, Y), F32), pltpu.VMEM((256, 256), BF16)],
        compiler_params=params,
        name="cells_backward",
    )(grad_pre, hall, y_back, depth_back, local_weight, repeat)
    return (
        output.reshape(field_in.shape),
        grad_input.reshape(field_in.shape),
        jnp.transpose(grad_spectral, (0, 3, 1, 2)),
        grad_local,
    )


def solution(mesh):
    placed = (
        P(None, "slab", None, None, "gy"),
        P(None, "slab", None, None, "gy"),
        P(None, "slab", None, "gy"),
        P(),
    )
    return jax.shard_map(
        per_device,
        mesh=mesh,
        in_specs=placed,
        out_specs=(
            P(None, "slab", None, None, "gy"),
            P(None, "slab", None, None, "gy"),
            P(None, "slab", None, "gy"),
            P(),
        ),
        check_vma=False,
    )
```

```python
import functools
import math
import types

import jax
import jax.numpy as jnp
import numpy as np
from jax import lax
from jax.experimental import pallas as pl
from jax.experimental.pallas import tpu as pltpu
from jax.sharding import PartitionSpec as P

C = 32
KX = 12
KY = 12
KZ = 12
NT = 2
NZ = 32
NX = 192
NY = 512
CX = 3
N_GY = 4
N_Y = 4
N_R = 16
Q = C // N_GY
K = NT * KZ
TZ = NT * NZ
Y = NY // N_GY
BLOCK = 54
OWN = 27
UNITS = 9
ROWS = 72
LANES = K * Q

FORWARD_SCALE = 1.0 / math.sqrt(NX * NY * NZ * NT)
INVERSE_SCALE = 1.0 / math.sqrt(KX * KY * KZ * NT)
ROOT_HALF = 0.7071067811865476
INV_ROOT_TWO_PI = 0.3989422804014327
HIGHEST = lax.Precision.HIGHEST
WINDOW = [(z % 4) * 4 + x * 2 + z // 4 for x in range(2) for z in range(8)]
PLANE = [(h, c, y) for h in range(2) for c in range(2) for y in range(N_Y) if (h, c, y) != (0, 0, 0)]
PLANE.sort(key=lambda d: -(2 * d[0] + min(d[2], N_Y - d[2])))
COLUMN = [(x, z) for x in range(2) for z in range(8) if (x, z) != (0, 0)]
COLUMN.sort(key=lambda d: -(d[0] + min(d[1], 8 - d[1])))
F32 = jnp.float32
BF16 = jnp.bfloat16
MESH = pl.DeviceIdType.MESH


def frequencies(kept):
    values = np.arange(kept)
    return np.where(values < kept // 2, values, values - kept)


def depth_table():
    t, z = np.divmod(np.arange(TZ), NZ)
    kt, kz = np.divmod(np.arange(K), KZ)
    product = (t[None] * kt[:, None] * NZ + z[None] * frequencies(KZ)[kz][:, None] * NT) % TZ
    angle = product * (2.0 * np.pi / TZ)
    parts = np.stack([np.cos(angle), -np.sin(angle)])
    full = np.einsum("pks,cd->pkcds", parts, np.eye(Q))
    return full.reshape(2 * K * Q, Q * TZ)


def y_tables():
    product = (frequencies(KY)[:, None] * np.arange(NY)[None]) % NY
    angle = product * (2.0 * np.pi / NY)
    cos, sin = np.cos(angle), np.sin(angle)
    full = np.stack([np.stack([cos, sin]), np.stack([-sin, cos])])
    full = full.reshape(2, 2, KY, N_GY, Y).transpose(3, 0, 2, 1, 4)
    return full.reshape(N_GY, 2 * KY, 2 * Y)


def unit_tables():
    lane = np.arange(128)
    row = np.arange(96)
    expand = (lane[None] // 3 == np.arange(16)[:, None]) & (lane[None] < OWN)
    keep = ((row[:, None] // 8) % 3 == lane[None] % 3) & (lane[None] < OWN)
    return expand.astype(np.float32), keep.astype(np.float32)


def row_tables():
    main = [9 * w + j for w in WINDOW for j in range(8)]
    ninth = [9 * w + 8 for w in WINDOW]
    pairs = np.array(main + main + ninth + ninth)
    part = np.array([0] * 128 + [1] * 128 + [0] * 16 + [1] * 16)
    y, x, part_in, ky = np.unravel_index(np.arange(288), (N_Y, CX, 2, KY))
    row = 48 * y[None] + 3 * np.arange(N_R)[:, None] + x[None]
    freq = frequencies(KX)[pairs // KY]
    angle = (freq[None, :, None] * row[:, None, :]) % NX * (2.0 * np.pi / NX)
    sign = np.where(part == 0, 1.0, -1.0)[:, None]
    value = np.where(part[:, None] == part_in[None], np.cos(angle), sign * np.sin(angle))
    value = np.where((pairs % KY)[:, None] == ky[None], value, 0.0)
    forward, inverse = value * FORWARD_SCALE, value.transpose(0, 2, 1) * INVERSE_SCALE
    parts = []
    for full in (forward, inverse):
        high = full.astype(BF16)
        parts += [high, (full - high.astype(np.float64)).astype(BF16)]
    return np.stack(parts, axis=1)


def owner_tables():
    select = np.zeros((4, 72, 128))
    place = np.zeros((8, 72, 128))
    gather = np.zeros((4, 8, OWN, 128))
    for t in range(4):
        count = [0] * 8
        for mode in range(BLOCK):
            unit = 18 * t + mode // 3
            part, other = unit % 8, 3 * (unit // 8) + mode % 3
            n = count[part]
            count[part] += 1
            select[t, 8 * part + n if n < 8 else 64 + part - 2 * t, mode] = 1.0
            for x in range(2):
                place[part, 16 * t + 8 * x + n if n < 8 else 64 + x, OWN * x + other] = 1.0
            gather[t, part, other, mode] = 1.0
    return select, place, gather.reshape(4, 8 * OWN, 128)


def dot(a, b, dims, precision=None):
    return lax.dot_general(a, b, (dims, ((), ())), precision=precision, preferred_element_type=F32)


NN = ((1,), (0,))
NT_DIMS = ((1,), (1,))
TN = ((0,), (0,))


def pack(g, corner):
    tail = g[:, 128:144]
    width = 80 - 8 * len(corner)
    below = jnp.concatenate([tail[0:8], tail[8:16], tail[16:24], *corner, jnp.zeros((8, width), F32)], axis=1)
    return jnp.concatenate([g[:, 0:128], below], axis=0)


def unpack(message):
    below = message[24:32]
    tail = jnp.concatenate([below[:, 0:16], below[:, 16:32], below[:, 32:48]], axis=0)
    body = message[0:24]
    return [body[:, 0:48], body[:, 48:96], jnp.concatenate([body[:, 96:128], tail], axis=1)]


def product(rows_ref, first, values):
    high = values.astype(BF16)
    low = (values - high.astype(F32)).astype(BF16)
    both = dot(rows_ref[first], jnp.concatenate([high, low], axis=1), NN)
    width = values.shape[1]
    return both[:, :width] + both[:, width:] + dot(rows_ref[first + 1], high, NN)


def chunk_of(values):
    values = values.astype(F32)
    return jnp.concatenate([values[:, 0:8].reshape(256, Y), values[:, 8:16].reshape(256, Y)], axis=1)


def unchunk(values):
    halves = [values[:, :Y].reshape(C, 8, Y), values[:, Y:].reshape(C, 8, Y)]
    return jnp.concatenate(halves, axis=1)


def same_row(shape):
    row = lax.broadcasted_iota(jnp.int32, shape, 0)
    col = lax.broadcasted_iota(jnp.int32, shape, 1)
    return row % 8 == col % 8


def channel_matrix(weight, repeat, transposed):
    half = dot(repeat, weight, NT_DIMS if transposed else NN).astype(BF16)
    full = dot(half, repeat, NT_DIMS)
    return jnp.where(same_row(full.shape), full, 0.0).astype(BF16)


CHUNKS = TZ // 16
BIG = (32, 128)
TILE = (8, 128)
DMA = pltpu.SemaphoreType.DMA

INPUTS = ["field", "cot", "weight", "lw", "depth", "depth_back", "y_table", "y_back", "rows", "expand", "keep"]
INPUTS += ["select", "place", "gather", "repeat"]
OUTPUTS = ["out", "grad_in", "grad_spectral", "grad_local"]
SCRATCH = {
    "v_field": ((CX, C, TZ, Y), BF16),
    "v_cot": ((CX, C, TZ, Y), BF16),
    "v_weight": ((2, C, Q, BLOCK), BF16),
    "v_lw": ((C, C), BF16),
    "v_depth": ((2 * K * Q, Q * TZ), BF16),
    "v_depth_back": ((Q * TZ, 2 * K * Q), BF16),
    "v_y_table": ((2 * KY, 2 * Y), BF16),
    "v_y_back": ((6 * KY, 2 * Y), BF16),
    "v_rows": ((4, 288, 288), BF16),
    "v_expand": ((16, 128), F32),
    "v_keep": ((96, 128), F32),
    "v_select": ((72, 128), F32),
    "v_place": ((72, 128), F32),
    "v_gather": ((8 * OWN, 128), F32),
    "v_repeat": ((256, C), BF16),
    "grad_pre": ((CX, C, TZ, Y), BF16),
    "spec": ((C, TZ, Y), F32),
    "cells": ((CX * CHUNKS, 256, 256), BF16),
    "cot_cells": ((CX * CHUNKS, 256, 256), F32),
    "local_part": ((CX * CHUNKS, 256, 256), F32),
    "acc": ((256, 256), F32),
    "z_all": ((N_GY, CX, LANES, 256), F32),
    "gsend": ((2, N_GY, N_Y, *BIG), F32),
    "grecv": ((2, 15, *BIG), F32),
    "g12": ((288, 128), F32),
    "msend": ((2, 128, 128), F32),
    "mrecv": ((2, 15, *TILE), F32),
    "qbuf": ((2, *TILE), F32),
    "qsend": ((2, *TILE), F32),
    "qrecv": (TILE, F32),
    "sums": ((N_GY, 16, 128), F32),
    "grads": (TILE, F32),
    "rsend": ((2, *TILE), F32),
    "rall": ((2, 128, 128), F32),
    "hsend": ((2, N_Y, *BIG), F32),
    "hall": ((2, N_Y, N_GY, *BIG), F32),
    "hx": ((CX, N_GY, 24, 256), F32),
    "wsend": ((8, 8, 512), F32),
    "wrecv": ((8, 8, 512), F32),
    "esend": ((2, *TILE), F32),
    "erecv": ((2, *TILE), F32),
    "owned": ((2 * C * Q, 128), F32),
    "home_modes": ((8, 2, *TILE), F32),
    "home_grads": ((8, *TILE), F32),
    "block_modes": ((64, 128), F32),
}
SEMAPHORES = {
    "load_sem": (13,),
    "cell_sem": (2, CX),
    "plane_sem": (2, 2, 2, 15),
    "column_sem": (2, 2, 2, 15),
    "core_sem": (2, 2),
    "w_sem": (2, 8),
    "e_sem": (2, 2),
    "home_sem": (2, 2, 8),
}


def layer_kernel(*refs):
    ref = types.SimpleNamespace(**dict(zip(INPUTS + OUTPUTS + list(SCRATCH) + list(SEMAPHORES), refs)))

    slab, gy = lax.axis_index("slab"), lax.axis_index("gy")
    yy, rr = lax.div(slab, N_R), lax.rem(slab, N_R)
    x_hi, core = lax.div(gy, 2), lax.rem(gy, 2)
    x_lo, z = lax.div(rr, 8), lax.rem(rr, 8)
    turn, half = lax.rem(z, 4), lax.div(z, 4)
    mine = 4 * x_hi + yy
    near = x_lo * 8 + half * 4

    sources = {
        "depth": ref.depth,
        "y_table": ref.y_table.at[gy],
        "weight": ref.weight,
        "select": ref.select.at[turn],
        "place": ref.place.at[mine],
        "rows": ref.rows.at[rr],
        "expand": ref.expand,
        "keep": ref.keep,
        "gather": ref.gather.at[turn],
        "lw": ref.lw,
        "repeat": ref.repeat,
        "depth_back": ref.depth_back,
        "y_back": ref.y_back.at[gy],
    }
    loads = {
        name: pltpu.make_async_copy(source, getattr(ref, "v_" + name), ref.load_sem.at[k])
        for k, (name, source) in enumerate(sources.items())
    }
    fields = [pltpu.make_async_copy(ref.field.at[:, x], ref.v_field.at[x], ref.cell_sem.at[0, x]) for x in range(CX)]
    cots = [pltpu.make_async_copy(ref.cot.at[:, x], ref.v_cot.at[x], ref.cell_sem.at[1, x]) for x in range(CX)]
    fields[0].start()
    loads["depth"].start()
    loads["y_table"].start()
    fields[1].start()
    fields[2].start()
    for name in list(loads)[2:]:
        loads[name].start()
    for copy in cots:
        copy.start()

    def ready(*names):
        for name in names:
            loads[name].wait()

    def plane(k):
        d_hi, d_core, dy = PLANE[k]
        g_to = lax.rem(x_hi + d_hi, 2) * 2 + lax.rem(core + d_core, 2)
        y_to = lax.rem(yy + dy, N_Y)
        return g_to, y_to, {"gy": g_to, "slab": y_to * N_R + rr}

    def column(k):
        d_lo, dz = COLUMN[k]
        r_to = lax.rem(x_lo + d_lo, 2) * 8 + lax.rem(z + dz, 8)
        return r_to, {"slab": yy * N_R + r_to}

    def across(slab_of):
        found = []
        for d_hi in range(2):
            to_hi = lax.rem(x_hi + d_hi, 2)
            for k in range(4):
                to = slab_of(k)
                found.append((to_hi, k, to, (to != slab) if d_hi == 0 else None))
        return found

    owners = across(lambda k: k * N_R + near + yy)
    blocks = across(lambda k: turn * N_R + near + k)
    at_home = (turn == yy).astype(jnp.int32)

    def guarded(away, action):
        if away is None:
            action()
        else:
            pl.when(away)(action)

    def device_of(to_hi, to):
        return {"gy": to_hi * 2 + core, "slab": to}

    barrier = pltpu.get_barrier_semaphore()

    def greet(device):
        pl.semaphore_signal(barrier, inc=1, device_id=device, device_id_type=MESH)

    for k in range(15):
        greet(plane(k)[2])
        greet(column(k)[1])
    for to_hi, _, to, away in owners + blocks:
        guarded(away, functools.partial(greet, device_of(to_hi, to)))

    def copy_to(source, target, send_sem, recv_sem, device):
        return pltpu.make_async_remote_copy(
            src_ref=source,
            dst_ref=target,
            send_sem=send_sem,
            recv_sem=recv_sem,
            device_id=device,
            device_id_type=MESH,
        )

    started = []

    def start_all(sem, copies):
        made = [copy_to(a, b, sem.at[0, k], sem.at[1, k], device) for k, (a, b, device) in enumerate(copies)]
        for copy in made:
            copy.start()
        started.extend((None, copy) for copy in made)
        return made

    def finish(made):
        for copy in made:
            copy.wait_recv()

    plane_to = [plane(k) for k in range(15)]
    column_to = [column(k) for k in range(15)]
    slot = {d: k for k, d in enumerate(PLANE)}

    def window(r):
        return pl.ds(pl.multiple_of(r * 8, 8), 8)

    def send_home(index, source, target):
        sem = ref.home_sem.at[index]
        for k, (to_hi, _, to, away) in enumerate(blocks):
            copy = copy_to(source, target.at[mine], sem.at[0, k], sem.at[1, mine], device_of(to_hi, to))
            guarded(away, copy.start)
            started.append((away, copy))

        @pl.when(turn == yy)
        def _():
            target[mine] = source[...]

    def come_home(index, source, target):
        sem = ref.home_sem.at[index]
        for k, (from_hi, y, origin, away) in enumerate(owners):
            place = 4 * from_hi + y
            copy = copy_to(source, target.at[place], sem.at[0, k], sem.at[1, place], device_of(from_hi, origin))
            guarded(away, copy.wait_recv)

    def in_block_order(messages):
        rows = []
        for n in range(4):
            rows.append(jnp.concatenate([m[:, OWN * n : OWN * n + OWN] for m in messages], axis=1))
        return dot(jnp.concatenate(rows, axis=0), ref.v_gather[...], NN, HIGHEST)

    def depth_stage(cells_of, x):
        for pair in range(2):
            pieces = [cells_of(x, slice((2 * pair + h) * Q, (2 * pair + h + 1) * Q)).reshape(Q * TZ, Y) for h in range(2)]
            zz = dot(ref.v_depth[...], jnp.concatenate(pieces, axis=1), NN)
            for h in range(2):
                part = zz[:, h * Y : (h + 1) * Y]
                ref.z_all[2 * pair + h, x, :, 0:Y] = part[:LANES]
                ref.z_all[2 * pair + h, x, :, Y:] = part[LANES:]

    def to_window(index, local, beside_first, beside_second):
        table = ref.v_y_table[...]
        gsend, grecv = ref.gsend.at[index], ref.grecv.at[index]
        for g in range(N_GY):
            for y in range(N_Y):
                lanes = slice(24 * (4 * (g // 2) + y), 24 * (4 * (g // 2) + y) + 24)
                rows = [ref.z_all[q, x, lanes, :] for x in range(CX) for q in (g % 2, g % 2 + 2)]
                piece = dot(table, jnp.concatenate(rows, axis=0).astype(BF16), NT_DIMS)
                corner = [] if local is None else [local[8 * g : 8 * g + 8, 8 * y : 8 * y + 8]]
                gsend[g, y] = pack(piece, corner)
        if index == 0:
            pl.semaphore_wait(barrier, 30 + 16 - 2 * at_home)
        sem = ref.plane_sem.at[index, 0]
        first = start_all(sem, [(gsend.at[g, y], grecv.at[k], to) for k, (g, y, to) in enumerate(plane_to)])
        beside_first()
        finish(first)
        block = jnp.zeros((8, 8), F32)
        for dy in range(N_Y):
            total = gsend[gy, yy] if dy == 0 else None
            for d_hi in range(2):
                for d_core in range(2):
                    if (d_hi, d_core, dy) in slot:
                        term = grecv[slot[d_hi, d_core, dy]]
                        total = term if total is None else total + term
            block = block + total[24:32, 48:56]
            base = lax.rem(yy + N_Y - dy, N_Y) * ROWS
            for x, piece in enumerate(unpack(total)):
                ref.g12[pl.ds(pl.multiple_of(base + 24 * x, 8), 24), 0:48] = piece

        f = product(ref.v_rows, 0, ref.g12[:, 0:48])
        msend, mrecv = ref.msend.at[index], ref.mrecv.at[index]
        blank = jnp.zeros((128, 24), F32)
        msend[...] = jnp.concatenate([f[0:128], f[128:256], blank, jnp.concatenate([block] * N_R, axis=0)], axis=1)
        ninth = jnp.concatenate([f[256:272], f[272:288]], axis=1)
        for j in range(4):
            old = msend[pl.ds(j, N_R, stride=8), :]
            msend[pl.ds(j, N_R, stride=8), :] = jnp.concatenate(
                [old[:, 0:96], ninth[:, 24 * j : 24 * j + 24], old[:, 120:128]], axis=1
            )
        sem = ref.column_sem.at[index, 0]
        second = start_all(sem, [(msend.at[window(r)], mrecv.at[k], to) for k, (r, to) in enumerate(column_to)])
        beside_second()
        finish(second)
        m = msend[window(rr), :]
        for k in range(15):
            m = m + mrecv[k]

        last = jnp.concatenate([m[j : j + 1, 96:120] for j in range(4)], axis=1)
        nine = jnp.concatenate([m[:, 0:96], last, jnp.zeros((7, 96), F32)], axis=0)
        spread = dot(nine, ref.v_expand[...], TN, HIGHEST) * ref.v_keep[...]
        parts = {}
        for n in range(4):
            base = 24 * n
            total = spread[base : base + 8] + spread[base + 8 : base + 16] + spread[base + 16 : base + 24]
            parts[n // 2, n % 2] = total[:, 0:OWN]
        return parts, m[:, 120:128]

    def packed(parts):
        end = jnp.zeros((Q, 128 - 4 * OWN), F32)
        return jnp.concatenate([parts[part, h] for h in range(2) for part in range(2)] + [end], axis=1)

    def from_mixed(index, mixed, corner, beside_first, beside_second):
        pad = jnp.zeros((Q, 128 - OWN), F32)
        wide = [jnp.concatenate([mixed[part, h], pad], axis=1) for part in range(2) for h in range(2)]
        tiled = jnp.concatenate([v for v in wide for _ in range(3)], axis=0) * ref.v_keep[...]
        u = dot(ref.v_expand[...], tiled, NT_DIMS, HIGHEST)
        last = jnp.concatenate([u[8:9, 24 * j : 24 * j + 24] for j in range(4)] + [jnp.zeros((4, 24), F32)], axis=0)
        rsend, rall = ref.rsend.at[index], ref.rall.at[index]
        rsend[...] = jnp.concatenate([u[0:8], last, jnp.zeros((8, 8), F32)], axis=1)
        rall[window(rr), :] = rsend[...]
        sem = ref.column_sem.at[index, 1]
        third = start_all(sem, [(rsend, rall.at[window(rr)], to) for _, to in column_to])
        beside_first()
        finish(third)
        ninth = jnp.concatenate([rall[pl.ds(j, N_R, stride=8), :][:, 96:120] for j in range(4)], axis=1)
        f = jnp.concatenate([rall[:, 0:48], rall[:, 48:96], ninth[:, 0:48], ninth[:, 48:96]], axis=0)
        h = product(ref.v_rows, 2, f)
        hsend, hall = ref.hsend.at[index], ref.hall.at[index]
        for y in range(N_Y):
            rows = [h[y * ROWS + 24 * x : y * ROWS + 24 * x + 24] for x in range(CX)]
            hsend[y] = pack(jnp.concatenate(rows, axis=1), corner)
        hall[yy, gy] = hsend[yy]
        sem = ref.plane_sem.at[index, 1]
        fourth = start_all(sem, [(hsend.at[y], hall.at[yy, gy], to) for _, y, to in plane_to])
        beside_second()
        finish(fourth)
        for y in range(N_Y):
            for g in range(N_GY):
                base = 24 * (4 * (g // 2) + y)
                for x, piece in enumerate(unpack(hall[y, g])):
                    for h in range(2):
                        ref.hx[x, 2 * h + g % 2, :, base : base + 24] = piece[:, 24 * h : 24 * h + 24]

    def spectral_rows(x):
        for pair in range(2):
            halves = []
            for q in (2 * pair, 2 * pair + 1):
                h = ref.hx[x, q, :, 0:LANES]
                high = h.astype(BF16).astype(F32)
                stacked = jnp.concatenate([high, high, h - high], axis=0).astype(BF16)
                u = dot(stacked, ref.v_y_back[...], TN)
                halves.append(jnp.concatenate([u[:, :Y], u[:, Y:]], axis=0).astype(BF16))
            s = dot(ref.v_depth_back[...], jnp.concatenate(halves, axis=1), NN)
            for h in range(2):
                q = 2 * pair + h
                ref.spec[q * Q : (q + 1) * Q] = s[:, h * Y : (h + 1) * Y].reshape(Q, TZ, Y)

    ready("depth", "y_table")
    for x in range(CX):
        fields[x].wait()
        depth_stage(lambda x, c: ref.v_field[x, c], x)

    def send_weights():
        ready("weight", "select", "place")
        flat = ref.v_weight[...].astype(F32).reshape(2 * C * Q, BLOCK).astype(BF16)
        picked = dot(ref.v_select[...][:, 0:BLOCK].astype(BF16), flat, NT_DIMS)
        for k in range(8):
            ref.wsend[k] = picked[8 * k : 8 * k + 8]
        for e in range(2):
            row = picked[64 + e : 65 + e]
            lanes = [row[:, 128 * j : 128 * j + 128] for j in range(4)]
            ref.esend[e] = jnp.concatenate([*lanes, jnp.zeros((4, 128), F32)], axis=0)
        own = 2 * turn + x_hi
        for k, (to_hi, y, to, away) in enumerate(owners):
            source = ref.wsend.at[4 * to_hi + y]
            copy = copy_to(source, ref.wrecv.at[own], ref.w_sem.at[0, k], ref.w_sem.at[1, own], device_of(to_hi, to))
            guarded(away, copy.start)
            started.append((away, copy))
        for e in range(2):
            to_hi, y = lax.div(turn, 2), lax.rem(2 * turn, 4) + e
            to = y * N_R + near + yy
            copy = copy_to(
                ref.esend.at[e], ref.erecv.at[x_hi], ref.e_sem.at[0, e], ref.e_sem.at[1, x_hi], device_of(to_hi, to)
            )
            here = jnp.logical_and(to_hi == x_hi, to == slab)
            away = jnp.logical_not(here)
            pl.when(away)(copy.start)
            started.append((away, copy))

            @pl.when(here)
            def _():
                ref.erecv[x_hi] = ref.esend[e]

        @pl.when(turn == yy)
        def _():
            ref.wrecv[own] = ref.wsend[mine]

        ready("rows", "expand", "keep")

    def receive_weights():
        for k, (from_hi, t, origin, away) in enumerate(blocks):
            at = 2 * t + from_hi
            copy = copy_to(
                ref.wsend.at[0], ref.wrecv.at[at], ref.w_sem.at[0, k], ref.w_sem.at[1, at], device_of(from_hi, origin)
            )
            guarded(away, copy.wait_recv)
        origin = turn * N_R + near + lax.div(mine, 2)
        for hi in range(2):
            copy = copy_to(
                ref.esend.at[0], ref.erecv.at[hi], ref.e_sem.at[0, hi], ref.e_sem.at[1, hi], device_of(hi, origin)
            )
            pl.when(jnp.logical_or(x_hi != hi, origin != slab))(copy.wait_recv)
        ninths = [jnp.concatenate([ref.erecv[hi, j : j + 1, :] for j in range(4)], axis=1) for hi in range(2)]
        received = jnp.concatenate([ref.wrecv[...].reshape(64, 512), *ninths, jnp.zeros((6, 512), F32)], axis=0)
        ref.owned[...] = dot(received.astype(BF16), ref.v_place[...].astype(BF16), TN)

    def local_products(weight_transposed, cells_of):
        kron = channel_matrix(ref.v_lw[...], ref.v_repeat[...], weight_transposed)
        for n in range(CX * CHUNKS):
            ref.local_part[n] = dot(kron, cells_of(n), NN)

    def prepare_cells():
        ready("lw", "repeat", "depth_back", "y_back", "gather")
        for copy in cots:
            copy.wait()
        for x in range(CX):
            for r in range(CHUNKS):
                n = x * CHUNKS + r
                ref.cells[n] = chunk_of(ref.v_field[x, :, 16 * r : 16 * r + 16, :]).astype(BF16)
                ref.cot_cells[n] = chunk_of(ref.v_cot[x, :, 16 * r : 16 * r + 16, :])

    def beside_column():
        receive_weights()
        prepare_cells()

    parts, _ = to_window(0, None, send_weights, beside_column)

    other_core = {"gy": x_hi * 2 + 1 - core}
    ref.qbuf[core] = packed(parts)
    copy = copy_to(ref.qbuf.at[core], ref.qbuf.at[core], ref.core_sem.at[0, 0], ref.core_sem.at[0, 1], other_core)
    copy.start()
    copy.wait_recv()
    started.append((None, copy))
    mixed_r = jnp.zeros((Q, BLOCK), F32)
    mixed_i = jnp.zeros((Q, BLOCK), F32)

    def weights(i):
        return ref.owned[8 * i : 8 * i + 8, 0:BLOCK], ref.owned[256 + 8 * i : 264 + 8 * i, 0:BLOCK]

    for q in range(N_GY):
        both = ref.qbuf[q % 2]
        base = 2 * OWN * (q // 2)
        real, imag = both[:, base : base + OWN], both[:, base + OWN : base + 2 * OWN]
        real, imag = jnp.concatenate([real, real], axis=1), jnp.concatenate([imag, imag], axis=1)
        for c in range(Q):
            mr, mi = real[c : c + 1], imag[c : c + 1]
            w0, w1 = weights(q * Q + c)
            mixed_r = mixed_r + (mr * w0 - mi * w1)
            mixed_i = mixed_i + (mr * w1 + mi * w0)
    mixed = {(p, h): v[:, OWN * h : OWN * h + OWN] for p, v in enumerate((mixed_r, mixed_i)) for h in range(2)}

    def beside_modes():
        send_home(0, ref.qbuf, ref.home_modes)
        local_products(True, lambda n: ref.cells[n])

    def modes_home():
        come_home(0, ref.qbuf, ref.home_modes)
        ref.block_modes[...] = in_block_order([ref.home_modes[k].reshape(16, 128) for k in range(8)])

    from_mixed(0, mixed, [], beside_modes, modes_home)

    ref.acc[...] = jnp.zeros_like(ref.acc)
    for x in range(CX):
        spectral_rows(x)
        for r in range(CHUNKS):
            n = x * CHUNKS + r
            rows = slice(16 * r, 16 * r + 16)
            pre = chunk_of(ref.spec[:, rows, :]) + ref.local_part[n]
            cdf = 0.5 * (1.0 + lax.erf(pre * ROOT_HALF))
            slope = cdf + pre * jnp.exp(-0.5 * pre * pre) * INV_ROOT_TWO_PI
            grad = ref.cot_cells[n] * slope
            ref.out[:, x, rows, :] = unchunk(pre * cdf).astype(BF16)
            ref.grad_pre[x, :, rows, :] = unchunk(grad).astype(BF16)
            ref.acc[...] += dot(ref.cells[n], grad.astype(BF16), NT_DIMS)
        depth_stage(lambda x, c: ref.grad_pre[x, c], x)
    kept = jnp.where(same_row((256, 256)), ref.acc[...], 0.0)
    repeat = ref.v_repeat[...].astype(F32)
    local = dot(dot(repeat, kept, TN, HIGHEST), repeat, NN, HIGHEST)

    def chunk_grad(n):
        x, r = divmod(n, CHUNKS)
        return chunk_of(ref.grad_pre[x, :, 16 * r : 16 * r + 16, :]).astype(BF16)

    parts, total_local = to_window(1, local, lambda: None, lambda: local_products(False, chunk_grad))
    ref.grads[...] = packed(parts)
    gr, gi = (jnp.concatenate([parts[p, 0], parts[p, 1]], axis=1) for p in range(2))
    for i in range(C):
        q, c = divmod(i, Q)
        w0, w1 = weights(i)
        ref.sums[q, c : c + 1, 0:BLOCK] = jnp.sum(gr * w0 + gi * w1, axis=0, keepdims=True)
        ref.sums[q, 8 + c : 9 + c, 0:BLOCK] = jnp.sum(gi * w0 - gr * w1, axis=0, keepdims=True)
    for k in range(2):
        found = {}
        for h in range(2):
            both = ref.sums[2 * h + k]
            both = both[:, 0:OWN] + both[:, OWN:BLOCK]
            found[0, h], found[1, h] = both[0:8], both[8:16]
        ref.qsend[k] = packed(found)
    copy = copy_to(ref.qsend.at[1 - core], ref.qrecv, ref.core_sem.at[1, 0], ref.core_sem.at[1, 1], other_core)
    copy.start()
    copy.wait_recv()
    started.append((None, copy))
    both = ref.qsend[core] + ref.qrecv[...]
    mixed = {(p, h): both[:, OWN * (2 * h + p) : OWN * (2 * h + p) + OWN] for p in range(2) for h in range(2)}

    def weight_gradient():
        come_home(1, ref.grads, ref.home_grads)
        grads = in_block_order([ref.home_grads[k] for k in range(8)])
        grads = jnp.where(x_hi == 0, grads[0:16], grads[16:32])
        gr, gi = grads[0:8, 0:BLOCK], grads[8:16, 0:BLOCK]
        for i in range(C):
            q, c = divmod(i, Q)
            row = 32 * (q // 2) + 8 * (q % 2) + c
            mr, mi = ref.block_modes[row : row + 1, 0:BLOCK], ref.block_modes[row + 16 : row + 17, 0:BLOCK]
            ref.grad_spectral[0, i] = mr * gr + mi * gi
            ref.grad_spectral[1, i] = mr * gi - mi * gr

    from_mixed(1, mixed, [total_local], lambda: send_home(1, ref.grads, ref.home_grads), weight_gradient)
    for y in range(N_Y):
        for g in range(N_GY):
            corner = ref.hall[1, y, g, 24:32, 48:56]
            ref.grad_local[8 * g : 8 * g + 8, 8 * y : 8 * y + 8] = corner * FORWARD_SCALE
    for x in range(CX):
        spectral_rows(x)
        for r in range(CHUNKS):
            rows = slice(16 * r, 16 * r + 16)
            total = chunk_of(ref.spec[:, rows, :]) + ref.local_part[x * CHUNKS + r]
            ref.grad_in[:, x, rows, :] = unchunk(total).astype(BF16)
    for away, copy in started:
        guarded(away, copy.wait_send)


def per_device(field_in, cotangent, spectral_weight, local_weight):
    cells = (C, CX, TZ, Y)
    depth = depth_table()
    tables = y_tables()
    high = tables.astype(BF16)
    low = (tables - high.astype(np.float64)).astype(BF16)
    expand, keep = unit_tables()
    select, place, gather = owner_tables()
    values = {
        "field": field_in.reshape(cells),
        "cot": cotangent.reshape(cells),
        "weight": jnp.transpose(spectral_weight, (0, 2, 3, 1)),
        "lw": local_weight,
        "depth": depth.astype(BF16),
        "depth_back": np.ascontiguousarray(depth.T).astype(BF16),
        "y_table": high,
        "y_back": np.concatenate([high, low, high], axis=1),
        "rows": row_tables(),
        "expand": expand,
        "keep": keep,
        "select": select.astype(np.float32),
        "place": place.astype(np.float32),
        "gather": gather.astype(np.float32),
        "repeat": np.repeat(np.eye(C), 8, axis=0).astype(BF16),
    }
    outs = [(cells, BF16), (cells, BF16), ((2, C, Q, BLOCK), F32), ((C, C), F32)]
    output, grad_input, grad_spectral, grad_local = pl.pallas_call(
        layer_kernel,
        out_shape=[jax.ShapeDtypeStruct(shape, dtype) for shape, dtype in outs],
        in_specs=[pl.BlockSpec(memory_space=pltpu.HBM) for _ in INPUTS],
        out_specs=[pl.BlockSpec(memory_space=pltpu.VMEM) for _ in OUTPUTS],
        scratch_shapes=[pltpu.VMEM(shape, dtype) for shape, dtype in SCRATCH.values()]
        + [DMA(shape) for shape in SEMAPHORES.values()],
        compiler_params=pltpu.CompilerParams(
            collective_id=0, has_side_effects=True, vmem_limit_bytes=56 * 1024 * 1024
        ),
        name="spectral_layer",
    )(*[jnp.asarray(values[name]) for name in INPUTS])
    return (
        output.reshape(field_in.shape),
        grad_input.reshape(field_in.shape),
        jnp.transpose(grad_spectral, (0, 3, 1, 2)),
        grad_local,
    )


def solution(mesh):
    placed = (
        P(None, "slab", None, None, "gy"),
        P(None, "slab", None, None, "gy"),
        P(None, "slab", None, "gy"),
        P(),
    )
    return jax.shard_map(
        per_device,
        mesh=mesh,
        in_specs=placed,
        out_specs=(
            P(None, "slab", None, None, "gy"),
            P(None, "slab", None, None, "gy"),
            P(None, "slab", None, "gy"),
            P(),
        ),
        check_vma=False,
    )
```

```python
import functools
import math
import types

import jax
import jax.numpy as jnp
import numpy as np
from jax import lax
from jax.experimental import pallas as pl
from jax.experimental.pallas import tpu as pltpu
from jax.sharding import PartitionSpec as P

C = 32
KX = 12
KY = 12
KZ = 12
NT = 2
NZ = 32
NX = 192
NY = 512
CX = 3
N_GY = 4
N_Y = 4
N_R = 16
Q = C // N_GY
K = NT * KZ
TZ = NT * NZ
Y = NY // N_GY
BLOCK = 54
OWN = 27
UNITS = 9
ROWS = 72
LANES = K * Q

FORWARD_SCALE = 1.0 / math.sqrt(NX * NY * NZ * NT)
INVERSE_SCALE = 1.0 / math.sqrt(KX * KY * KZ * NT)
ROOT_HALF = 0.7071067811865476
INV_ROOT_TWO_PI = 0.3989422804014327
HIGHEST = lax.Precision.HIGHEST
PLANE = [(h, c, y) for h in range(2) for c in range(2) for y in range(N_Y) if (h, c, y) != (0, 0, 0)]
PLANE.sort(key=lambda d: -(2 * d[0] + min(d[2], N_Y - d[2])))
COLUMN = [(x, z) for x in range(2) for z in range(8) if (x, z) != (0, 0)]
COLUMN.sort(key=lambda d: -(d[0] + min(d[1], 8 - d[1])))
F32 = jnp.float32
BF16 = jnp.bfloat16
MESH = pl.DeviceIdType.MESH


def frequencies(kept):
    values = np.arange(kept)
    return np.where(values < kept // 2, values, values - kept)


def depth_table():
    t, z = np.divmod(np.arange(TZ), NZ)
    kt, kz = np.divmod(np.arange(K), KZ)
    product = (t[None] * kt[:, None] * NZ + z[None] * frequencies(KZ)[kz][:, None] * NT) % TZ
    angle = product * (2.0 * np.pi / TZ)
    parts = np.stack([np.cos(angle), -np.sin(angle)])
    full = np.einsum("pks,cd->pkcds", parts, np.eye(Q))
    return full.reshape(2 * K * Q, Q * TZ)


def y_tables():
    product = (frequencies(KY)[:, None] * np.arange(NY)[None]) % NY
    angle = product * (2.0 * np.pi / NY)
    cos, sin = np.cos(angle), np.sin(angle)
    full = np.stack([np.stack([cos, sin]), np.stack([-sin, cos])])
    full = full.reshape(2, 2, KY, N_GY, Y).transpose(3, 0, 2, 1, 4)
    return full.reshape(N_GY, 2 * KY, 2 * Y)


def unit_tables():
    lane = np.arange(128)
    row = np.arange(96)
    expand = (lane[None] // 3 == np.arange(16)[:, None]) & (lane[None] < OWN)
    keep = ((row[:, None] // 8) % 3 == lane[None] % 3) & (lane[None] < OWN)
    return expand.astype(np.float32), keep.astype(np.float32)


def row_tables():
    main = [9 * w + j for w in range(N_R) for j in range(8)]
    ninth = [9 * w + 8 for w in range(N_R)]
    pairs = np.array(main + main + ninth + ninth)
    part = np.array([0] * 128 + [1] * 128 + [0] * 16 + [1] * 16)
    y, x, part_in, ky = np.unravel_index(np.arange(288), (N_Y, CX, 2, KY))
    row = 48 * y[None] + 3 * np.arange(N_R)[:, None] + x[None]
    freq = frequencies(KX)[pairs // KY]
    angle = (freq[None, :, None] * row[:, None, :]) % NX * (2.0 * np.pi / NX)
    sign = np.where(part == 0, 1.0, -1.0)[:, None]
    value = np.where(part[:, None] == part_in[None], np.cos(angle), sign * np.sin(angle))
    value = np.where((pairs % KY)[:, None] == ky[None], value, 0.0)
    forward, inverse = value * FORWARD_SCALE, value.transpose(0, 2, 1) * INVERSE_SCALE
    parts = []
    for full in (forward, inverse):
        high = full.astype(BF16)
        parts += [high, (full - high.astype(np.float64)).astype(BF16)]
    return np.stack(parts, axis=1)


def owner_tables():
    select = np.zeros((4, 72, 128))
    place = np.zeros((8, 72, 128))
    gather = np.zeros((4, 8, OWN, 128))
    for t in range(4):
        count = [0] * 8
        for mode in range(BLOCK):
            unit = 18 * t + mode // 3
            part, other = unit % 8, 3 * (unit // 8) + mode % 3
            n = count[part]
            count[part] += 1
            select[t, 8 * part + n if n < 8 else 64 + part - 2 * t, mode] = 1.0
            for x in range(2):
                place[part, 16 * t + 8 * x + n if n < 8 else 64 + x, OWN * x + other] = 1.0
            gather[t, part, other, mode] = 1.0
    return select, place, gather.reshape(4, 8 * OWN, 128)


def dot(a, b, dims, precision=None):
    return lax.dot_general(a, b, (dims, ((), ())), precision=precision, preferred_element_type=F32)


NN = ((1,), (0,))
NT_DIMS = ((1,), (1,))
TN = ((0,), (0,))


def pack(g, corner):
    tail = g[:, 128:144]
    width = 80 - 8 * len(corner)
    below = jnp.concatenate([tail[0:8], tail[8:16], tail[16:24], *corner, jnp.zeros((8, width), F32)], axis=1)
    return jnp.concatenate([g[:, 0:128], below], axis=0)


def unpack(message):
    below = message[24:32]
    tail = jnp.concatenate([below[:, 0:16], below[:, 16:32], below[:, 32:48]], axis=0)
    body = message[0:24]
    return [body[:, 0:48], body[:, 48:96], jnp.concatenate([body[:, 96:128], tail], axis=1)]


def halves_of(values):
    high = values.astype(BF16)
    return high, (values - high.astype(F32)).astype(BF16)


def product(rows_ref, first, values):
    high, low = halves_of(values)
    both = dot(rows_ref[first], jnp.concatenate([high, low], axis=1), NN)
    width = values.shape[1]
    return both[:, :width] + both[:, width:] + dot(rows_ref[first + 1], high, NN)


def chunk_of(values):
    values = values.astype(F32)
    return jnp.concatenate([values[:, 0:8].reshape(256, Y), values[:, 8:16].reshape(256, Y)], axis=1)


def unchunk(values):
    halves = [values[:, :Y].reshape(C, 8, Y), values[:, Y:].reshape(C, 8, Y)]
    return jnp.concatenate(halves, axis=1)


def same_row(shape):
    row = lax.broadcasted_iota(jnp.int32, shape, 0)
    col = lax.broadcasted_iota(jnp.int32, shape, 1)
    return row % 8 == col % 8


def channel_matrix(weight, repeat, transposed):
    half = dot(repeat, weight, NT_DIMS if transposed else NN).astype(BF16)
    full = dot(half, repeat, NT_DIMS)
    return jnp.where(same_row(full.shape), full, 0.0).astype(BF16)


CHUNKS = TZ // 16
BIG = (32, 128)
TILE = (8, 128)
DMA = pltpu.SemaphoreType.DMA

INPUTS = ["field", "cot", "weight", "lw", "depth", "depth_back", "y_table", "y_back", "rows", "expand", "keep"]
INPUTS += ["select", "place", "gather", "repeat"]
OUTPUTS = ["out", "grad_cells", "grad_spectral", "hx", "grad_local"]
SCRATCH = {
    "v_field": ((CX, C, TZ, Y), BF16),
    "v_cot": ((CX, C, TZ, Y), BF16),
    "v_weight": ((2, C, Q, BLOCK), BF16),
    "v_lw": ((C, C), BF16),
    "v_depth": ((2 * K * Q, Q * TZ), BF16),
    "v_depth_back": ((Q * TZ, 2 * K * Q), BF16),
    "v_y_table": ((2 * KY, 2 * Y), BF16),
    "v_y_back": ((6 * KY, 2 * Y), BF16),
    "v_rows": ((4, 288, 288), BF16),
    "v_expand": ((16, 128), F32),
    "v_keep": ((96, 128), F32),
    "v_select": ((72, 128), F32),
    "v_place": ((72, 128), F32),
    "v_gather": ((8 * OWN, 128), F32),
    "v_repeat": ((256, C), BF16),
    "grad_pre": ((CX, C, TZ, Y), BF16),
    "spec": ((C, TZ, Y), F32),
    "cells": ((CX * CHUNKS, 256, 256), BF16),
    "cot_cells": ((CX * CHUNKS, 256, 256), F32),
    "local_part": ((CX * CHUNKS, 256, 256), F32),
    "lsend": ((N_GY, N_Y, *TILE), F32),
    "lrecv": ((15, *TILE), F32),
    "z_all": ((N_GY, CX, LANES, 256), F32),
    "gsend": ((2, N_GY, N_Y, *BIG), F32),
    "grecv": ((2, 15, *BIG), F32),
    "g12": ((288, 128), F32),
    "msend": ((2, 128, 128), F32),
    "mrecv": ((2, 15, *TILE), F32),
    "qbuf": ((2, *TILE), F32),
    "qsend": ((2, *TILE), F32),
    "qrecv": (TILE, F32),
    "sums": ((N_GY, 16, 128), F32),
    "grads": (TILE, F32),
    "rsend": ((2, *TILE), F32),
    "rall": ((2, 128, 128), F32),
    "hsend": ((2, N_Y, *BIG), F32),
    "hall": ((2, N_Y, N_GY, *BIG), F32),
    "v_out": ((CX, C, TZ, Y), BF16),
    "v_grad_spectral": ((2, C, Q, BLOCK), F32),
    "wsend": ((8, 8, 512), F32),
    "wrecv": ((8, 8, 512), F32),
    "esend": ((2, *TILE), F32),
    "erecv": ((2, *TILE), F32),
    "owned": ((2 * C * Q, 128), F32),
    "home_modes": ((8, 2, *TILE), F32),
    "home_grads": ((8, *TILE), F32),
    "block_modes": ((64, 128), F32),
}
SEMAPHORES = {
    "load_sem": (13,),
    "cell_sem": (2, CX),
    "store_sem": (2 * CX + 1,),
    "plane_sem": (2, 2, 2, 15),
    "column_sem": (2, 2, 2, 15),
    "core_sem": (2, 2),
    "local_sem": (2, 15),
    "w_sem": (2, 8),
    "e_sem": (2, 2),
    "home_sem": (2, 2, 8),
}


def spectral_rows(hx, y_back, depth_back, spec, x):
    for pair in range(2):
        halves = []
        for q in (2 * pair, 2 * pair + 1):
            h = hx[x, q, :, 0:LANES]
            high = h.astype(BF16).astype(F32)
            stacked = jnp.concatenate([high, high, h - high], axis=0).astype(BF16)
            u = dot(stacked, y_back[...], TN)
            halves.append(jnp.concatenate([u[:, :Y], u[:, Y:]], axis=0).astype(BF16))
        s = dot(depth_back[...], jnp.concatenate(halves, axis=1), NN)
        for h in range(2):
            q = 2 * pair + h
            spec[q * Q : (q + 1) * Q] = s[:, h * Y : (h + 1) * Y].reshape(Q, TZ, Y)


def layer_kernel(*refs):
    ref = types.SimpleNamespace(**dict(zip(INPUTS + OUTPUTS + list(SCRATCH) + list(SEMAPHORES), refs)))

    slab, gy = lax.axis_index("slab"), lax.axis_index("gy")
    yy, rr = lax.div(slab, N_R), lax.rem(slab, N_R)
    x_hi, core = lax.div(gy, 2), lax.rem(gy, 2)
    x_lo, z = lax.div(rr, 8), lax.rem(rr, 8)
    turn, half = lax.rem(z, 4), lax.div(z, 4)
    mine = 4 * x_hi + yy
    near = x_lo * 8 + half * 4
    from_y = lax.rem(turn + 4 - yy, 4)
    own_window = from_y * 4 + x_lo * 2 + half
    home = turn == lax.rem(2 * yy, 4)

    sources = {
        "depth": ref.depth,
        "y_table": ref.y_table.at[gy],
        "weight": ref.weight,
        "select": ref.select.at[turn],
        "place": ref.place.at[mine],
        "rows": ref.rows.at[rr],
        "expand": ref.expand,
        "keep": ref.keep,
        "gather": ref.gather.at[turn],
        "lw": ref.lw,
        "repeat": ref.repeat,
        "depth_back": ref.depth_back,
        "y_back": ref.y_back.at[gy],
    }
    loads = {
        name: pltpu.make_async_copy(source, getattr(ref, "v_" + name), ref.load_sem.at[k])
        for k, (name, source) in enumerate(sources.items())
    }
    fields = [pltpu.make_async_copy(ref.field.at[:, x], ref.v_field.at[x], ref.cell_sem.at[0, x]) for x in range(CX)]
    cots = [pltpu.make_async_copy(ref.cot.at[:, x], ref.v_cot.at[x], ref.cell_sem.at[1, x]) for x in range(CX)]
    fields[0].start()
    loads["depth"].start()
    loads["y_table"].start()
    fields[1].start()
    fields[2].start()
    for name in list(loads)[2:]:
        loads[name].start()
    for copy in cots:
        copy.start()

    def ready(*names):
        for name in names:
            loads[name].wait()

    def plane(k):
        d_hi, d_core, dy = PLANE[k]
        g_to = lax.rem(x_hi + d_hi, 2) * 2 + lax.rem(core + d_core, 2)
        y_to = lax.rem(yy + dy, N_Y)
        return g_to, y_to, {"gy": g_to, "slab": y_to * N_R + rr}

    def column(k):
        d_lo, dz = COLUMN[k]
        x_to, z_to = lax.rem(x_lo + d_lo, 2), lax.rem(z + dz, 8)
        w_to = lax.rem(lax.rem(z_to, 4) + 4 - yy, 4) * 4 + x_to * 2 + lax.div(z_to, 4)
        return w_to, {"slab": yy * N_R + x_to * 8 + z_to}

    def across(slab_of):
        found = []
        for d_hi in range(2):
            to_hi = lax.rem(x_hi + d_hi, 2)
            for k in range(4):
                to = slab_of(k)
                found.append((to_hi, k, to, (to != slab) if d_hi == 0 else None))
        return found

    owners = across(lambda k: k * N_R + near + lax.rem(yy + k, 4))
    blocks = across(lambda k: from_y * N_R + near + k)
    at_home = home.astype(jnp.int32)

    def guarded(away, action):
        if away is None:
            action()
        else:
            pl.when(away)(action)

    def device_of(to_hi, to):
        return {"gy": to_hi * 2 + core, "slab": to}

    barrier = pltpu.get_barrier_semaphore()

    def greet(device):
        pl.semaphore_signal(barrier, inc=1, device_id=device, device_id_type=MESH)

    for k in range(15):
        greet(plane(k)[2])
        greet(column(k)[1])
    for to_hi, _, to, away in owners + blocks:
        guarded(away, functools.partial(greet, device_of(to_hi, to)))

    def copy_to(source, target, send_sem, recv_sem, device):
        return pltpu.make_async_remote_copy(
            src_ref=source,
            dst_ref=target,
            send_sem=send_sem,
            recv_sem=recv_sem,
            device_id=device,
            device_id_type=MESH,
        )

    started = []

    def start_all(sem, copies):
        made = [copy_to(a, b, sem.at[0, k], sem.at[1, k], device) for k, (a, b, device) in enumerate(copies)]
        for copy in made:
            copy.start()
        started.extend((None, copy) for copy in made)
        return made

    def finish(made):
        for copy in made:
            copy.wait_recv()

    plane_to = [plane(k) for k in range(15)]
    column_to = [column(k) for k in range(15)]
    slot = {d: k for k, d in enumerate(PLANE)}

    def window(w):
        return pl.ds(pl.multiple_of(w * 8, 8), 8)

    def send_home(index, source, target):
        sem = ref.home_sem.at[index]
        for k, (to_hi, _, to, away) in enumerate(blocks):
            copy = copy_to(source, target.at[mine], sem.at[0, k], sem.at[1, mine], device_of(to_hi, to))
            guarded(away, copy.start)
            started.append((away, copy))

        @pl.when(home)
        def _():
            target[mine] = source[...]

    def come_home(index, source, target):
        sem = ref.home_sem.at[index]
        for k, (from_hi, y, origin, away) in enumerate(owners):
            place = 4 * from_hi + y
            copy = copy_to(source, target.at[place], sem.at[0, k], sem.at[1, place], device_of(from_hi, origin))
            guarded(away, copy.wait_recv)

    def in_block_order(messages):
        rows = []
        for n in range(4):
            rows.append(jnp.concatenate([m[:, OWN * n : OWN * n + OWN] for m in messages], axis=1))
        return dot(jnp.concatenate(rows, axis=0), ref.v_gather[...], NN, HIGHEST)

    def depth_stage(cells_of, x):
        for pair in range(2):
            pieces = [cells_of(x, slice((2 * pair + h) * Q, (2 * pair + h + 1) * Q)).reshape(Q * TZ, Y) for h in range(2)]
            zz = dot(ref.v_depth[...], jnp.concatenate(pieces, axis=1), NN)
            for h in range(2):
                part = zz[:, h * Y : (h + 1) * Y]
                ref.z_all[2 * pair + h, x, :, 0:Y] = part[:LANES]
                ref.z_all[2 * pair + h, x, :, Y:] = part[LANES:]

    def to_window(index, beside_first, beside_second):
        table = ref.v_y_table[...]
        gsend, grecv = ref.gsend.at[index], ref.grecv.at[index]
        for g in range(N_GY):
            for y in range(N_Y):
                lanes = slice(24 * (4 * (g // 2) + y), 24 * (4 * (g // 2) + y) + 24)
                rows = [ref.z_all[q, x, lanes, :] for x in range(CX) for q in (g % 2, g % 2 + 2)]
                piece = dot(table, jnp.concatenate(rows, axis=0).astype(BF16), NT_DIMS)
                gsend[g, y] = pack(piece, [])
        if index == 0:
            pl.semaphore_wait(barrier, 30 + 16 - 2 * at_home)
        sem = ref.plane_sem.at[index, 0]
        first = start_all(sem, [(gsend.at[g, y], grecv.at[k], to) for k, (g, y, to) in enumerate(plane_to)])
        beside_first()
        finish(first)
        for dy in range(N_Y):
            total = gsend[gy, yy] if dy == 0 else None
            for d_hi in range(2):
                for d_core in range(2):
                    if (d_hi, d_core, dy) in slot:
                        term = grecv[slot[d_hi, d_core, dy]]
                        total = term if total is None else total + term
            base = lax.rem(yy + N_Y - dy, N_Y) * ROWS
            for x, piece in enumerate(unpack(total)):
                ref.g12[pl.ds(pl.multiple_of(base + 24 * x, 8), 24), 0:48] = piece

        f = product(ref.v_rows, 0, ref.g12[:, 0:48])
        msend, mrecv = ref.msend.at[index], ref.mrecv.at[index]
        msend[...] = jnp.concatenate([f[0:128], f[128:256], jnp.zeros((128, 32), F32)], axis=1)
        ninth = jnp.concatenate([f[256:272], f[272:288]], axis=1)
        for j in range(4):
            old = msend[pl.ds(j, N_R, stride=8), :]
            msend[pl.ds(j, N_R, stride=8), :] = jnp.concatenate(
                [old[:, 0:96], ninth[:, 24 * j : 24 * j + 24], old[:, 120:128]], axis=1
            )
        sem = ref.column_sem.at[index, 0]
        second = start_all(sem, [(msend.at[window(w)], mrecv.at[k], to) for k, (w, to) in enumerate(column_to)])
        beside_second()
        finish(second)
        m = msend[window(own_window), :]
        for k in range(15):
            m = m + mrecv[k]

        last = jnp.concatenate([m[j : j + 1, 96:120] for j in range(4)], axis=1)
        nine = jnp.concatenate([m[:, 0:96], last, jnp.zeros((7, 96), F32)], axis=0)
        expand = ref.v_expand[...].astype(BF16)
        high, low = halves_of(nine)
        spread = dot(jnp.concatenate([high, low], axis=0), jnp.concatenate([expand, expand], axis=0), TN)
        spread = spread * ref.v_keep[...]
        parts = {}
        for n in range(4):
            base = 24 * n
            total = spread[base : base + 8] + spread[base + 8 : base + 16] + spread[base + 16 : base + 24]
            parts[n // 2, n % 2] = total[:, 0:OWN]
        return parts

    def packed(parts):
        end = jnp.zeros((Q, 128 - 4 * OWN), F32)
        return jnp.concatenate([parts[part, h] for h in range(2) for part in range(2)] + [end], axis=1)

    def from_mixed(index, mixed, local, beside_first, beside_second):
        pad = jnp.zeros((Q, 128 - OWN), F32)
        wide = [jnp.concatenate([mixed[part, h], pad], axis=1) for part in range(2) for h in range(2)]
        tiled = jnp.concatenate([v for v in wide for _ in range(3)], axis=0) * ref.v_keep[...]
        expand = ref.v_expand[...].astype(BF16)
        u = dot(jnp.concatenate([expand, expand], axis=1), jnp.concatenate(halves_of(tiled), axis=1), NT_DIMS)
        last = jnp.concatenate([u[8:9, 24 * j : 24 * j + 24] for j in range(4)] + [jnp.zeros((4, 24), F32)], axis=0)
        rsend, rall = ref.rsend.at[index], ref.rall.at[index]
        rsend[...] = jnp.concatenate([u[0:8], last, local], axis=1)
        rall[window(own_window), :] = rsend[...]
        sem = ref.column_sem.at[index, 1]
        third = start_all(sem, [(rsend, rall.at[window(own_window)], to) for _, to in column_to])
        beside_first()
        finish(third)
        ninth = jnp.concatenate([rall[pl.ds(j, N_R, stride=8), :][:, 96:120] for j in range(4)], axis=1)
        f = jnp.concatenate([rall[:, 0:48], rall[:, 48:96], ninth[:, 0:48], ninth[:, 48:96]], axis=0)
        h = product(ref.v_rows, 2, f)
        local = rall[0:8, 120:128]
        for w in range(1, N_R):
            local = local + rall[8 * w : 8 * w + 8, 120:128]
        hsend, hall = ref.hsend.at[index], ref.hall.at[index]
        for y in range(N_Y):
            rows = [h[y * ROWS + 24 * x : y * ROWS + 24 * x + 24] for x in range(CX)]
            hsend[y] = pack(jnp.concatenate(rows, axis=1), [local])
        hall[yy, gy] = hsend[yy]
        sem = ref.plane_sem.at[index, 1]
        fourth = start_all(sem, [(hsend.at[y], hall.at[yy, gy], to) for _, y, to in plane_to])
        beside_second()
        finish(fourth)
        for y in range(N_Y):
            for g in range(N_GY):
                base = 24 * (4 * (g // 2) + y)
                for x, piece in enumerate(unpack(hall[y, g])):
                    for h in range(2):
                        ref.hx[x, 2 * h + g % 2, :, base : base + 24] = piece[:, 24 * h : 24 * h + 24]

    ready("depth", "y_table")
    for x in range(CX):
        fields[x].wait()
        depth_stage(lambda x, c: ref.v_field[x, c], x)

    def send_weights():
        ready("weight", "select", "place")
        flat = ref.v_weight[...].astype(F32).reshape(2 * C * Q, BLOCK).astype(BF16)
        picked = dot(ref.v_select[...][:, 0:BLOCK].astype(BF16), flat, NT_DIMS)
        for k in range(8):
            ref.wsend[k] = picked[8 * k : 8 * k + 8]
        for e in range(2):
            row = picked[64 + e : 65 + e]
            lanes = [row[:, 128 * j : 128 * j + 128] for j in range(4)]
            ref.esend[e] = jnp.concatenate([*lanes, jnp.zeros((4, 128), F32)], axis=0)
        own = 2 * turn + x_hi
        for k, (to_hi, y, to, away) in enumerate(owners):
            source = ref.wsend.at[4 * to_hi + y]
            copy = copy_to(source, ref.wrecv.at[own], ref.w_sem.at[0, k], ref.w_sem.at[1, own], device_of(to_hi, to))
            guarded(away, copy.start)
            started.append((away, copy))
        for e in range(2):
            to_hi, y = lax.div(turn, 2), lax.rem(2 * turn, 4) + e
            to = y * N_R + near + lax.rem(yy + y, 4)
            copy = copy_to(
                ref.esend.at[e], ref.erecv.at[x_hi], ref.e_sem.at[0, e], ref.e_sem.at[1, x_hi], device_of(to_hi, to)
            )
            here = jnp.logical_and(to_hi == x_hi, to == slab)
            away = jnp.logical_not(here)
            pl.when(away)(copy.start)
            started.append((away, copy))

            @pl.when(here)
            def _():
                ref.erecv[x_hi] = ref.esend[e]

        @pl.when(home)
        def _():
            ref.wrecv[own] = ref.wsend[mine]

        ready("rows", "expand", "keep")

    def receive_weights():
        for k, (from_hi, t, origin, away) in enumerate(blocks):
            at = 2 * t + from_hi
            copy = copy_to(
                ref.wsend.at[0], ref.wrecv.at[at], ref.w_sem.at[0, k], ref.w_sem.at[1, at], device_of(from_hi, origin)
            )
            guarded(away, copy.wait_recv)
        origin = from_y * N_R + near + lax.div(mine, 2)
        for hi in range(2):
            copy = copy_to(
                ref.esend.at[0], ref.erecv.at[hi], ref.e_sem.at[0, hi], ref.e_sem.at[1, hi], device_of(hi, origin)
            )
            pl.when(jnp.logical_or(x_hi != hi, origin != slab))(copy.wait_recv)
        ninths = [jnp.concatenate([ref.erecv[hi, j : j + 1, :] for j in range(4)], axis=1) for hi in range(2)]
        received = jnp.concatenate([ref.wrecv[...].reshape(64, 512), *ninths, jnp.zeros((6, 512), F32)], axis=0)
        ref.owned[...] = dot(received.astype(BF16), ref.v_place[...].astype(BF16), TN)

    def local_products():
        kron = channel_matrix(ref.v_lw[...], ref.v_repeat[...], True)
        for n in range(CX * CHUNKS):
            ref.local_part[n] = dot(kron, ref.cells[n], NN)

    def prepare_cells():
        ready("lw", "repeat", "depth_back", "y_back", "gather")
        for copy in cots:
            copy.wait()
        for x in range(CX):
            for r in range(CHUNKS):
                n = x * CHUNKS + r
                ref.cells[n] = chunk_of(ref.v_field[x, :, 16 * r : 16 * r + 16, :]).astype(BF16)
                ref.cot_cells[n] = chunk_of(ref.v_cot[x, :, 16 * r : 16 * r + 16, :])

    def beside_column():
        receive_weights()
        prepare_cells()

    parts = to_window(0, send_weights, beside_column)

    other_core = {"gy": x_hi * 2 + 1 - core}
    ref.qbuf[core] = packed(parts)
    copy = copy_to(ref.qbuf.at[core], ref.qbuf.at[core], ref.core_sem.at[0, 0], ref.core_sem.at[0, 1], other_core)
    copy.start()
    copy.wait_recv()
    started.append((None, copy))
    mixed_r = jnp.zeros((Q, BLOCK), F32)
    mixed_i = jnp.zeros((Q, BLOCK), F32)

    def weights(i):
        return ref.owned[8 * i : 8 * i + 8, 0:BLOCK], ref.owned[256 + 8 * i : 264 + 8 * i, 0:BLOCK]

    for q in range(N_GY):
        both = ref.qbuf[q % 2]
        base = 2 * OWN * (q // 2)
        real, imag = both[:, base : base + OWN], both[:, base + OWN : base + 2 * OWN]
        real, imag = jnp.concatenate([real, real], axis=1), jnp.concatenate([imag, imag], axis=1)
        for c in range(Q):
            mr, mi = real[c : c + 1], imag[c : c + 1]
            w0, w1 = weights(q * Q + c)
            mixed_r = mixed_r + (mr * w0 - mi * w1)
            mixed_i = mixed_i + (mr * w1 + mi * w0)
    mixed = {(p, h): v[:, OWN * h : OWN * h + OWN] for p, v in enumerate((mixed_r, mixed_i)) for h in range(2)}

    def beside_modes():
        send_home(0, ref.qbuf, ref.home_modes)
        local_products()

    def modes_home():
        come_home(0, ref.qbuf, ref.home_modes)
        ref.block_modes[...] = in_block_order([ref.home_modes[k].reshape(16, 128) for k in range(8)])

    from_mixed(0, mixed, jnp.zeros((8, 8), F32), beside_modes, modes_home)

    stores = []

    def store(source, target):
        copy = pltpu.make_async_copy(source, target, ref.store_sem.at[len(stores)])
        copy.start()
        stores.append(copy)

    for x in range(CX):
        spectral_rows(ref.hx, ref.v_y_back, ref.v_depth_back, ref.spec, x)
        for r in range(CHUNKS):
            n = x * CHUNKS + r
            rows = slice(16 * r, 16 * r + 16)
            pre = chunk_of(ref.spec[:, rows, :]) + ref.local_part[n]
            cdf = 0.5 * (1.0 + lax.erf(pre * ROOT_HALF))
            slope = cdf + pre * jnp.exp(-0.5 * pre * pre) * INV_ROOT_TWO_PI
            grad = ref.cot_cells[n] * slope
            ref.v_out[x, :, rows, :] = unchunk(pre * cdf).astype(BF16)
            ref.grad_pre[x, :, rows, :] = unchunk(grad).astype(BF16)
        store(ref.v_out.at[x], ref.out.at[:, x])
        store(ref.grad_pre.at[x], ref.grad_cells.at[:, x])
        depth_stage(lambda x, c: ref.grad_pre[x, c], x)
    def local_terms():
        total = jnp.zeros((256, 256), F32)
        for n in range(CX * CHUNKS):
            x, r = divmod(n, CHUNKS)
            grad = chunk_of(ref.grad_pre[x, :, 16 * r : 16 * r + 16, :]).astype(BF16)
            total = total + dot(ref.cells[n], grad, NT_DIMS)
        kept = jnp.where(same_row((256, 256)), total, 0.0)
        repeat = ref.v_repeat[...].astype(F32)
        local = dot(dot(repeat, kept, TN, HIGHEST), repeat, NN, HIGHEST)
        for g in range(N_GY):
            for y in range(N_Y):
                ref.lsend[g, y, :, 0:8] = local[8 * g : 8 * g + 8, 8 * y : 8 * y + 8]
        copies = [(ref.lsend.at[g, y], ref.lrecv.at[k], to) for k, (g, y, to) in enumerate(plane_to)]
        local_copies.extend(start_all(ref.local_sem, copies))

    local_copies = []
    parts = to_window(1, local_terms, lambda: None)
    ref.grads[...] = packed(parts)
    gr, gi = (jnp.concatenate([parts[p, 0], parts[p, 1]], axis=1) for p in range(2))
    for i in range(C):
        q, c = divmod(i, Q)
        w0, w1 = weights(i)
        ref.sums[q, c : c + 1, 0:BLOCK] = jnp.sum(gr * w0 + gi * w1, axis=0, keepdims=True)
        ref.sums[q, 8 + c : 9 + c, 0:BLOCK] = jnp.sum(gi * w0 - gr * w1, axis=0, keepdims=True)
    for k in range(2):
        found = {}
        for h in range(2):
            both = ref.sums[2 * h + k]
            both = both[:, 0:OWN] + both[:, OWN:BLOCK]
            found[0, h], found[1, h] = both[0:8], both[8:16]
        ref.qsend[k] = packed(found)
    copy = copy_to(ref.qsend.at[1 - core], ref.qrecv, ref.core_sem.at[1, 0], ref.core_sem.at[1, 1], other_core)
    copy.start()
    copy.wait_recv()
    started.append((None, copy))
    both = ref.qsend[core] + ref.qrecv[...]
    mixed = {(p, h): both[:, OWN * (2 * h + p) : OWN * (2 * h + p) + OWN] for p in range(2) for h in range(2)}

    def weight_gradient():
        come_home(1, ref.grads, ref.home_grads)
        grads = in_block_order([ref.home_grads[k] for k in range(8)])
        grads = jnp.where(x_hi == 0, grads[0:16], grads[16:32])
        gr, gi = grads[0:8, 0:BLOCK], grads[8:16, 0:BLOCK]
        for i in range(C):
            q, c = divmod(i, Q)
            row = 32 * (q // 2) + 8 * (q % 2) + c
            mr, mi = ref.block_modes[row : row + 1, 0:BLOCK], ref.block_modes[row + 16 : row + 17, 0:BLOCK]
            ref.v_grad_spectral[0, i] = mr * gr + mi * gi
            ref.v_grad_spectral[1, i] = mr * gi - mi * gr
        store(ref.v_grad_spectral, ref.grad_spectral)

    finish(local_copies)
    local = ref.lsend[gy, yy, :, 0:8]
    for k in range(15):
        local = local + ref.lrecv[k, :, 0:8]
    from_mixed(1, mixed, local, lambda: send_home(1, ref.grads, ref.home_grads), weight_gradient)
    for y in range(N_Y):
        for g in range(N_GY):
            corner = ref.hall[1, y, g, 24:32, 48:56]
            ref.grad_local[8 * g : 8 * g + 8, 8 * y : 8 * y + 8] = corner * FORWARD_SCALE
    for copy in stores:
        copy.wait()
    for away, copy in started:
        guarded(away, copy.wait_send)


def last_kernel(
    grad_cells, hx, early_out, early_spectral, early_local, lw, repeat, y_back, depth_back,
    out, grad_in, grad_spectral, grad_local,
    v_hx, v_cells, v_lw, v_repeat, v_y_back, v_depth_back, v_out, spec, v_pass, v_spectral, v_local, sem, pass_sem, store_sem,
):
    gy = lax.axis_index("gy")
    staged = [
        (hx, v_hx),
        (y_back.at[gy], v_y_back),
        (depth_back, v_depth_back),
        (lw, v_lw),
        (repeat, v_repeat),
        *[(grad_cells.at[:, x], v_cells.at[x]) for x in range(CX)],
    ]
    loads = [pltpu.make_async_copy(a, b, sem.at[k]) for k, (a, b) in enumerate(staged)]
    passed = [(early_out, v_pass, out), (early_spectral, v_spectral, grad_spectral), (early_local, v_local, grad_local)]
    arrive = [pltpu.make_async_copy(a, b, pass_sem.at[0, k]) for k, (a, b, _) in enumerate(passed)]
    leave = [pltpu.make_async_copy(b, c, pass_sem.at[1, k]) for k, (_, b, c) in enumerate(passed)]
    for copy in loads + arrive:
        copy.start()
    for copy in loads[:5]:
        copy.wait()
    kron = channel_matrix(v_lw[...], v_repeat[...], False)
    stores = []
    for x in range(CX):
        spectral_rows(v_hx, v_y_back, v_depth_back, spec, x)
        if x == 0:
            for first, second in zip(arrive, leave):
                first.wait()
                second.start()
        loads[5 + x].wait()
        for r in range(CHUNKS):
            rows = slice(16 * r, 16 * r + 16)
            cells = chunk_of(v_cells[x, :, rows, :]).astype(BF16)
            total = chunk_of(spec[:, rows, :]) + dot(kron, cells, NN)
            v_out[x, :, rows, :] = unchunk(total).astype(BF16)
        copy = pltpu.make_async_copy(v_out.at[x], grad_in.at[:, x], store_sem.at[x])
        copy.start()
        stores.append(copy)
    for copy in leave + stores:
        copy.wait()


def per_device(field_in, cotangent, spectral_weight, local_weight):
    cells = (C, CX, TZ, Y)
    depth = depth_table()
    tables = y_tables()
    high = tables.astype(BF16)
    low = (tables - high.astype(np.float64)).astype(BF16)
    expand, keep = unit_tables()
    select, place, gather = owner_tables()
    values = {
        "field": field_in.reshape(cells),
        "cot": cotangent.reshape(cells),
        "weight": jnp.transpose(spectral_weight, (0, 2, 3, 1)),
        "lw": local_weight,
        "depth": depth.astype(BF16),
        "depth_back": np.ascontiguousarray(depth.T).astype(BF16),
        "y_table": high,
        "y_back": np.concatenate([high, low, high], axis=1),
        "rows": row_tables(),
        "expand": expand,
        "keep": keep,
        "select": select.astype(np.float32),
        "place": place.astype(np.float32),
        "gather": gather.astype(np.float32),
        "repeat": np.repeat(np.eye(C), 8, axis=0).astype(BF16),
    }
    values = {name: jnp.asarray(value) for name, value in values.items()}
    vmem, anywhere = pl.BlockSpec(memory_space=pltpu.VMEM), pl.BlockSpec(memory_space=pl.ANY)
    field, mixed, local = ((cells, BF16), ((2, C, Q, BLOCK), F32), ((C, C), F32))
    outs = [field, field, mixed, ((CX, N_GY, 24, 256), F32), local]
    early_out, grad_cells, early_spectral, hx, early_local = pl.pallas_call(
        layer_kernel,
        out_shape=[jax.ShapeDtypeStruct(shape, dtype) for shape, dtype in outs],
        in_specs=[anywhere for _ in INPUTS],
        out_specs=[anywhere] * 3 + [vmem] * 2,
        scratch_shapes=[pltpu.VMEM(shape, dtype) for shape, dtype in SCRATCH.values()]
        + [DMA(shape) for shape in SEMAPHORES.values()],
        compiler_params=pltpu.CompilerParams(
            collective_id=0, has_side_effects=True, vmem_limit_bytes=56 * 1024 * 1024
        ),
        name="spectral_layer",
    )(*[values[name] for name in INPUTS])
    output, grad_input, grad_spectral, grad_local = pl.pallas_call(
        last_kernel,
        out_shape=[jax.ShapeDtypeStruct(shape, dtype) for shape, dtype in (field, field, mixed, local)],
        in_specs=[anywhere] * 9,
        out_specs=[anywhere] * 4,
        scratch_shapes=[
            pltpu.VMEM((CX, N_GY, 24, 256), F32),
            pltpu.VMEM((CX, C, TZ, Y), BF16),
            pltpu.VMEM((C, C), BF16),
            pltpu.VMEM((256, C), BF16),
            pltpu.VMEM((6 * KY, 2 * Y), BF16),
            pltpu.VMEM((Q * TZ, 2 * K * Q), BF16),
            pltpu.VMEM((CX, C, TZ, Y), BF16),
            pltpu.VMEM((C, TZ, Y), F32),
            *[pltpu.VMEM(shape, dtype) for shape, dtype in (field, mixed, local)],
            DMA((8,)),
            DMA((2, 3)),
            DMA((CX,)),
        ],
        compiler_params=pltpu.CompilerParams(vmem_limit_bytes=56 * 1024 * 1024),
        name="last_cells",
    )(grad_cells, hx, early_out, early_spectral, early_local, *[values[n] for n in ("lw", "repeat", "y_back", "depth_back")])
    return (
        output.reshape(field_in.shape),
        grad_input.reshape(field_in.shape),
        jnp.transpose(grad_spectral, (0, 3, 1, 2)),
        grad_local,
    )


def solution(mesh):
    placed = (
        P(None, "slab", None, None, "gy"),
        P(None, "slab", None, None, "gy"),
        P(None, "slab", None, "gy"),
        P(),
    )
    return jax.shard_map(
        per_device,
        mesh=mesh,
        in_specs=placed,
        out_specs=(
            P(None, "slab", None, None, "gy"),
            P(None, "slab", None, None, "gy"),
            P(None, "slab", None, "gy"),
            P(),
        ),
        check_vma=False,
    )
```

```python
import functools
import math
import types

import jax
import jax.numpy as jnp
import numpy as np
from jax import lax
from jax.experimental import pallas as pl
from jax.experimental.pallas import tpu as pltpu
from jax.sharding import PartitionSpec as P

C = 32
KX = 12
KY = 12
KZ = 12
NT = 2
NZ = 32
NX = 192
NY = 512
CX = 3
N_GY = 4
N_Y = 4
N_R = 16
Q = C // N_GY
K = NT * KZ
TZ = NT * NZ
Y = NY // N_GY
BLOCK = 54
OWN = 27
UNITS = 9
ROWS = 72
LANES = K * Q

FORWARD_SCALE = 1.0 / math.sqrt(NX * NY * NZ * NT)
INVERSE_SCALE = 1.0 / math.sqrt(KX * KY * KZ * NT)
ROOT_HALF = 0.7071067811865476
INV_ROOT_TWO_PI = 0.3989422804014327
HIGHEST = lax.Precision.HIGHEST
PLANE = [(h, c, y) for h in range(2) for c in range(2) for y in range(N_Y) if (h, c, y) != (0, 0, 0)]
PLANE.sort(key=lambda d: -(3 * d[0] + min(d[2], N_Y - d[2])))
COLUMN = [(x, z) for x in range(2) for z in range(8) if (x, z) != (0, 0)]
COLUMN.sort(key=lambda d: -(0.5 * d[0] + min(d[1], 8 - d[1])))
F32 = jnp.float32
BF16 = jnp.bfloat16
MESH = pl.DeviceIdType.MESH


def frequencies(kept):
    values = np.arange(kept)
    return np.where(values < kept // 2, values, values - kept)


def depth_table():
    t, z = np.divmod(np.arange(TZ), NZ)
    kt, kz = np.divmod(np.arange(K), KZ)
    product = (t[None] * kt[:, None] * NZ + z[None] * frequencies(KZ)[kz][:, None] * NT) % TZ
    angle = product * (2.0 * np.pi / TZ)
    parts = np.stack([np.cos(angle), -np.sin(angle)])
    full = np.einsum("pks,cd->pkcds", parts, np.eye(Q))
    return full.reshape(2 * K * Q, Q * TZ)


def y_tables():
    product = (frequencies(KY)[:, None] * np.arange(NY)[None]) % NY
    angle = product * (2.0 * np.pi / NY)
    cos, sin = np.cos(angle), np.sin(angle)
    full = np.stack([np.stack([cos, sin]), np.stack([-sin, cos])])
    full = full.reshape(2, 2, KY, N_GY, Y).transpose(3, 0, 2, 1, 4)
    return full.reshape(N_GY, 2 * KY, 2 * Y)


def unit_tables():
    lane = np.arange(128)
    row = np.arange(96)
    expand = (lane[None] // 3 == np.arange(16)[:, None]) & (lane[None] < OWN)
    keep = ((row[:, None] // 8) % 3 == lane[None] % 3) & (lane[None] < OWN)
    return expand.astype(np.float32), keep.astype(np.float32)


def row_tables():
    main = [9 * w + j for w in range(N_R) for j in range(8)]
    ninth = [9 * w + 8 for w in range(N_R)]
    pairs = np.array(main + main + ninth + ninth)
    part = np.array([0] * 128 + [1] * 128 + [0] * 16 + [1] * 16)
    y, x, part_in, ky = np.unravel_index(np.arange(288), (N_Y, CX, 2, KY))
    row = 48 * y[None] + 3 * np.arange(N_R)[:, None] + x[None]
    freq = frequencies(KX)[pairs // KY]
    angle = (freq[None, :, None] * row[:, None, :]) % NX * (2.0 * np.pi / NX)
    sign = np.where(part == 0, 1.0, -1.0)[:, None]
    value = np.where(part[:, None] == part_in[None], np.cos(angle), sign * np.sin(angle))
    value = np.where((pairs % KY)[:, None] == ky[None], value, 0.0)
    forward, inverse = value * FORWARD_SCALE, value.transpose(0, 2, 1) * INVERSE_SCALE
    parts = []
    for full in (forward, inverse):
        high = full.astype(BF16)
        parts += [high, (full - high.astype(np.float64)).astype(BF16)]
    return np.stack(parts, axis=1)


def owner_tables():
    select = np.zeros((4, 72, 128))
    place = np.zeros((8, 72, 128))
    gather = np.zeros((4, 8, OWN, 128))
    for t in range(4):
        count = [0] * 8
        for mode in range(BLOCK):
            unit = 18 * t + mode // 3
            part, other = unit % 8, 3 * (unit // 8) + mode % 3
            n = count[part]
            count[part] += 1
            select[t, 8 * part + n if n < 8 else 64 + part - 2 * t, mode] = 1.0
            for x in range(2):
                place[part, 16 * t + 8 * x + n if n < 8 else 64 + x, OWN * x + other] = 1.0
            gather[t, part, other, mode] = 1.0
    return select, place, gather.reshape(4, 8 * OWN, 128)


def dot(a, b, dims, precision=None):
    return lax.dot_general(a, b, (dims, ((), ())), precision=precision, preferred_element_type=F32)


NN = ((1,), (0,))
NT_DIMS = ((1,), (1,))
TN = ((0,), (0,))


def pack(g, corner):
    tail = g[:, 128:144]
    width = 80 - 8 * len(corner)
    below = jnp.concatenate([tail[0:8], tail[8:16], tail[16:24], *corner, jnp.zeros((8, width), F32)], axis=1)
    return jnp.concatenate([g[:, 0:128], below], axis=0)


def unpack(message):
    below = message[24:32]
    tail = jnp.concatenate([below[:, 0:16], below[:, 16:32], below[:, 32:48]], axis=0)
    body = message[0:24]
    return [body[:, 0:48], body[:, 48:96], jnp.concatenate([body[:, 96:128], tail], axis=1)]


def halves_of(values):
    high = values.astype(BF16)
    return high, (values - high.astype(F32)).astype(BF16)


def product(rows_ref, first, values):
    high, low = halves_of(values)
    both = dot(rows_ref[first], jnp.concatenate([high, low], axis=1), NN)
    width = values.shape[1]
    return both[:, :width] + both[:, width:] + dot(rows_ref[first + 1], high, NN)


def chunk_of(values):
    values = values.astype(F32)
    return jnp.concatenate([values[:, 0:8].reshape(256, Y), values[:, 8:16].reshape(256, Y)], axis=1)


def unchunk(values):
    halves = [values[:, :Y].reshape(C, 8, Y), values[:, Y:].reshape(C, 8, Y)]
    return jnp.concatenate(halves, axis=1)


def same_row(shape):
    row = lax.broadcasted_iota(jnp.int32, shape, 0)
    col = lax.broadcasted_iota(jnp.int32, shape, 1)
    return row % 8 == col % 8


def channel_matrix(weight, repeat, transposed):
    half = dot(repeat, weight, NT_DIMS if transposed else NN).astype(BF16)
    full = dot(half, repeat, NT_DIMS)
    return jnp.where(same_row(full.shape), full, 0.0).astype(BF16)


CHUNKS = TZ // 16
BIG = (32, 128)
TILE = (8, 128)
DMA = pltpu.SemaphoreType.DMA

INPUTS = ["field", "cot", "weight", "lw", "depth", "depth_back", "y_table", "y_back", "rows", "expand", "keep"]
INPUTS += ["select", "place", "gather", "repeat"]
OUTPUTS = ["out", "grad_cells", "grad_spectral", "hx", "grad_local"]
SCRATCH = {
    "v_field": ((CX, C, TZ, Y), BF16),
    "v_cot": ((CX, C, TZ, Y), BF16),
    "v_weight": ((2, C, Q, BLOCK), BF16),
    "v_lw": ((C, C), BF16),
    "v_depth": ((2 * K * Q, Q * TZ), BF16),
    "v_depth_back": ((Q * TZ, 2 * K * Q), BF16),
    "v_y_table": ((2 * KY, 2 * Y), BF16),
    "v_y_back": ((6 * KY, 2 * Y), BF16),
    "v_rows": ((4, 288, 288), BF16),
    "v_expand": ((16, 128), F32),
    "v_keep": ((96, 128), F32),
    "v_select": ((72, 128), F32),
    "v_place": ((72, 128), F32),
    "v_gather": ((8 * OWN, 128), F32),
    "v_repeat": ((256, C), BF16),
    "grad_pre": ((CX, C, TZ, Y), BF16),
    "spec": ((CX, C, TZ, Y), F32),
    "cells": ((CX * CHUNKS, 256, 256), BF16),
    "cot_cells": ((CX * CHUNKS, 256, 256), F32),
    "local_part": ((CX * CHUNKS, 256, 256), F32),
    "lsend": ((N_GY, N_Y, *TILE), F32),
    "lrecv": ((15, *TILE), F32),
    "z_all": ((N_GY, CX, LANES, 256), F32),
    "gsend": ((2, N_GY, N_Y, *BIG), F32),
    "grecv": ((2, 15, *BIG), F32),
    "g12": ((288, 128), F32),
    "msend": ((2, 128, 128), F32),
    "mrecv": ((2, 15, *TILE), F32),
    "qbuf": ((2, *TILE), F32),
    "qsend": ((2, *TILE), F32),
    "qrecv": (TILE, F32),
    "sums": ((N_GY, 16, 128), F32),
    "grads": (TILE, F32),
    "rsend": ((2, *TILE), F32),
    "rall": ((2, 128, 128), F32),
    "hsend": ((2, N_Y, *BIG), F32),
    "hall": ((2, N_Y, N_GY, *BIG), F32),
    "v_out": ((CX, C, TZ, Y), BF16),
    "v_grad_spectral": ((2, C, Q, BLOCK), F32),
    "wsend": ((8, 8, 512), F32),
    "wrecv": ((8, 8, 512), F32),
    "esend": ((2, *TILE), F32),
    "erecv": ((2, *TILE), F32),
    "owned": ((2 * C * Q, 128), F32),
    "home_modes": ((8, 2, *TILE), F32),
    "home_grads": ((8, *TILE), F32),
    "block_modes": ((64, 128), F32),
}
SEMAPHORES = {
    "load_sem": (13,),
    "cell_sem": (2, CX),
    "store_sem": (2 * CX + 1,),
    "plane_sem": (2, 2, 2, 15),
    "column_sem": (2, 2, 2, 15),
    "core_sem": (2, 2),
    "local_sem": (2, 15),
    "w_sem": (2, 8),
    "e_sem": (2, 2),
    "home_sem": (2, 2, 8),
}


def spectral_rows(hx, y_back, depth_back, spec, x):
    for pair in range(2):
        halves = []
        for q in (2 * pair, 2 * pair + 1):
            h = hx[x, q, :, 0:LANES]
            high = h.astype(BF16).astype(F32)
            stacked = jnp.concatenate([high, high, h - high], axis=0).astype(BF16)
            u = dot(stacked, y_back[...], TN)
            halves.append(jnp.concatenate([u[:, :Y], u[:, Y:]], axis=0).astype(BF16))
        s = dot(depth_back[...], jnp.concatenate(halves, axis=1), NN)
        for h in range(2):
            q = 2 * pair + h
            spec[q * Q : (q + 1) * Q] = s[:, h * Y : (h + 1) * Y].reshape(Q, TZ, Y)


def layer_kernel(*refs):
    ref = types.SimpleNamespace(**dict(zip(INPUTS + OUTPUTS + list(SCRATCH) + list(SEMAPHORES), refs)))

    slab, gy = lax.axis_index("slab"), lax.axis_index("gy")
    yy, rr = lax.div(slab, N_R), lax.rem(slab, N_R)
    x_hi, core = lax.div(gy, 2), lax.rem(gy, 2)
    x_lo, z = lax.div(rr, 8), lax.rem(rr, 8)
    turn, half = lax.rem(z, 4), lax.div(z, 4)
    mine = 4 * x_hi + yy
    near = x_lo * 8 + half * 4
    from_y = lax.rem(turn + 4 - yy, 4)
    own_window = from_y * 4 + x_lo * 2 + half
    home = turn == lax.rem(2 * yy, 4)

    sources = {
        "depth": ref.depth,
        "y_table": ref.y_table.at[gy],
        "weight": ref.weight,
        "select": ref.select.at[turn],
        "place": ref.place.at[mine],
        "rows": ref.rows.at[rr],
        "expand": ref.expand,
        "keep": ref.keep,
        "gather": ref.gather.at[turn],
        "lw": ref.lw,
        "repeat": ref.repeat,
        "depth_back": ref.depth_back,
        "y_back": ref.y_back.at[gy],
    }
    loads = {
        name: pltpu.make_async_copy(source, getattr(ref, "v_" + name), ref.load_sem.at[k])
        for k, (name, source) in enumerate(sources.items())
    }
    fields = [pltpu.make_async_copy(ref.field.at[:, x], ref.v_field.at[x], ref.cell_sem.at[0, x]) for x in range(CX)]
    cots = [pltpu.make_async_copy(ref.cot.at[:, x], ref.v_cot.at[x], ref.cell_sem.at[1, x]) for x in range(CX)]
    fields[0].start()
    loads["depth"].start()
    loads["y_table"].start()
    fields[1].start()
    fields[2].start()
    for name in list(loads)[2:]:
        loads[name].start()
    for copy in cots:
        copy.start()

    def ready(*names):
        for name in names:
            loads[name].wait()

    def plane(k):
        d_hi, d_core, dy = PLANE[k]
        g_to = lax.rem(x_hi + d_hi, 2) * 2 + lax.rem(core + d_core, 2)
        y_to = lax.rem(yy + dy, N_Y)
        return g_to, y_to, {"gy": g_to, "slab": y_to * N_R + rr}

    def column(k):
        d_lo, dz = COLUMN[k]
        x_to, z_to = lax.rem(x_lo + d_lo, 2), lax.rem(z + dz, 8)
        w_to = lax.rem(lax.rem(z_to, 4) + 4 - yy, 4) * 4 + x_to * 2 + lax.div(z_to, 4)
        return w_to, {"slab": yy * N_R + x_to * 8 + z_to}

    def across(slab_of):
        found = []
        for d_hi in range(2):
            to_hi = lax.rem(x_hi + d_hi, 2)
            for k in range(4):
                to = slab_of(k)
                found.append((to_hi, k, to, (to != slab) if d_hi == 0 else None))
        return found

    owners = across(lambda k: k * N_R + near + lax.rem(yy + k, 4))
    blocks = across(lambda k: from_y * N_R + near + k)
    at_home = home.astype(jnp.int32)

    def guarded(away, action):
        if away is None:
            action()
        else:
            pl.when(away)(action)

    def device_of(to_hi, to):
        return {"gy": to_hi * 2 + core, "slab": to}

    barrier = pltpu.get_barrier_semaphore()

    def greet(device):
        pl.semaphore_signal(barrier, inc=1, device_id=device, device_id_type=MESH)

    for k in range(15):
        greet(plane(k)[2])
        greet(column(k)[1])
    for to_hi, _, to, away in owners + blocks:
        guarded(away, functools.partial(greet, device_of(to_hi, to)))

    def copy_to(source, target, send_sem, recv_sem, device):
        return pltpu.make_async_remote_copy(
            src_ref=source,
            dst_ref=target,
            send_sem=send_sem,
            recv_sem=recv_sem,
            device_id=device,
            device_id_type=MESH,
        )

    started = []

    def start_all(sem, copies):
        made = [copy_to(a, b, sem.at[0, k], sem.at[1, k], device) for k, (a, b, device) in enumerate(copies)]
        for copy in made:
            copy.start()
        started.extend((None, copy) for copy in made)
        return made

    def finish(made):
        for copy in made:
            copy.wait_recv()

    def drain(count):
        for away, copy in started[:count]:
            guarded(away, copy.wait_send)
        del started[:count]

    plane_to = [plane(k) for k in range(15)]
    column_to = [column(k) for k in range(15)]
    slot = {d: k for k, d in enumerate(PLANE)}

    def window(w):
        return pl.ds(pl.multiple_of(w * 8, 8), 8)

    def send_home(index, source, target):
        sem = ref.home_sem.at[index]
        for k, (to_hi, _, to, away) in enumerate(blocks):
            copy = copy_to(source, target.at[mine], sem.at[0, k], sem.at[1, mine], device_of(to_hi, to))
            guarded(away, copy.start)
            started.append((away, copy))

        @pl.when(home)
        def _():
            target[mine] = source[...]

    def come_home(index, source, target):
        sem = ref.home_sem.at[index]
        for k, (from_hi, y, origin, away) in enumerate(owners):
            place = 4 * from_hi + y
            copy = copy_to(source, target.at[place], sem.at[0, k], sem.at[1, place], device_of(from_hi, origin))
            guarded(away, copy.wait_recv)

    def in_block_order(messages):
        rows = []
        for n in range(4):
            rows.append(jnp.concatenate([m[:, OWN * n : OWN * n + OWN] for m in messages], axis=1))
        return dot(jnp.concatenate(rows, axis=0), ref.v_gather[...], NN, HIGHEST)

    def depth_stage(cells_of, x):
        for pair in range(2):
            pieces = [cells_of(x, slice((2 * pair + h) * Q, (2 * pair + h + 1) * Q)).reshape(Q * TZ, Y) for h in range(2)]
            zz = dot(ref.v_depth[...], jnp.concatenate(pieces, axis=1), NN)
            for h in range(2):
                part = zz[:, h * Y : (h + 1) * Y]
                ref.z_all[2 * pair + h, x, :, 0:Y] = part[:LANES]
                ref.z_all[2 * pair + h, x, :, Y:] = part[LANES:]

    def to_window(index, beside_first, beside_second):
        table = ref.v_y_table[...]
        gsend, grecv = ref.gsend.at[index], ref.grecv.at[index]
        for c in range(2):
            rows = [ref.z_all[q, x, 24 * p : 24 * p + 24, :] for p in range(8) for x in range(CX) for q in (c, c + 2)]
            wide = dot(table, jnp.concatenate(rows, axis=0).astype(BF16), NT_DIMS)
            for p in range(8):
                gsend[2 * (p // 4) + c, p % 4] = pack(wide[:, 144 * p : 144 * p + 144], [])
        if index == 0:
            pl.semaphore_wait(barrier, 30 + 16 - 2 * at_home)
        sem = ref.plane_sem.at[index, 0]
        first = start_all(sem, [(gsend.at[g, y], grecv.at[k], to) for k, (g, y, to) in enumerate(plane_to)])
        beside_first()
        finish(first)
        for dy in range(N_Y):
            total = gsend[gy, yy] if dy == 0 else None
            for d_hi in range(2):
                for d_core in range(2):
                    if (d_hi, d_core, dy) in slot:
                        term = grecv[slot[d_hi, d_core, dy]]
                        total = term if total is None else total + term
            base = lax.rem(yy + N_Y - dy, N_Y) * ROWS
            for x, piece in enumerate(unpack(total)):
                ref.g12[pl.ds(pl.multiple_of(base + 24 * x, 8), 24), 0:48] = piece

        f = product(ref.v_rows, 0, ref.g12[:, 0:48])
        msend, mrecv = ref.msend.at[index], ref.mrecv.at[index]
        msend[...] = jnp.concatenate([f[0:128], f[128:256], jnp.zeros((128, 32), F32)], axis=1)
        ninth = jnp.concatenate([f[256:272], f[272:288]], axis=1)
        for j in range(4):
            old = msend[pl.ds(j, N_R, stride=8), :]
            msend[pl.ds(j, N_R, stride=8), :] = jnp.concatenate(
                [old[:, 0:96], ninth[:, 24 * j : 24 * j + 24], old[:, 120:128]], axis=1
            )
        sem = ref.column_sem.at[index, 0]
        before = len(started)
        second = start_all(sem, [(msend.at[window(w)], mrecv.at[k], to) for k, (w, to) in enumerate(column_to)])
        drain(before)
        beside_second()
        finish(second)
        m = msend[window(own_window), :]
        for k in range(15):
            m = m + mrecv[k]

        last = jnp.concatenate([m[j : j + 1, 96:120] for j in range(4)], axis=1)
        nine = jnp.concatenate([m[:, 0:96], last, jnp.zeros((7, 96), F32)], axis=0)
        expand = ref.v_expand[...].astype(BF16)
        high, low = halves_of(nine)
        spread = dot(jnp.concatenate([high, low], axis=0), jnp.concatenate([expand, expand], axis=0), TN)
        spread = spread * ref.v_keep[...]
        parts = {}
        for n in range(4):
            base = 24 * n
            total = spread[base : base + 8] + spread[base + 8 : base + 16] + spread[base + 16 : base + 24]
            parts[n // 2, n % 2] = total[:, 0:OWN]
        return parts

    def packed(parts):
        end = jnp.zeros((Q, 128 - 4 * OWN), F32)
        return jnp.concatenate([parts[part, h] for h in range(2) for part in range(2)] + [end], axis=1)

    def from_mixed(index, mixed, local, beside_first, beside_second):
        pad = jnp.zeros((Q, 128 - OWN), F32)
        wide = [jnp.concatenate([mixed[part, h], pad], axis=1) for part in range(2) for h in range(2)]
        tiled = jnp.concatenate([v for v in wide for _ in range(3)], axis=0) * ref.v_keep[...]
        expand = ref.v_expand[...].astype(BF16)
        u = dot(jnp.concatenate([expand, expand], axis=1), jnp.concatenate(halves_of(tiled), axis=1), NT_DIMS)
        last = jnp.concatenate([u[8:9, 24 * j : 24 * j + 24] for j in range(4)] + [jnp.zeros((4, 24), F32)], axis=0)
        rsend, rall = ref.rsend.at[index], ref.rall.at[index]
        rsend[...] = jnp.concatenate([u[0:8], last, local], axis=1)
        rall[window(own_window), :] = rsend[...]
        sem = ref.column_sem.at[index, 1]
        before = len(started)
        third = start_all(sem, [(rsend, rall.at[window(own_window)], to) for _, to in column_to])
        drain(before)
        beside_first()
        finish(third)
        ninth = jnp.concatenate([rall[pl.ds(j, N_R, stride=8), :][:, 96:120] for j in range(4)], axis=1)
        f = jnp.concatenate([rall[:, 0:48], rall[:, 48:96], ninth[:, 0:48], ninth[:, 48:96]], axis=0)
        h = product(ref.v_rows, 2, f)
        local = rall[0:8, 120:128]
        for w in range(1, N_R):
            local = local + rall[8 * w : 8 * w + 8, 120:128]
        hsend, hall = ref.hsend.at[index], ref.hall.at[index]
        for y in range(N_Y):
            rows = [h[y * ROWS + 24 * x : y * ROWS + 24 * x + 24] for x in range(CX)]
            hsend[y] = pack(jnp.concatenate(rows, axis=1), [local])
        hall[yy, gy] = hsend[yy]
        sem = ref.plane_sem.at[index, 1]
        before = len(started)
        fourth = start_all(sem, [(hsend.at[y], hall.at[yy, gy], to) for _, y, to in plane_to])
        drain(before)
        beside_second()
        finish(fourth)
        for y in range(N_Y):
            for g in range(N_GY):
                base = 24 * (4 * (g // 2) + y)
                for x, piece in enumerate(unpack(hall[y, g])):
                    for h in range(2):
                        ref.hx[x, 2 * h + g % 2, :, base : base + 24] = piece[:, 24 * h : 24 * h + 24]

    ready("depth", "y_table")
    for x in range(CX):
        fields[x].wait()
        depth_stage(lambda x, c: ref.v_field[x, c], x)

    def send_weights():
        ready("weight", "select", "place")
        flat = ref.v_weight[...].astype(F32).reshape(2 * C * Q, BLOCK).astype(BF16)
        picked = dot(ref.v_select[...][:, 0:BLOCK].astype(BF16), flat, NT_DIMS)
        for k in range(8):
            ref.wsend[k] = picked[8 * k : 8 * k + 8]
        for e in range(2):
            row = picked[64 + e : 65 + e]
            lanes = [row[:, 128 * j : 128 * j + 128] for j in range(4)]
            ref.esend[e] = jnp.concatenate([*lanes, jnp.zeros((4, 128), F32)], axis=0)
        own = 2 * turn + x_hi
        for k, (to_hi, y, to, away) in enumerate(owners):
            source = ref.wsend.at[4 * to_hi + y]
            copy = copy_to(source, ref.wrecv.at[own], ref.w_sem.at[0, k], ref.w_sem.at[1, own], device_of(to_hi, to))
            guarded(away, copy.start)
            started.append((away, copy))
        for e in range(2):
            to_hi, y = lax.div(turn, 2), lax.rem(2 * turn, 4) + e
            to = y * N_R + near + lax.rem(yy + y, 4)
            copy = copy_to(
                ref.esend.at[e], ref.erecv.at[x_hi], ref.e_sem.at[0, e], ref.e_sem.at[1, x_hi], device_of(to_hi, to)
            )
            here = jnp.logical_and(to_hi == x_hi, to == slab)
            away = jnp.logical_not(here)
            pl.when(away)(copy.start)
            started.append((away, copy))

            @pl.when(here)
            def _():
                ref.erecv[x_hi] = ref.esend[e]

        @pl.when(home)
        def _():
            ref.wrecv[own] = ref.wsend[mine]

        ready("rows", "expand", "keep")

    def receive_weights():
        for k, (from_hi, t, origin, away) in enumerate(blocks):
            at = 2 * t + from_hi
            copy = copy_to(
                ref.wsend.at[0], ref.wrecv.at[at], ref.w_sem.at[0, k], ref.w_sem.at[1, at], device_of(from_hi, origin)
            )
            guarded(away, copy.wait_recv)
        origin = from_y * N_R + near + lax.div(mine, 2)
        for hi in range(2):
            copy = copy_to(
                ref.esend.at[0], ref.erecv.at[hi], ref.e_sem.at[0, hi], ref.e_sem.at[1, hi], device_of(hi, origin)
            )
            pl.when(jnp.logical_or(x_hi != hi, origin != slab))(copy.wait_recv)
        ninths = [jnp.concatenate([ref.erecv[hi, j : j + 1, :] for j in range(4)], axis=1) for hi in range(2)]
        received = jnp.concatenate([ref.wrecv[...].reshape(64, 512), *ninths, jnp.zeros((6, 512), F32)], axis=0)
        ref.owned[...] = dot(received.astype(BF16), ref.v_place[...].astype(BF16), TN)

    def local_products():
        kron = channel_matrix(ref.v_lw[...], ref.v_repeat[...], True)
        for n in range(CX * CHUNKS):
            ref.local_part[n] = dot(kron, ref.cells[n], NN)

    def prepare_cells():
        ready("lw", "repeat", "depth_back", "y_back", "gather")
        for copy in cots:
            copy.wait()
        for x in range(CX):
            for r in range(CHUNKS):
                n = x * CHUNKS + r
                ref.cells[n] = chunk_of(ref.v_field[x, :, 16 * r : 16 * r + 16, :]).astype(BF16)
                ref.cot_cells[n] = chunk_of(ref.v_cot[x, :, 16 * r : 16 * r + 16, :])

    def beside_column():
        receive_weights()
        prepare_cells()

    parts = to_window(0, send_weights, beside_column)

    other_core = {"gy": x_hi * 2 + 1 - core}
    ref.qbuf[core] = packed(parts)
    copy = copy_to(ref.qbuf.at[core], ref.qbuf.at[core], ref.core_sem.at[0, 0], ref.core_sem.at[0, 1], other_core)
    copy.start()
    copy.wait_recv()
    started.append((None, copy))
    mixed_r = jnp.zeros((Q, BLOCK), F32)
    mixed_i = jnp.zeros((Q, BLOCK), F32)

    def weights(i):
        return ref.owned[8 * i : 8 * i + 8, 0:BLOCK], ref.owned[256 + 8 * i : 264 + 8 * i, 0:BLOCK]

    for q in range(N_GY):
        both = ref.qbuf[q % 2]
        base = 2 * OWN * (q // 2)
        real, imag = both[:, base : base + OWN], both[:, base + OWN : base + 2 * OWN]
        real, imag = jnp.concatenate([real, real], axis=1), jnp.concatenate([imag, imag], axis=1)
        for c in range(Q):
            mr, mi = real[c : c + 1], imag[c : c + 1]
            w0, w1 = weights(q * Q + c)
            mixed_r = mixed_r + (mr * w0 - mi * w1)
            mixed_i = mixed_i + (mr * w1 + mi * w0)
    mixed = {(p, h): v[:, OWN * h : OWN * h + OWN] for p, v in enumerate((mixed_r, mixed_i)) for h in range(2)}

    def beside_modes():
        send_home(0, ref.qbuf, ref.home_modes)
        local_products()

    def modes_home():
        come_home(0, ref.qbuf, ref.home_modes)
        ref.block_modes[...] = in_block_order([ref.home_modes[k].reshape(16, 128) for k in range(8)])

    from_mixed(0, mixed, jnp.zeros((8, 8), F32), beside_modes, modes_home)

    stores = []

    def store(source, target):
        copy = pltpu.make_async_copy(source, target, ref.store_sem.at[len(stores)])
        copy.start()
        stores.append(copy)

    for x in range(CX):
        spectral_rows(ref.hx, ref.v_y_back, ref.v_depth_back, ref.spec.at[x], x)
    for x in range(CX):
        for r in range(CHUNKS):
            n = x * CHUNKS + r
            rows = slice(16 * r, 16 * r + 16)
            pre = chunk_of(ref.spec[x, :, rows, :]) + ref.local_part[n]
            cdf = 0.5 * (1.0 + lax.erf(pre * ROOT_HALF))
            slope = cdf + pre * jnp.exp(-0.5 * pre * pre) * INV_ROOT_TWO_PI
            grad = ref.cot_cells[n] * slope
            ref.v_out[x, :, rows, :] = unchunk(pre * cdf).astype(BF16)
            ref.grad_pre[x, :, rows, :] = unchunk(grad).astype(BF16)
        store(ref.v_out.at[x], ref.out.at[:, x])
        store(ref.grad_pre.at[x], ref.grad_cells.at[:, x])
        depth_stage(lambda x, c: ref.grad_pre[x, c], x)
    def local_terms():
        total = jnp.zeros((256, 256), F32)
        for n in range(CX * CHUNKS):
            x, r = divmod(n, CHUNKS)
            grad = chunk_of(ref.grad_pre[x, :, 16 * r : 16 * r + 16, :]).astype(BF16)
            total = total + dot(ref.cells[n], grad, NT_DIMS)
        kept = jnp.where(same_row((256, 256)), total, 0.0)
        repeat = ref.v_repeat[...].astype(F32)
        local = dot(dot(repeat, kept, TN, HIGHEST), repeat, NN, HIGHEST)
        for g in range(N_GY):
            for y in range(N_Y):
                ref.lsend[g, y, :, 0:8] = local[8 * g : 8 * g + 8, 8 * y : 8 * y + 8]
        copies = [(ref.lsend.at[g, y], ref.lrecv.at[k], to) for k, (g, y, to) in enumerate(plane_to)]
        local_copies.extend(start_all(ref.local_sem, copies))

    local_copies = []
    parts = to_window(1, local_terms, lambda: None)
    ref.grads[...] = packed(parts)
    gr, gi = (jnp.concatenate([parts[p, 0], parts[p, 1]], axis=1) for p in range(2))
    for i in range(C):
        q, c = divmod(i, Q)
        w0, w1 = weights(i)
        ref.sums[q, c : c + 1, 0:BLOCK] = jnp.sum(gr * w0 + gi * w1, axis=0, keepdims=True)
        ref.sums[q, 8 + c : 9 + c, 0:BLOCK] = jnp.sum(gi * w0 - gr * w1, axis=0, keepdims=True)
    for k in range(2):
        found = {}
        for h in range(2):
            both = ref.sums[2 * h + k]
            both = both[:, 0:OWN] + both[:, OWN:BLOCK]
            found[0, h], found[1, h] = both[0:8], both[8:16]
        ref.qsend[k] = packed(found)
    copy = copy_to(ref.qsend.at[1 - core], ref.qrecv, ref.core_sem.at[1, 0], ref.core_sem.at[1, 1], other_core)
    copy.start()
    copy.wait_recv()
    started.append((None, copy))
    both = ref.qsend[core] + ref.qrecv[...]
    mixed = {(p, h): both[:, OWN * (2 * h + p) : OWN * (2 * h + p) + OWN] for p in range(2) for h in range(2)}

    def weight_gradient():
        come_home(1, ref.grads, ref.home_grads)
        grads = in_block_order([ref.home_grads[k] for k in range(8)])
        grads = jnp.where(x_hi == 0, grads[0:16], grads[16:32])
        gr, gi = grads[0:8, 0:BLOCK], grads[8:16, 0:BLOCK]
        for i in range(C):
            q, c = divmod(i, Q)
            row = 32 * (q // 2) + 8 * (q % 2) + c
            mr, mi = ref.block_modes[row : row + 1, 0:BLOCK], ref.block_modes[row + 16 : row + 17, 0:BLOCK]
            ref.v_grad_spectral[0, i] = mr * gr + mi * gi
            ref.v_grad_spectral[1, i] = mr * gi - mi * gr
        store(ref.v_grad_spectral, ref.grad_spectral)

    finish(local_copies)
    local = ref.lsend[gy, yy, :, 0:8]
    for k in range(15):
        local = local + ref.lrecv[k, :, 0:8]
    from_mixed(1, mixed, local, lambda: send_home(1, ref.grads, ref.home_grads), weight_gradient)
    for y in range(N_Y):
        for g in range(N_GY):
            corner = ref.hall[1, y, g, 24:32, 48:56]
            ref.grad_local[8 * g : 8 * g + 8, 8 * y : 8 * y + 8] = corner * FORWARD_SCALE
    for copy in stores:
        copy.wait()
    drain(len(started))


def last_kernel(
    grad_cells, hx, early_out, early_spectral, early_local, lw, repeat, y_back, depth_back,
    out, grad_in, grad_spectral, grad_local,
    v_hx, v_cells, v_lw, v_repeat, v_y_back, v_depth_back, v_out, spec, v_pass, v_spectral, v_local, sem, pass_sem, store_sem,
):
    gy = lax.axis_index("gy")
    staged = [
        (hx, v_hx),
        (y_back.at[gy], v_y_back),
        (depth_back, v_depth_back),
        (lw, v_lw),
        (repeat, v_repeat),
        *[(grad_cells.at[:, x], v_cells.at[x]) for x in range(CX)],
    ]
    loads = [pltpu.make_async_copy(a, b, sem.at[k]) for k, (a, b) in enumerate(staged)]
    passed = [(early_out, v_pass, out), (early_spectral, v_spectral, grad_spectral), (early_local, v_local, grad_local)]
    arrive = [pltpu.make_async_copy(a, b, pass_sem.at[0, k]) for k, (a, b, _) in enumerate(passed)]
    leave = [pltpu.make_async_copy(b, c, pass_sem.at[1, k]) for k, (_, b, c) in enumerate(passed)]
    for copy in loads + arrive:
        copy.start()
    for copy in loads[:5]:
        copy.wait()
    kron = channel_matrix(v_lw[...], v_repeat[...], False)
    stores = []
    for x in range(CX):
        spectral_rows(v_hx, v_y_back, v_depth_back, spec, x)
        if x == 0:
            for first, second in zip(arrive, leave):
                first.wait()
                second.start()
        loads[5 + x].wait()
        for r in range(CHUNKS):
            rows = slice(16 * r, 16 * r + 16)
            cells = chunk_of(v_cells[x, :, rows, :]).astype(BF16)
            total = chunk_of(spec[:, rows, :]) + dot(kron, cells, NN)
            v_out[x, :, rows, :] = unchunk(total).astype(BF16)
        copy = pltpu.make_async_copy(v_out.at[x], grad_in.at[:, x], store_sem.at[x])
        copy.start()
        stores.append(copy)
    for copy in leave + stores:
        copy.wait()


def per_device(field_in, cotangent, spectral_weight, local_weight):
    cells = (C, CX, TZ, Y)
    depth = depth_table()
    tables = y_tables()
    high = tables.astype(BF16)
    low = (tables - high.astype(np.float64)).astype(BF16)
    expand, keep = unit_tables()
    select, place, gather = owner_tables()
    values = {
        "field": field_in.reshape(cells),
        "cot": cotangent.reshape(cells),
        "weight": jnp.transpose(spectral_weight, (0, 2, 3, 1)),
        "lw": local_weight,
        "depth": depth.astype(BF16),
        "depth_back": np.ascontiguousarray(depth.T).astype(BF16),
        "y_table": high,
        "y_back": np.concatenate([high, low, high], axis=1),
        "rows": row_tables(),
        "expand": expand,
        "keep": keep,
        "select": select.astype(np.float32),
        "place": place.astype(np.float32),
        "gather": gather.astype(np.float32),
        "repeat": np.repeat(np.eye(C), 8, axis=0).astype(BF16),
    }
    values = {name: jnp.asarray(value) for name, value in values.items()}
    vmem, anywhere = pl.BlockSpec(memory_space=pltpu.VMEM), pl.BlockSpec(memory_space=pl.ANY)
    field, mixed, local = ((cells, BF16), ((2, C, Q, BLOCK), F32), ((C, C), F32))
    outs = [field, field, mixed, ((CX, N_GY, 24, 256), F32), local]
    early_out, grad_cells, early_spectral, hx, early_local = pl.pallas_call(
        layer_kernel,
        out_shape=[jax.ShapeDtypeStruct(shape, dtype) for shape, dtype in outs],
        in_specs=[anywhere for _ in INPUTS],
        out_specs=[anywhere] * 3 + [vmem] * 2,
        scratch_shapes=[pltpu.VMEM(shape, dtype) for shape, dtype in SCRATCH.values()]
        + [DMA(shape) for shape in SEMAPHORES.values()],
        compiler_params=pltpu.CompilerParams(
            collective_id=0, has_side_effects=True, vmem_limit_bytes=56 * 1024 * 1024
        ),
        name="spectral_layer",
    )(*[values[name] for name in INPUTS])
    output, grad_input, grad_spectral, grad_local = pl.pallas_call(
        last_kernel,
        out_shape=[jax.ShapeDtypeStruct(shape, dtype) for shape, dtype in (field, field, mixed, local)],
        in_specs=[anywhere] * 9,
        out_specs=[anywhere] * 4,
        scratch_shapes=[
            pltpu.VMEM((CX, N_GY, 24, 256), F32),
            pltpu.VMEM((CX, C, TZ, Y), BF16),
            pltpu.VMEM((C, C), BF16),
            pltpu.VMEM((256, C), BF16),
            pltpu.VMEM((6 * KY, 2 * Y), BF16),
            pltpu.VMEM((Q * TZ, 2 * K * Q), BF16),
            pltpu.VMEM((CX, C, TZ, Y), BF16),
            pltpu.VMEM((C, TZ, Y), F32),
            *[pltpu.VMEM(shape, dtype) for shape, dtype in (field, mixed, local)],
            DMA((8,)),
            DMA((2, 3)),
            DMA((CX,)),
        ],
        compiler_params=pltpu.CompilerParams(vmem_limit_bytes=56 * 1024 * 1024),
        name="last_cells",
    )(grad_cells, hx, early_out, early_spectral, early_local, *[values[n] for n in ("lw", "repeat", "y_back", "depth_back")])
    return (
        output.reshape(field_in.shape),
        grad_input.reshape(field_in.shape),
        jnp.transpose(grad_spectral, (0, 3, 1, 2)),
        grad_local,
    )


def solution(mesh):
    placed = (
        P(None, "slab", None, None, "gy"),
        P(None, "slab", None, None, "gy"),
        P(None, "slab", None, "gy"),
        P(),
    )
    return jax.shard_map(
        per_device,
        mesh=mesh,
        in_specs=placed,
        out_specs=(
            P(None, "slab", None, None, "gy"),
            P(None, "slab", None, None, "gy"),
            P(None, "slab", None, "gy"),
            P(),
        ),
        check_vma=False,
    )
```

```python
import functools
import math
import types

import jax
import jax.numpy as jnp
import numpy as np
from jax import lax
from jax.experimental import pallas as pl
from jax.experimental.pallas import tpu as pltpu
from jax.sharding import PartitionSpec as P

C = 32
KX = 12
KY = 12
KZ = 12
NT = 2
NZ = 32
NX = 192
NY = 512
CX = 3
N_GY = 4
N_Y = 4
N_R = 16
Q = C // N_GY
K = NT * KZ
TZ = NT * NZ
Y = NY // N_GY
BLOCK = 54
OWN = 27
UNITS = 9
ROWS = 72
LANES = K * Q

FORWARD_SCALE = 1.0 / math.sqrt(NX * NY * NZ * NT)
INVERSE_SCALE = 1.0 / math.sqrt(KX * KY * KZ * NT)
ROOT_HALF = 0.7071067811865476
INV_ROOT_TWO_PI = 0.3989422804014327
HIGHEST = lax.Precision.HIGHEST
PLANE = [(h, c, y) for h in range(2) for c in range(2) for y in range(N_Y) if (h, c, y) != (0, 0, 0)]
PLANE.sort(key=lambda d: -(3 * d[0] + min(d[2], N_Y - d[2])))
COLUMN = [(x, z) for x in range(2) for z in range(8) if (x, z) != (0, 0)]
COLUMN.sort(key=lambda d: -(0.5 * d[0] + min(d[1], 8 - d[1])))
F32 = jnp.float32
BF16 = jnp.bfloat16
MESH = pl.DeviceIdType.MESH


def frequencies(kept):
    values = np.arange(kept)
    return np.where(values < kept // 2, values, values - kept)


def depth_table():
    t, z = np.divmod(np.arange(TZ), NZ)
    kt, kz = np.divmod(np.arange(K), KZ)
    product = (t[None] * kt[:, None] * NZ + z[None] * frequencies(KZ)[kz][:, None] * NT) % TZ
    angle = product * (2.0 * np.pi / TZ)
    parts = np.stack([np.cos(angle), -np.sin(angle)])
    full = np.einsum("pks,cd->pkcds", parts, np.eye(Q))
    return full.reshape(2 * K * Q, Q * TZ)


def y_tables():
    product = (frequencies(KY)[:, None] * np.arange(NY)[None]) % NY
    angle = product * (2.0 * np.pi / NY)
    cos, sin = np.cos(angle), np.sin(angle)
    full = np.stack([np.stack([cos, sin]), np.stack([-sin, cos])])
    full = full.reshape(2, 2, KY, N_GY, Y).transpose(3, 0, 2, 1, 4)
    return full.reshape(N_GY, 2 * KY, 2 * Y)


def unit_tables():
    lane = np.arange(128)
    row = np.arange(96)
    expand = (lane[None] // 3 == np.arange(16)[:, None]) & (lane[None] < OWN)
    keep = ((row[:, None] // 8) % 3 == lane[None] % 3) & (lane[None] < OWN)
    return expand.astype(np.float32), keep.astype(np.float32)


def row_tables():
    main = [9 * w + j for w in range(N_R) for j in range(8)]
    ninth = [9 * w + 8 for w in range(N_R)]
    pairs = np.array(main + main + ninth + ninth)
    part = np.array([0] * 128 + [1] * 128 + [0] * 16 + [1] * 16)
    y, x, part_in, ky = np.unravel_index(np.arange(288), (N_Y, CX, 2, KY))
    row = 48 * y[None] + 3 * np.arange(N_R)[:, None] + x[None]
    freq = frequencies(KX)[pairs // KY]
    angle = (freq[None, :, None] * row[:, None, :]) % NX * (2.0 * np.pi / NX)
    sign = np.where(part == 0, 1.0, -1.0)[:, None]
    value = np.where(part[:, None] == part_in[None], np.cos(angle), sign * np.sin(angle))
    value = np.where((pairs % KY)[:, None] == ky[None], value, 0.0)
    forward, inverse = value * FORWARD_SCALE, value.transpose(0, 2, 1) * INVERSE_SCALE
    parts = []
    for full in (forward, inverse):
        high = full.astype(BF16)
        parts += [high, (full - high.astype(np.float64)).astype(BF16)]
    return np.stack(parts, axis=1)


def owner_tables():
    select = np.zeros((4, 72, 128))
    place = np.zeros((8, 72, 128))
    gather = np.zeros((4, 8, OWN, 128))
    for t in range(4):
        count = [0] * 8
        for mode in range(BLOCK):
            unit = 18 * t + mode // 3
            part, other = unit % 8, 3 * (unit // 8) + mode % 3
            n = count[part]
            count[part] += 1
            select[t, 8 * part + n if n < 8 else 64 + part - 2 * t, mode] = 1.0
            for x in range(2):
                place[part, 16 * t + 8 * x + n if n < 8 else 64 + x, OWN * x + other] = 1.0
            gather[t, part, other, mode] = 1.0
    return select, place, gather.reshape(4, 8 * OWN, 128)


def dot(a, b, dims, precision=None):
    return lax.dot_general(a, b, (dims, ((), ())), precision=precision, preferred_element_type=F32)


NN = ((1,), (0,))
NT_DIMS = ((1,), (1,))
TN = ((0,), (0,))


def pack(g, corner):
    tail = g[:, 128:144]
    width = 80 - 8 * len(corner)
    below = jnp.concatenate([tail[0:8], tail[8:16], tail[16:24], *corner, jnp.zeros((8, width), F32)], axis=1)
    return jnp.concatenate([g[:, 0:128], below], axis=0)


def unpack(message):
    below = message[24:32]
    tail = jnp.concatenate([below[:, 0:16], below[:, 16:32], below[:, 32:48]], axis=0)
    body = message[0:24]
    return [body[:, 0:48], body[:, 48:96], jnp.concatenate([body[:, 96:128], tail], axis=1)]


def halves_of(values):
    high = values.astype(BF16)
    return high, (values - high.astype(F32)).astype(BF16)


def product(rows_ref, first, values):
    high, low = halves_of(values)
    both = dot(rows_ref[first], jnp.concatenate([high, low], axis=1), NN)
    width = values.shape[1]
    return both[:, :width] + both[:, width:] + dot(rows_ref[first + 1], high, NN)


def chunk_of(values):
    values = values.astype(F32)
    return jnp.concatenate([values[:, 0:8].reshape(256, Y), values[:, 8:16].reshape(256, Y)], axis=1)


def unchunk(values):
    halves = [values[:, :Y].reshape(C, 8, Y), values[:, Y:].reshape(C, 8, Y)]
    return jnp.concatenate(halves, axis=1)


def same_row(shape):
    row = lax.broadcasted_iota(jnp.int32, shape, 0)
    col = lax.broadcasted_iota(jnp.int32, shape, 1)
    return row % 8 == col % 8


def channel_matrix(weight, repeat, transposed):
    half = dot(repeat, weight, NT_DIMS if transposed else NN).astype(BF16)
    full = dot(half, repeat, NT_DIMS)
    return jnp.where(same_row(full.shape), full, 0.0).astype(BF16)


CHUNKS = TZ // 16
BIG = (32, 128)
TILE = (8, 128)
DMA = pltpu.SemaphoreType.DMA

INPUTS = ["field", "cot", "weight", "lw", "depth", "depth_back", "y_table", "y_back", "rows", "expand", "keep"]
INPUTS += ["select", "place", "gather", "repeat"]
OUTPUTS = ["out", "grad_cells", "grad_spectral", "hx", "grad_local"]
SCRATCH = {
    "v_field": ((CX, C, TZ, Y), BF16),
    "v_cot": ((CX, C, TZ, Y), BF16),
    "v_weight": ((2 * C * Q, BLOCK), BF16),
    "v_lw": ((C, C), BF16),
    "v_depth": ((2 * K * Q, Q * TZ), BF16),
    "v_depth_back": ((Q * TZ, 2 * K * Q), BF16),
    "v_y_table": ((32, 2 * Y), BF16),
    "v_y_back": ((80, 2 * Y), BF16),
    "v_rows": ((4, 288, 288), BF16),
    "v_expand": ((16, 128), F32),
    "v_keep": ((96, 128), F32),
    "v_select": ((72, 128), F32),
    "v_place": ((72, 128), F32),
    "v_gather": ((8 * OWN, 128), F32),
    "v_repeat": ((256, C), BF16),
    "grad_pre": ((CX, C, TZ, Y), BF16),
    "spec": ((CX, C, TZ, Y), F32),
    "cells": ((CX * CHUNKS, 256, 256), BF16),
    "cot_cells": ((CX * CHUNKS, 256, 256), F32),
    "local_part": ((CX * CHUNKS, 256, 256), F32),
    "lsend": ((N_GY, N_Y, *TILE), F32),
    "lrecv": ((15, *TILE), F32),
    "z_all": ((N_GY, CX, LANES, 256), F32),
    "gsend": ((2, N_GY, N_Y, *BIG), F32),
    "grecv": ((2, 15, *BIG), F32),
    "g12": ((288, 128), F32),
    "msend": ((2, 136, 128), F32),
    "mrecv": ((2, 15, *TILE), F32),
    "qbuf": ((2, *TILE), F32),
    "qsend": ((2, *TILE), F32),
    "qrecv": (TILE, F32),
    "sums": ((N_GY, 16, 128), F32),
    "grads": (TILE, F32),
    "rsend": ((2, *TILE), F32),
    "rall": ((2, 136, 128), F32),
    "hsend": ((2, N_Y, *BIG), F32),
    "hall": ((2, N_Y, N_GY, *BIG), F32),
    "v_out": ((CX, C, TZ, Y), BF16),
    "v_grad_spectral": ((2, C, Q, BLOCK), F32),
    "wsend": ((8, 8, 512), F32),
    "wrecv": ((8, 8, 512), F32),
    "esend": ((2, *TILE), F32),
    "erecv": ((2, *TILE), F32),
    "owned": ((2 * C * Q, 128), F32),
    "home_modes": ((8, 2, *TILE), F32),
    "home_grads": ((8, *TILE), F32),
    "block_modes": ((64, 128), F32),
}
SEMAPHORES = {
    "load_sem": (13,),
    "cell_sem": (2, CX),
    "store_sem": (2 * CX + 1,),
    "plane_sem": (2, 2, 2, 15),
    "column_sem": (2, 2, 2, 15),
    "core_sem": (2, 2),
    "local_sem": (2, 15),
    "w_sem": (2, 8),
    "e_sem": (2, 2),
    "home_sem": (2, 2, 8),
}


def spectral_rows(hx, y_back, depth_back, spec, x):
    for pair in range(2):
        halves = []
        for q in (2 * pair, 2 * pair + 1):
            h = hx[x, q, :, 0:LANES]
            high = h.astype(BF16).astype(F32)
            stacked = jnp.concatenate([high, high, h - high, jnp.zeros((8, LANES), F32)], axis=0).astype(BF16)
            u = dot(stacked, y_back[...], TN)
            halves.append(jnp.concatenate([u[:, :Y], u[:, Y:]], axis=0).astype(BF16))
        s = dot(depth_back[...], jnp.concatenate(halves, axis=1), NN)
        for h in range(2):
            q = 2 * pair + h
            spec[q * Q : (q + 1) * Q] = s[:, h * Y : (h + 1) * Y].reshape(Q, TZ, Y)


def layer_kernel(*refs):
    ref = types.SimpleNamespace(**dict(zip(INPUTS + OUTPUTS + list(SCRATCH) + list(SEMAPHORES), refs)))

    slab, gy = lax.axis_index("slab"), lax.axis_index("gy")
    yy, rr = lax.div(slab, N_R), lax.rem(slab, N_R)
    x_hi, core = lax.div(gy, 2), lax.rem(gy, 2)
    x_lo, z = lax.div(rr, 8), lax.rem(rr, 8)
    turn, half = lax.rem(z, 4), lax.div(z, 4)
    mine = 4 * x_hi + yy
    near = x_lo * 8 + half * 4
    from_y = lax.rem(turn + 4 - yy, 4)
    own_window = from_y * 4 + x_lo * 2 + half
    home = turn == lax.rem(2 * yy, 4)

    sources = {
        "depth": ref.depth,
        "y_table": ref.y_table.at[gy],
        "weight": ref.weight,
        "select": ref.select.at[turn],
        "place": ref.place.at[mine],
        "rows": ref.rows.at[rr],
        "expand": ref.expand,
        "keep": ref.keep,
        "gather": ref.gather.at[turn],
        "lw": ref.lw,
        "repeat": ref.repeat,
        "depth_back": ref.depth_back,
        "y_back": ref.y_back.at[gy],
    }
    loads = {
        name: pltpu.make_async_copy(source, getattr(ref, "v_" + name), ref.load_sem.at[k])
        for k, (name, source) in enumerate(sources.items())
    }
    fields = [pltpu.make_async_copy(ref.field.at[:, x], ref.v_field.at[x], ref.cell_sem.at[0, x]) for x in range(CX)]
    cots = [pltpu.make_async_copy(ref.cot.at[:, x], ref.v_cot.at[x], ref.cell_sem.at[1, x]) for x in range(CX)]
    fields[0].start()
    loads["depth"].start()
    loads["y_table"].start()
    fields[1].start()
    fields[2].start()
    for name in list(loads)[2:]:
        loads[name].start()
    for copy in cots:
        copy.start()

    def ready(*names):
        for name in names:
            loads[name].wait()

    def plane(k):
        d_hi, d_core, dy = PLANE[k]
        g_to = lax.rem(x_hi + d_hi, 2) * 2 + lax.rem(core + d_core, 2)
        y_to = lax.rem(yy + dy, N_Y)
        return g_to, y_to, {"gy": g_to, "slab": y_to * N_R + rr}

    def column(k):
        d_lo, dz = COLUMN[k]
        x_to, z_to = lax.rem(x_lo + d_lo, 2), lax.rem(z + dz, 8)
        w_to = lax.rem(lax.rem(z_to, 4) + 4 - yy, 4) * 4 + x_to * 2 + lax.div(z_to, 4)
        return w_to, {"slab": yy * N_R + x_to * 8 + z_to}

    def across(slab_of):
        found = []
        for d_hi in range(2):
            to_hi = lax.rem(x_hi + d_hi, 2)
            for k in range(4):
                to = slab_of(k)
                found.append((to_hi, k, to, (to != slab) if d_hi == 0 else None))
        return found

    owners = across(lambda k: k * N_R + near + lax.rem(yy + k, 4))
    blocks = across(lambda k: from_y * N_R + near + k)
    at_home = home.astype(jnp.int32)

    def guarded(away, action):
        if away is None:
            action()
        else:
            pl.when(away)(action)

    def device_of(to_hi, to):
        return {"gy": to_hi * 2 + core, "slab": to}

    barrier = pltpu.get_barrier_semaphore()

    def greet(device):
        pl.semaphore_signal(barrier, inc=1, device_id=device, device_id_type=MESH)

    for k in range(15):
        greet(plane(k)[2])
        greet(column(k)[1])
    for to_hi, _, to, away in owners + blocks:
        guarded(away, functools.partial(greet, device_of(to_hi, to)))

    def copy_to(source, target, send_sem, recv_sem, device):
        return pltpu.make_async_remote_copy(
            src_ref=source,
            dst_ref=target,
            send_sem=send_sem,
            recv_sem=recv_sem,
            device_id=device,
            device_id_type=MESH,
        )

    started = []

    def start_all(sem, copies):
        made = [copy_to(a, b, sem.at[0, k], sem.at[1, k], device) for k, (a, b, device) in enumerate(copies)]
        for copy in made:
            copy.start()
        started.extend((None, copy) for copy in made)
        return made

    def finish(made):
        for copy in made:
            copy.wait_recv()

    def drain(count):
        for away, copy in started[:count]:
            guarded(away, copy.wait_send)
        del started[:count]

    plane_to = [plane(k) for k in range(15)]
    column_to = [column(k) for k in range(15)]
    slot = {d: k for k, d in enumerate(PLANE)}

    def window(w):
        return pl.ds(pl.multiple_of(w * 8, 8), 8)

    def send_home(index, source, target):
        sem = ref.home_sem.at[index]
        for k, (to_hi, _, to, away) in enumerate(blocks):
            copy = copy_to(source, target.at[mine], sem.at[0, k], sem.at[1, mine], device_of(to_hi, to))
            guarded(away, copy.start)
            started.append((away, copy))

        @pl.when(home)
        def _():
            target[mine] = source[...]

    def come_home(index, source, target):
        sem = ref.home_sem.at[index]
        for k, (from_hi, y, origin, away) in enumerate(owners):
            place = 4 * from_hi + y
            copy = copy_to(source, target.at[place], sem.at[0, k], sem.at[1, place], device_of(from_hi, origin))
            guarded(away, copy.wait_recv)

    def in_block_order(messages):
        rows = []
        for n in range(4):
            rows.append(jnp.concatenate([m[:, OWN * n : OWN * n + OWN] for m in messages], axis=1))
        return dot(jnp.concatenate(rows, axis=0), ref.v_gather[...], NN, HIGHEST)

    def depth_stage(cells_of, x):
        for pair in range(2):
            pieces = [cells_of(x, slice((2 * pair + h) * Q, (2 * pair + h + 1) * Q)).reshape(Q * TZ, Y) for h in range(2)]
            zz = dot(ref.v_depth[...], jnp.concatenate(pieces, axis=1), NN)
            for h in range(2):
                part = zz[:, h * Y : (h + 1) * Y]
                ref.z_all[2 * pair + h, x, :, 0:Y] = part[:LANES]
                ref.z_all[2 * pair + h, x, :, Y:] = part[LANES:]

    def to_window(index, beside_first, beside_second):
        table = ref.v_y_table[...]
        gsend, grecv = ref.gsend.at[index], ref.grecv.at[index]
        for c in range(2):
            rows = [ref.z_all[q, x, 24 * p : 24 * p + 24, :] for p in range(8) for x in range(CX) for q in (c, c + 2)]
            wide = dot(table, jnp.concatenate(rows, axis=0).astype(BF16), NT_DIMS)[0 : 2 * KY]
            for p in range(8):
                gsend[2 * (p // 4) + c, p % 4] = pack(wide[:, 144 * p : 144 * p + 144], [])
        if index == 0:
            pl.semaphore_wait(barrier, 30 + 16 - 2 * at_home)
        sem = ref.plane_sem.at[index, 0]
        first = start_all(sem, [(gsend.at[g, y], grecv.at[k], to) for k, (g, y, to) in enumerate(plane_to)])
        beside_first()
        finish(first)
        for dy in range(N_Y):
            total = gsend[gy, yy] if dy == 0 else None
            for d_hi in range(2):
                for d_core in range(2):
                    if (d_hi, d_core, dy) in slot:
                        term = grecv[slot[d_hi, d_core, dy]]
                        total = term if total is None else total + term
            base = lax.rem(yy + N_Y - dy, N_Y) * ROWS
            for x, piece in enumerate(unpack(total)):
                ref.g12[pl.ds(pl.multiple_of(base + 24 * x, 8), 24), 0:48] = piece

        f = product(ref.v_rows, 0, ref.g12[:, 0:48])
        msend, mrecv = ref.msend.at[index], ref.mrecv.at[index]
        msend[0:128, :] = jnp.concatenate([f[0:128], f[128:256], jnp.zeros((128, 32), F32)], axis=1)
        ninth = jnp.concatenate([f[256:272], f[272:288]], axis=1)
        for j in range(4):
            old = msend[pl.ds(j, N_R, stride=8), :]
            msend[pl.ds(j, N_R, stride=8), :] = jnp.concatenate(
                [old[:, 0:96], ninth[:, 24 * j : 24 * j + 24], old[:, 120:128]], axis=1
            )
        sem = ref.column_sem.at[index, 0]
        before = len(started)
        second = start_all(sem, [(msend.at[window(w)], mrecv.at[k], to) for k, (w, to) in enumerate(column_to)])
        drain(before)
        beside_second()
        finish(second)
        m = msend[window(own_window), :]
        for k in range(15):
            m = m + mrecv[k]

        last = jnp.concatenate([m[j : j + 1, 96:120] for j in range(4)], axis=1)
        nine = jnp.concatenate([m[:, 0:96], last, jnp.zeros((7, 96), F32)], axis=0)
        expand = ref.v_expand[...].astype(BF16)
        high, low = halves_of(nine)
        spread = dot(jnp.concatenate([high, low], axis=0), jnp.concatenate([expand, expand], axis=0), TN)
        spread = spread * ref.v_keep[...]
        parts = {}
        for n in range(4):
            base = 24 * n
            total = spread[base : base + 8] + spread[base + 8 : base + 16] + spread[base + 16 : base + 24]
            parts[n // 2, n % 2] = total[:, 0:OWN]
        return parts

    def packed(parts):
        end = jnp.zeros((Q, 128 - 4 * OWN), F32)
        return jnp.concatenate([parts[part, h] for h in range(2) for part in range(2)] + [end], axis=1)

    def from_mixed(index, mixed, local, beside_first, beside_second):
        pad = jnp.zeros((Q, 128 - OWN), F32)
        wide = [jnp.concatenate([mixed[part, h], pad], axis=1) for part in range(2) for h in range(2)]
        tiled = jnp.concatenate([v for v in wide for _ in range(3)], axis=0) * ref.v_keep[...]
        expand = ref.v_expand[...].astype(BF16)
        u = dot(jnp.concatenate([expand, expand], axis=1), jnp.concatenate(halves_of(tiled), axis=1), NT_DIMS)
        last = jnp.concatenate([u[8:9, 24 * j : 24 * j + 24] for j in range(4)] + [jnp.zeros((4, 24), F32)], axis=0)
        rsend, rall = ref.rsend.at[index], ref.rall.at[index]
        rsend[...] = jnp.concatenate([u[0:8], last, local], axis=1)
        rall[window(own_window), :] = rsend[...]
        sem = ref.column_sem.at[index, 1]
        before = len(started)
        third = start_all(sem, [(rsend, rall.at[window(own_window)], to) for _, to in column_to])
        drain(before)
        beside_first()
        finish(third)
        ninth = jnp.concatenate([rall[pl.ds(j, N_R, stride=8), :][:, 96:120] for j in range(4)], axis=1)
        f = jnp.concatenate([rall[0:128, 0:48], rall[0:128, 48:96], ninth[:, 0:48], ninth[:, 48:96]], axis=0)
        h = product(ref.v_rows, 2, f)
        local = rall[0:8, 120:128]
        for w in range(1, N_R):
            local = local + rall[8 * w : 8 * w + 8, 120:128]
        hsend, hall = ref.hsend.at[index], ref.hall.at[index]
        for y in range(N_Y):
            rows = [h[y * ROWS + 24 * x : y * ROWS + 24 * x + 24] for x in range(CX)]
            hsend[y] = pack(jnp.concatenate(rows, axis=1), [local])
        hall[yy, gy] = hsend[yy]
        sem = ref.plane_sem.at[index, 1]
        before = len(started)
        fourth = start_all(sem, [(hsend.at[y], hall.at[yy, gy], to) for _, y, to in plane_to])
        drain(before)
        beside_second()
        finish(fourth)
        for y in range(N_Y):
            for g in range(N_GY):
                base = 24 * (4 * (g // 2) + y)
                for x, piece in enumerate(unpack(hall[y, g])):
                    for h in range(2):
                        ref.hx[x, 2 * h + g % 2, :, base : base + 24] = piece[:, 24 * h : 24 * h + 24]

    ready("depth", "y_table")
    for x in range(CX):
        fields[x].wait()
        depth_stage(lambda x, c: ref.v_field[x, c], x)

    def send_weights():
        ready("weight", "select", "place")
        picked = dot(ref.v_select[...][:, 0:BLOCK].astype(BF16), ref.v_weight[...], NT_DIMS)
        for k in range(8):
            ref.wsend[k] = picked[8 * k : 8 * k + 8]
        for e in range(2):
            row = picked[64 + e : 65 + e]
            lanes = [row[:, 128 * j : 128 * j + 128] for j in range(4)]
            ref.esend[e] = jnp.concatenate([*lanes, jnp.zeros((4, 128), F32)], axis=0)
        own = 2 * turn + x_hi
        for k, (to_hi, y, to, away) in enumerate(owners):
            source = ref.wsend.at[4 * to_hi + y]
            copy = copy_to(source, ref.wrecv.at[own], ref.w_sem.at[0, k], ref.w_sem.at[1, own], device_of(to_hi, to))
            guarded(away, copy.start)
            started.append((away, copy))
        for e in range(2):
            to_hi, y = lax.div(turn, 2), lax.rem(2 * turn, 4) + e
            to = y * N_R + near + lax.rem(yy + y, 4)
            copy = copy_to(
                ref.esend.at[e], ref.erecv.at[x_hi], ref.e_sem.at[0, e], ref.e_sem.at[1, x_hi], device_of(to_hi, to)
            )
            here = jnp.logical_and(to_hi == x_hi, to == slab)
            away = jnp.logical_not(here)
            pl.when(away)(copy.start)
            started.append((away, copy))

            @pl.when(here)
            def _():
                ref.erecv[x_hi] = ref.esend[e]

        @pl.when(home)
        def _():
            ref.wrecv[own] = ref.wsend[mine]

        ready("rows", "expand", "keep")

    def receive_weights():
        for k, (from_hi, t, origin, away) in enumerate(blocks):
            at = 2 * t + from_hi
            copy = copy_to(
                ref.wsend.at[0], ref.wrecv.at[at], ref.w_sem.at[0, k], ref.w_sem.at[1, at], device_of(from_hi, origin)
            )
            guarded(away, copy.wait_recv)
        origin = from_y * N_R + near + lax.div(mine, 2)
        for hi in range(2):
            copy = copy_to(
                ref.esend.at[0], ref.erecv.at[hi], ref.e_sem.at[0, hi], ref.e_sem.at[1, hi], device_of(hi, origin)
            )
            pl.when(jnp.logical_or(x_hi != hi, origin != slab))(copy.wait_recv)
        ninths = [jnp.concatenate([ref.erecv[hi, j : j + 1, :] for j in range(4)], axis=1) for hi in range(2)]
        received = jnp.concatenate([ref.wrecv[...].reshape(64, 512), *ninths, jnp.zeros((6, 512), F32)], axis=0)
        ref.owned[...] = dot(received.astype(BF16), ref.v_place[...].astype(BF16), TN)

    def local_products():
        kron = channel_matrix(ref.v_lw[...], ref.v_repeat[...], True)
        for n in range(CX * CHUNKS):
            ref.local_part[n] = dot(kron, ref.cells[n], NN)

    def prepare_cells():
        ready("lw", "repeat", "depth_back", "y_back", "gather")
        for copy in cots:
            copy.wait()
        for x in range(CX):
            for r in range(CHUNKS):
                n = x * CHUNKS + r
                ref.cells[n] = chunk_of(ref.v_field[x, :, 16 * r : 16 * r + 16, :]).astype(BF16)
                ref.cot_cells[n] = chunk_of(ref.v_cot[x, :, 16 * r : 16 * r + 16, :])

    def beside_column():
        receive_weights()
        prepare_cells()

    parts = to_window(0, send_weights, beside_column)

    other_core = {"gy": x_hi * 2 + 1 - core}
    ref.qbuf[core] = packed(parts)
    copy = copy_to(ref.qbuf.at[core], ref.qbuf.at[core], ref.core_sem.at[0, 0], ref.core_sem.at[0, 1], other_core)
    copy.start()
    copy.wait_recv()
    started.append((None, copy))
    mixed_r = jnp.zeros((Q, BLOCK), F32)
    mixed_i = jnp.zeros((Q, BLOCK), F32)

    def weights(i):
        return ref.owned[8 * i : 8 * i + 8, 0:BLOCK], ref.owned[256 + 8 * i : 264 + 8 * i, 0:BLOCK]

    for q in range(N_GY):
        both = ref.qbuf[q % 2]
        base = 2 * OWN * (q // 2)
        real, imag = both[:, base : base + OWN], both[:, base + OWN : base + 2 * OWN]
        real, imag = jnp.concatenate([real, real], axis=1), jnp.concatenate([imag, imag], axis=1)
        for c in range(Q):
            mr, mi = real[c : c + 1], imag[c : c + 1]
            w0, w1 = weights(q * Q + c)
            mixed_r = mixed_r + (mr * w0 - mi * w1)
            mixed_i = mixed_i + (mr * w1 + mi * w0)
    mixed = {(p, h): v[:, OWN * h : OWN * h + OWN] for p, v in enumerate((mixed_r, mixed_i)) for h in range(2)}

    def beside_modes():
        send_home(0, ref.qbuf, ref.home_modes)
        local_products()

    def modes_home():
        come_home(0, ref.qbuf, ref.home_modes)
        ref.block_modes[...] = in_block_order([ref.home_modes[k].reshape(16, 128) for k in range(8)])

    from_mixed(0, mixed, jnp.zeros((8, 8), F32), beside_modes, modes_home)

    stores = []

    def store(source, target):
        copy = pltpu.make_async_copy(source, target, ref.store_sem.at[len(stores)])
        copy.start()
        stores.append(copy)

    for x in range(CX):
        spectral_rows(ref.hx, ref.v_y_back, ref.v_depth_back, ref.spec.at[x], x)
    for x in range(CX):
        for r in range(CHUNKS):
            n = x * CHUNKS + r
            rows = slice(16 * r, 16 * r + 16)
            pre = chunk_of(ref.spec[x, :, rows, :]) + ref.local_part[n]
            cdf = 0.5 * (1.0 + lax.erf(pre * ROOT_HALF))
            slope = cdf + pre * jnp.exp(-0.5 * pre * pre) * INV_ROOT_TWO_PI
            grad = ref.cot_cells[n] * slope
            ref.v_out[x, :, rows, :] = unchunk(pre * cdf).astype(BF16)
            ref.grad_pre[x, :, rows, :] = unchunk(grad).astype(BF16)
        store(ref.v_out.at[x], ref.out.at[:, x])
        store(ref.grad_pre.at[x], ref.grad_cells.at[:, x])
        depth_stage(lambda x, c: ref.grad_pre[x, c], x)
    def local_terms():
        total = jnp.zeros((256, 256), F32)
        for n in range(CX * CHUNKS):
            x, r = divmod(n, CHUNKS)
            grad = chunk_of(ref.grad_pre[x, :, 16 * r : 16 * r + 16, :]).astype(BF16)
            total = total + dot(ref.cells[n], grad, NT_DIMS)
        kept = jnp.where(same_row((256, 256)), total, 0.0)
        repeat = ref.v_repeat[...].astype(F32)
        local = dot(dot(repeat, kept, TN, HIGHEST), repeat, NN, HIGHEST)
        for g in range(N_GY):
            for y in range(N_Y):
                ref.lsend[g, y, :, 0:8] = local[8 * g : 8 * g + 8, 8 * y : 8 * y + 8]
        copies = [(ref.lsend.at[g, y], ref.lrecv.at[k], to) for k, (g, y, to) in enumerate(plane_to)]
        local_copies.extend(start_all(ref.local_sem, copies))

    local_copies = []
    parts = to_window(1, local_terms, lambda: None)
    ref.grads[...] = packed(parts)
    gr, gi = (jnp.concatenate([parts[p, 0], parts[p, 1]], axis=1) for p in range(2))
    for i in range(C):
        q, c = divmod(i, Q)
        w0, w1 = weights(i)
        ref.sums[q, c : c + 1, 0:BLOCK] = jnp.sum(gr * w0 + gi * w1, axis=0, keepdims=True)
        ref.sums[q, 8 + c : 9 + c, 0:BLOCK] = jnp.sum(gi * w0 - gr * w1, axis=0, keepdims=True)
    for k in range(2):
        found = {}
        for h in range(2):
            both = ref.sums[2 * h + k]
            both = both[:, 0:OWN] + both[:, OWN:BLOCK]
            found[0, h], found[1, h] = both[0:8], both[8:16]
        ref.qsend[k] = packed(found)
    copy = copy_to(ref.qsend.at[1 - core], ref.qrecv, ref.core_sem.at[1, 0], ref.core_sem.at[1, 1], other_core)
    copy.start()
    copy.wait_recv()
    started.append((None, copy))
    both = ref.qsend[core] + ref.qrecv[...]
    mixed = {(p, h): both[:, OWN * (2 * h + p) : OWN * (2 * h + p) + OWN] for p in range(2) for h in range(2)}

    def weight_gradient():
        come_home(1, ref.grads, ref.home_grads)
        grads = in_block_order([ref.home_grads[k] for k in range(8)])
        grads = jnp.where(x_hi == 0, grads[0:16], grads[16:32])
        gr, gi = grads[0:8, 0:BLOCK], grads[8:16, 0:BLOCK]
        for i in range(C):
            q, c = divmod(i, Q)
            row = 32 * (q // 2) + 8 * (q % 2) + c
            mr, mi = ref.block_modes[row : row + 1, 0:BLOCK], ref.block_modes[row + 16 : row + 17, 0:BLOCK]
            ref.v_grad_spectral[0, i] = mr * gr + mi * gi
            ref.v_grad_spectral[1, i] = mr * gi - mi * gr
        store(ref.v_grad_spectral, ref.grad_spectral)

    finish(local_copies)
    local = ref.lsend[gy, yy, :, 0:8]
    for k in range(15):
        local = local + ref.lrecv[k, :, 0:8]
    from_mixed(1, mixed, local, lambda: send_home(1, ref.grads, ref.home_grads), weight_gradient)
    for y in range(N_Y):
        for g in range(N_GY):
            corner = ref.hall[1, y, g, 24:32, 48:56]
            ref.grad_local[8 * g : 8 * g + 8, 8 * y : 8 * y + 8] = corner * FORWARD_SCALE
    for copy in stores:
        copy.wait()
    drain(len(started))


def last_kernel(
    grad_cells, hx, early_out, early_spectral, early_local, lw, repeat, y_back, depth_back,
    out, grad_in, grad_spectral, grad_local,
    v_hx, v_cells, v_lw, v_repeat, v_y_back, v_depth_back, v_out, spec, v_pass, v_spectral, v_local, sem, pass_sem, store_sem,
):
    gy = lax.axis_index("gy")
    staged = [
        (hx, v_hx),
        (y_back.at[gy], v_y_back),
        (depth_back, v_depth_back),
        (lw, v_lw),
        (repeat, v_repeat),
        *[(grad_cells.at[:, x], v_cells.at[x]) for x in range(CX)],
    ]
    loads = [pltpu.make_async_copy(a, b, sem.at[k]) for k, (a, b) in enumerate(staged)]
    passed = [(early_out, v_pass, out), (early_spectral, v_spectral, grad_spectral), (early_local, v_local, grad_local)]
    arrive = [pltpu.make_async_copy(a, b, pass_sem.at[0, k]) for k, (a, b, _) in enumerate(passed)]
    leave = [pltpu.make_async_copy(b, c, pass_sem.at[1, k]) for k, (_, b, c) in enumerate(passed)]
    for copy in loads + arrive:
        copy.start()
    for copy in loads[:5]:
        copy.wait()
    kron = channel_matrix(v_lw[...], v_repeat[...], False)
    stores = []
    for x in range(CX):
        spectral_rows(v_hx, v_y_back, v_depth_back, spec, x)
        if x == 0:
            for first, second in zip(arrive, leave):
                first.wait()
                second.start()
        loads[5 + x].wait()
        for r in range(CHUNKS):
            rows = slice(16 * r, 16 * r + 16)
            cells = chunk_of(v_cells[x, :, rows, :]).astype(BF16)
            total = chunk_of(spec[:, rows, :]) + dot(kron, cells, NN)
            v_out[x, :, rows, :] = unchunk(total).astype(BF16)
        copy = pltpu.make_async_copy(v_out.at[x], grad_in.at[:, x], store_sem.at[x])
        copy.start()
        stores.append(copy)
    for copy in leave + stores:
        copy.wait()


def per_device(field_in, cotangent, spectral_weight, local_weight):
    cells = (C, CX, TZ, Y)
    depth = depth_table()
    tables = y_tables()
    high = tables.astype(BF16)
    low = (tables - high.astype(np.float64)).astype(BF16)
    blank = np.zeros((N_GY, 8, 2 * Y), BF16)
    expand, keep = unit_tables()
    select, place, gather = owner_tables()
    values = {
        "field": field_in.reshape(cells),
        "cot": cotangent.reshape(cells),
        "weight": jnp.transpose(spectral_weight, (0, 2, 3, 1)).reshape(2 * C * Q, BLOCK),
        "lw": local_weight,
        "depth": depth.astype(BF16),
        "depth_back": np.ascontiguousarray(depth.T).astype(BF16),
        "y_table": np.concatenate([high, blank], axis=1),
        "y_back": np.concatenate([high, low, high, blank], axis=1),
        "rows": row_tables(),
        "expand": expand,
        "keep": keep,
        "select": select.astype(np.float32),
        "place": place.astype(np.float32),
        "gather": gather.astype(np.float32),
        "repeat": np.repeat(np.eye(C), 8, axis=0).astype(BF16),
    }
    values = {name: jnp.asarray(value) for name, value in values.items()}
    vmem, anywhere = pl.BlockSpec(memory_space=pltpu.VMEM), pl.BlockSpec(memory_space=pl.ANY)
    field, mixed, local = ((cells, BF16), ((2, C, Q, BLOCK), F32), ((C, C), F32))
    outs = [field, field, mixed, ((CX, N_GY, 24, 256), F32), local]
    early_out, grad_cells, early_spectral, hx, early_local = pl.pallas_call(
        layer_kernel,
        out_shape=[jax.ShapeDtypeStruct(shape, dtype) for shape, dtype in outs],
        in_specs=[anywhere for _ in INPUTS],
        out_specs=[anywhere] * 3 + [vmem] * 2,
        scratch_shapes=[pltpu.VMEM(shape, dtype) for shape, dtype in SCRATCH.values()]
        + [DMA(shape) for shape in SEMAPHORES.values()],
        compiler_params=pltpu.CompilerParams(
            collective_id=0, has_side_effects=True, vmem_limit_bytes=56 * 1024 * 1024
        ),
        name="spectral_layer",
    )(*[values[name] for name in INPUTS])
    output, grad_input, grad_spectral, grad_local = pl.pallas_call(
        last_kernel,
        out_shape=[jax.ShapeDtypeStruct(shape, dtype) for shape, dtype in (field, field, mixed, local)],
        in_specs=[anywhere] * 9,
        out_specs=[anywhere] * 4,
        scratch_shapes=[
            pltpu.VMEM((CX, N_GY, 24, 256), F32),
            pltpu.VMEM((CX, C, TZ, Y), BF16),
            pltpu.VMEM((C, C), BF16),
            pltpu.VMEM((256, C), BF16),
            pltpu.VMEM((80, 2 * Y), BF16),
            pltpu.VMEM((Q * TZ, 2 * K * Q), BF16),
            pltpu.VMEM((CX, C, TZ, Y), BF16),
            pltpu.VMEM((C, TZ, Y), F32),
            *[pltpu.VMEM(shape, dtype) for shape, dtype in (field, mixed, local)],
            DMA((8,)),
            DMA((2, 3)),
            DMA((CX,)),
        ],
        compiler_params=pltpu.CompilerParams(vmem_limit_bytes=56 * 1024 * 1024),
        name="last_cells",
    )(grad_cells, hx, early_out, early_spectral, early_local, *[values[n] for n in ("lw", "repeat", "y_back", "depth_back")])
    return (
        output.reshape(field_in.shape),
        grad_input.reshape(field_in.shape),
        jnp.transpose(grad_spectral, (0, 3, 1, 2)),
        grad_local,
    )


def solution(mesh):
    placed = (
        P(None, "slab", None, None, "gy"),
        P(None, "slab", None, None, "gy"),
        P(None, "slab", None, "gy"),
        P(),
    )
    return jax.shard_map(
        per_device,
        mesh=mesh,
        in_specs=placed,
        out_specs=(
            P(None, "slab", None, None, "gy"),
            P(None, "slab", None, None, "gy"),
            P(None, "slab", None, "gy"),
            P(),
        ),
        check_vma=False,
    )
```
